32 devices in a mesh: dp: 16 (over z, y, core), mem: 2 (over x).
Axes of the slice: x: 2, y: 2, z: 4, core: 2. Of those that a mesh axis runs over, the one named last changes fastest.
Arguments:
- decoder_in: bfloat16 [16, 1024, 768], P('dp', 'mem'), may hold values from -6 to 6
- encoder_out: bfloat16 [16, 1024, 768], P('dp', 'mem'), may hold values from -6 to 6
- dec_segments: int32 [16, 1024], P('dp', 'mem'), may hold values from 0 to 2, as said below
- dec_mask: int32 [16, 1024], P('dp', 'mem'), may hold values from 0 to 1, as said below
- enc_segments: int32 [16, 1024], P('dp', 'mem'), may hold values from 0 to 2, as said below
- enc_mask: int32 [16, 1024], P('dp', 'mem'), may hold values from 0 to 1, as said below
- self_gain: float32 [768], replicated, may hold values from 0.25 to 1.75
- cross_gain: float32 [768], replicated, may hold values from 0.25 to 1.75
- ffn_gain: float32 [768], replicated, may hold values from 0.25 to 1.75
- rel_bias: float32 [32, 12], replicated, may hold values from -4 to 4
- self_query: bfloat16 [768, 768], replicated, may hold values from -0.109375 to 0.109375
- self_key: bfloat16 [768, 768], replicated, may hold values from -0.109375 to 0.109375
- self_value: bfloat16 [768, 768], replicated, may hold values from -0.21875 to 0.21875
- self_out: bfloat16 [768, 768], replicated, may hold values from -1.25 to 1.25
- cross_query: bfloat16 [768, 768], replicated, may hold values from -0.109375 to 0.109375
- cross_key: bfloat16 [768, 768], replicated, may hold values from -0.109375 to 0.109375
- cross_value: bfloat16 [768, 768], replicated, may hold values from -0.21875 to 0.21875
- cross_out: bfloat16 [768, 768], replicated, may hold values from -1.25 to 1.25
- ffn_in: bfloat16 [768, 3072], replicated, may hold values from -0.21875 to 0.21875
- ffn_out: bfloat16 [3072, 768], replicated, may hold values from -0.109375 to 0.109375
- out_grad: bfloat16 [16, 1024, 768], P('dp', 'mem'), may hold values from -6 to 6
Outputs:
- layer_out: bfloat16 [16, 1024, 768], P('dp', 'mem')
- decoder_in_grad: bfloat16 [16, 1024, 768], P('dp', 'mem')
- encoder_out_grad: bfloat16 [16, 1024, 768], P('dp', 'mem')
- self_gain_grad: float32 [768], replicated
- cross_gain_grad: float32 [768], replicated
- ffn_gain_grad: float32 [768], replicated
- rel_bias_grad: float32 [32, 12], replicated
- self_query_grad: float32 [768, 768], P('dp', 'mem')
- self_key_grad: float32 [768, 768], P('dp', 'mem')
- self_value_grad: float32 [768, 768], P('dp', 'mem')
- self_out_grad: float32 [768, 768], P('dp', 'mem')
- cross_query_grad: float32 [768, 768], P('dp', 'mem')
- cross_key_grad: float32 [768, 768], P('dp', 'mem')
- cross_value_grad: float32 [768, 768], P('dp', 'mem')
- cross_out_grad: float32 [768, 768], P('dp', 'mem')
- ffn_in_grad: float32 [768, 3072], P('dp', 'mem')
- ffn_out_grad: float32 [3072, 768], P('dp', 'mem')
The draws below stay inside these ranges and needn't reach their ends.
Inputs may be any that keep to these rules, and one draw needn't show every extreme that they name: `dec_segments`: every row holds three decoder documents 0, 1, 2 in order, never falling; document 0 ends within the first 128 positions and document 2 takes at least the last 64 positions, so document 1 starts in the first eighth and ends in the last eighth of the row. `dec_mask`: the zeros of a row are its last positions, fewer than 32 of them. `enc_segments`: every row holds three encoder documents 0, 1, 2 in order, never falling; document 0 ends within the first 128 positions and document 2 takes at least the last 64 positions. `enc_mask`: the zeros of a row are its last positions, fewer than 32 of them.
All inputs are finite; a program needn't handle non-finite values.
Results may differ from the reference program's by a relative error of at most 0.029.
The reference program's roundings to bfloat16 on the way count: a program that leaves them out, or rounds other values in their place, can miss the bound.
Values may be sent and summed in bfloat16 or wider, within the bound.
No kernel may reach another device: no remote copies, remote signals or barrier semaphores. Data moves between devices by JAX's collectives and lax.ppermute only.
A program may use at most 320 MiB of HBM per device.

```python
import math
import jax
import jax.numpy as jnp
from jax import lax

D = 768
HEADS = 12
HEAD_DIM = 64
FF = 3072
BUCKETS = 32
MAX_DIST = 128
SEQ = 1024
ENC_LEN = 1024
ROWS = 16


def segment_layout(key):

    def ids_and_mask(sub_key, length):
        unit_len = length // 64
        first_cut = jax.random.randint(jax.random.fold_in(sub_key, 1), (ROWS,), 1, 8)
        last_cut = jax.random.randint(jax.random.fold_in(sub_key, 2), (ROWS,), 57, 61)
        places = jnp.arange(length)
        segments = (places[None, :] >= first_cut[:, None] * unit_len).astype(jnp.int32) + (places[None, :] >= last_cut[:, None] * unit_len).astype(jnp.int32)
        pads = jax.random.randint(jax.random.fold_in(sub_key, 3), (ROWS,), 0, 2 * unit_len)
        mask_rows = (places[None, :] < length - pads[:, None]).astype(jnp.int32)
        return (segments.astype(jnp.int32), mask_rows)
    return (ids_and_mask(jax.random.fold_in(key, 103), SEQ), ids_and_mask(jax.random.fold_in(key, 104), ENC_LEN))


def draw_dec_segments(key, part):
    layout = segment_layout(key)
    return layout[0][0]


def draw_dec_mask(key, part):
    layout = segment_layout(key)
    return layout[0][1]


def draw_enc_segments(key, part):
    layout = segment_layout(key)
    return layout[1][0]


def draw_enc_mask(key, part):
    layout = segment_layout(key)
    return layout[1][1]


def block_levels(stream_key, shape, split, smallest, top_value):
    level = 1.0
    for position, parts in split:
        heights = jax.random.uniform(jax.random.fold_in(jax.random.fold_in(stream_key, 6), position), (parts,), jnp.float32, smallest / len(split), top_value / len(split))
        level = level * jnp.repeat(jnp.exp(heights), shape[position] // parts).reshape((-1,) + (1,) * (len(shape) - 1 - position))
    return level


def centred(rng, shape, spread, reach, split=(), held_as=jnp.bfloat16):
    level = block_levels(rng, shape, split, -0.22, 0.18) if split else 1.0
    values = jax.random.normal(rng, shape, jnp.float32) * spread * level
    return jnp.minimum(jnp.maximum(values, -reach), reach).astype(held_as)


def setup_inputs(seed: int = 0) -> dict:
    arg_keys = jax.random.split(jax.random.key(seed), 22)
    return {
        "decoder_in": centred(arg_keys[0], (ROWS, SEQ, D), 1.0, 6.0, ((0, 16), (1, 2))),
        "encoder_out": centred(arg_keys[1], (ROWS, ENC_LEN, D), 1.0, 6.0, ((0, 16), (1, 2))),
        "dec_segments": draw_dec_segments(jax.random.fold_in(arg_keys[21], 71), 0),
        "dec_mask": draw_dec_mask(jax.random.fold_in(arg_keys[21], 71), 0),
        "enc_segments": draw_enc_segments(jax.random.fold_in(arg_keys[21], 71), 0),
        "enc_mask": draw_enc_mask(jax.random.fold_in(arg_keys[21], 71), 0),
        "self_gain": jnp.clip(1.0 + 0.15 * jax.random.normal(arg_keys[6], (D,), jnp.float32), 0.25, 1.75),
        "cross_gain": jnp.clip(1.0 + 0.15 * jax.random.normal(arg_keys[7], (D,), jnp.float32), 0.25, 1.75),
        "ffn_gain": jnp.clip(1.0 + 0.15 * jax.random.normal(arg_keys[8], (D,), jnp.float32), 0.25, 1.75),
        "rel_bias": centred(arg_keys[9], (BUCKETS, HEADS), 1.0, 4.0, (), jnp.float32),
        "self_query": centred(arg_keys[10], (D, D), (4 * D) ** -0.5, 0.109375),
        "self_key": centred(arg_keys[11], (D, D), (4 * D) ** -0.5, 0.109375),
        "self_value": centred(arg_keys[12], (D, D), D ** -0.5, 0.21875),
        "self_out": centred(arg_keys[13], (D, D), (D // 32) ** -0.5, 1.25),
        "cross_query": centred(arg_keys[14], (D, D), (4 * D) ** -0.5, 0.109375),
        "cross_key": centred(arg_keys[15], (D, D), (4 * D) ** -0.5, 0.109375),
        "cross_value": centred(arg_keys[16], (D, D), D ** -0.5, 0.21875),
        "cross_out": centred(arg_keys[17], (D, D), (D // 32) ** -0.5, 1.25),
        "ffn_in": centred(arg_keys[18], (D, FF), D ** -0.5, 0.21875),
        "ffn_out": centred(arg_keys[19], (FF, D), FF ** -0.5, 0.109375),
        "out_grad": centred(arg_keys[20], (ROWS, SEQ, D), 1.0, 6.0, ((0, 16), (1, 2))),
    }


@jax.custom_vjp
def low(v):
    return lax.optimization_barrier(v.astype(jnp.bfloat16)).astype(jnp.float32)

@jax.custom_vjp
def low_back(v):
    return v

def low_keep(v):
    return (low(v), None)

def low_pass(kept, grad):
    return (grad,)

def back_keep(v):
    return (v, None)

def back_low(kept, grad):
    return (low(grad),)
low.defvjp(low_keep, low_pass)
low_back.defvjp(back_keep, back_low)
EPSILON = 1e-06
NEGATIVE = -1000000000.0
HIGHEST = lax.Precision.HIGHEST

def rel_bucket(distance):
    exact_max = BUCKETS // 2
    bucket_edges = [math.ceil(exact_max * (MAX_DIST / exact_max) ** (degree / exact_max)) for degree in range(1, exact_max)]
    log_bucket = exact_max + sum(((distance >= edge_value).astype(jnp.int32) for edge_value in bucket_edges))
    return jnp.where(distance < exact_max, distance, log_bucket)

def rms_scale(hidden, gain):
    return hidden * lax.rsqrt(lax.optimization_barrier(jnp.mean(hidden * hidden, axis=-1, keepdims=True)) + EPSILON) * gain

def dense(values, weight):
    return jnp.einsum('bsd,de->bse', values, weight, precision=HIGHEST)

def split_heads(values):
    return values.reshape(values.shape[0], values.shape[1], HEADS, HEAD_DIM)

def softmax_mix(query_rows, key_rows, value_rows, allowed, bias):
    scores = jnp.einsum('bqhd,bkhd->bhqk', split_heads(query_rows), split_heads(key_rows), precision=HIGHEST)
    if bias is not None:
        scores = scores + bias[None]
    scores = low_back(scores)
    masked = jnp.where(allowed[:, None], scores, NEGATIVE)
    top_score = lax.optimization_barrier(jnp.max(masked, axis=-1, keepdims=True))
    weights = jnp.exp(masked - top_score)
    probs = weights / lax.optimization_barrier(jnp.sum(weights, axis=-1, keepdims=True))
    mixed = jnp.einsum('bhqk,bkhd->bqhd', low(probs), split_heads(value_rows), precision=HIGHEST)
    return low_back(low(mixed.reshape(query_rows.shape)))

def layer(decoder_rows, encoder_rows, dec_seg, dec_msk, enc_seg, enc_msk, self_gain, cross_gain, ffn_gain, rel_bias, self_query, self_key, self_value, self_out, cross_query, cross_key, cross_value, cross_out, ffn_in, ffn_out):
    positions = jnp.arange(SEQ)
    distance = jnp.maximum(positions[:, None] - positions[None, :], 0)
    bias = jnp.transpose(rel_bias[rel_bucket(distance)], (2, 0, 1))
    causal = positions[:, None] >= positions[None, :]
    self_allowed = (dec_seg[:, :, None] == dec_seg[:, None, :]) & causal[None] & (dec_msk[:, None, :] > 0)
    self_in = low(rms_scale(decoder_rows, self_gain))
    query_rows = low_back(low(dense(self_in, self_query)))
    key_rows = low_back(low(dense(self_in, self_key)))
    value_rows = low_back(low(dense(self_in, self_value)))
    self_mixed = softmax_mix(query_rows, key_rows, value_rows, self_allowed, bias)
    hidden_one = decoder_rows + low_back(dense(self_mixed, self_out))
    cross_in = low(rms_scale(hidden_one, cross_gain))
    cross_rows = low_back(low(dense(cross_in, cross_query)))
    cross_keys = low_back(low(dense(encoder_rows, cross_key)))
    cross_values = low_back(low(dense(encoder_rows, cross_value)))
    cross_allowed = (dec_seg[:, :, None] == enc_seg[:, None, :]) & (enc_msk[:, None, :] > 0)
    cross_mixed = softmax_mix(cross_rows, cross_keys, cross_values, cross_allowed, None)
    hidden_two = hidden_one + low_back(dense(cross_mixed, cross_out))
    ffn_input = low(rms_scale(hidden_two, ffn_gain))
    ffn_pre = low_back(dense(ffn_input, ffn_in))
    ffn_act = low(jax.nn.gelu(ffn_pre, approximate=True))
    return hidden_two + low_back(dense(ffn_act, ffn_out))

def reference(decoder_in, encoder_out, dec_segments, dec_mask, enc_segments, enc_mask, self_gain, cross_gain, ffn_gain, rel_bias, self_query, self_key, self_value, self_out, cross_query, cross_key, cross_value, cross_out, ffn_in, ffn_out, out_grad):
    weights_wide = (self_gain.astype(jnp.float32), cross_gain.astype(jnp.float32), ffn_gain.astype(jnp.float32), rel_bias.astype(jnp.float32), self_query.astype(jnp.float32), self_key.astype(jnp.float32), self_value.astype(jnp.float32), self_out.astype(jnp.float32), cross_query.astype(jnp.float32), cross_key.astype(jnp.float32), cross_value.astype(jnp.float32), cross_out.astype(jnp.float32), ffn_in.astype(jnp.float32), ffn_out.astype(jnp.float32))
    block_rows = math.gcd(ROWS, 2)
    block_count = ROWS // block_rows

    def blocked(array):
        return array.reshape((block_count, block_rows) + array.shape[1:])

    def one_block(running, pieces):
        dec_rows, enc_rows, dec_seg, dec_msk, enc_seg, enc_msk, cotangent = pieces

        def forward(dec_values, enc_values, *weight_values):
            return layer(dec_values, enc_values, dec_seg, dec_msk, enc_seg, enc_msk, *weight_values)
        out_value, pull_back = jax.vjp(forward, dec_rows.astype(jnp.float32), enc_rows.astype(jnp.float32), *weights_wide)
        grads = pull_back(cotangent.astype(jnp.float32))
        running = tuple((total + grad_value for total, grad_value in zip(running, grads[2:])))
        return (running, (out_value.astype(jnp.bfloat16), grads[0].astype(jnp.bfloat16), grads[1].astype(jnp.bfloat16)))
    start_grads = tuple((jnp.zeros_like(weight_value) for weight_value in weights_wide))
    totals, results = lax.scan(one_block, start_grads, (blocked(decoder_in), blocked(encoder_out), blocked(dec_segments), blocked(dec_mask), blocked(enc_segments), blocked(enc_mask), blocked(out_grad)))
    layer_out = results[0].reshape(ROWS, SEQ, D)
    decoder_in_grad = results[1].reshape(ROWS, SEQ, D)
    encoder_out_grad = results[2].reshape(ROWS, ENC_LEN, D)
    return (layer_out, decoder_in_grad, encoder_out_grad, totals[0], totals[1], totals[2], totals[3], totals[4], totals[5], totals[6], totals[7], totals[8], totals[9], totals[10], totals[11], totals[12], totals[13])
```

```python
import copy
import functools
import math

import jax
import jax.numpy as jnp
import numpy as np
from jax import lax
from jax.experimental import pallas as pl
from jax.experimental.pallas import tpu as pltpu
from jax.sharding import PartitionSpec as P

HEADS = 12
HEAD_DIM = 64
BUCKETS = 32
MAX_DIST = 128
PAIRS = HEADS // 2
LANES = 128

EPSILON = 1e-06
NEGATIVE = -(2.0**30)
LOG2E = math.log2(math.e)
LN2 = math.log(2.0)
VMEM_LIMIT = 12 * 1024 * 1024
BF16 = jnp.bfloat16
F32 = jnp.float32


def bucket_edges():
    exact_max = BUCKETS // 2
    return [
        math.ceil(exact_max * (MAX_DIST / exact_max) ** (degree / exact_max))
        for degree in range(1, exact_max)
    ]


def rel_bucket(distance):
    exact_max = BUCKETS // 2
    log_bucket = exact_max + sum(
        (distance >= edge).astype(np.int32) for edge in bucket_edges()
    )
    return np.where(distance < exact_max, distance, log_bucket)


FAR = bucket_edges()[-1]


def near_types(block):
    return (FAR - 1 + block - 1) // block + 1


def group_of(dp, mem, mem_size):
    half = mem_size // 2
    return (dp % 2) * half + mem % half


def row_moves(dp_size, mem_size):
    half = mem_size // 2
    moves = ([], [])
    for dp in range(dp_size):
        for mem in range(mem_size):
            for piece in range(2):
                chunk = 2 * mem + piece
                group = chunk if chunk < mem_size else 2 * mem_size - 1 - chunk
                to_dp = dp - dp % 2 + group // half
                to_mem = (dp % 2) * half + group % half
                moves[piece].append((dp * mem_size + mem, to_dp * mem_size + to_mem))
    return moves


def to_rows(values, axis=0):
    moves = row_moves(lax.axis_size("dp"), lax.axis_size("mem"))
    return tuple(
        lax.ppermute(piece, ("dp", "mem"), move) for piece, move in zip(jnp.split(values, 2, axis=axis), moves)
    )


def arranged(pieces, odd, axis=0):
    first, second = pieces
    return jnp.concatenate(
        [jnp.where(odd, second, first), jnp.where(odd, first, second)], axis=axis
    )


def from_rows(values, odd, axis=0):
    moves = row_moves(lax.axis_size("dp"), lax.axis_size("mem"))
    low, high = jnp.split(values, 2, axis=axis)
    first, second = jnp.where(odd, high, low), jnp.where(odd, low, high)
    back = [[(there, here) for here, there in move] for move in moves]
    first = lax.ppermute(first, ("dp", "mem"), back[0])
    second = lax.ppermute(second, ("dp", "mem"), back[1])
    return jnp.concatenate([first, second], axis=axis)


def group_shift(values, step):
    dp_size, mem_size = lax.axis_size("dp"), lax.axis_size("mem")
    half = mem_size // 2
    moves = []
    for dp in range(dp_size):
        for mem in range(mem_size):
            group = (group_of(dp, mem, mem_size) + step) % mem_size
            to_dp = dp - dp % 2 + group // half
            to_mem = mem - mem % half + group % half
            moves.append((dp * mem_size + mem, to_dp * mem_size + to_mem))
    return lax.ppermute(values, ("dp", "mem"), moves)


def others(values):
    return [group_shift(values, step) for step in range(1, lax.axis_size("mem"))]


def came_parts(parts, rows):
    came = [
        group_shift(parts[:, (step - 1) * rows : step * rows], -step) for step in range(1, lax.axis_size("mem"))
    ]
    return came[0] if len(came) == 1 else sum(part.astype(F32) for part in came)


def block_list(group, mem_size, rows):
    piece = rows // 2
    q_at, k_at, kinds, is_low = [], [], [], []
    for i in range(2 * mem_size + 1):
        low = i <= group
        chunk = jnp.where(low, i, i - (group + 1))
        owner = jnp.where(chunk < mem_size, chunk, 2 * mem_size - 1 - chunk)
        slot = (group - owner) % mem_size
        q_at.append(jnp.where(low, 0, piece))
        k_at.append(slot * rows + jnp.where(chunk < mem_size, 0, piece))
        kinds.append(jnp.where(low, group - i, 2 * mem_size - i))
        is_low.append(low.astype(jnp.int32))
    return jnp.stack([jnp.stack(v).astype(jnp.int32) for v in (q_at, k_at, kinds, is_low)])


def bias_of(distance, rel_bias):
    hot = (rel_bucket(np.maximum(distance, 0))[..., None] == np.arange(BUCKETS)).astype(np.float32)
    values = jnp.einsum(
        "...b,bh->h...", jnp.asarray(hot), rel_bias - rel_bias[BUCKETS - 1], precision=lax.Precision.HIGHEST
    )
    return jnp.where(jnp.asarray(distance >= 0), values * LOG2E, NEGATIVE)


def spread(row, rows):
    width = row.shape[1]
    table = jnp.broadcast_to(row, (8, width))
    place = lax.broadcasted_iota(jnp.int32, (8, width), 0)
    for bit in range(3):
        moved = pltpu.roll(table, 1 << bit, 1)
        table = jnp.where((place >> bit) & 1 == 1, moved, table)
    size = 8
    while size < rows:
        table = jnp.concatenate([table, pltpu.roll(table, size, 1)], axis=0)
        size *= 2
    return table


def small_block(block):
    return min(LANES, block)


def table_kernel(base_ref, base_t_ref, table_ref, table_t_ref):
    heads, kinds, block = table_ref.shape[0], table_ref.shape[1] - 2, table_ref.shape[2]
    for head in range(heads):
        for base, table in ((base_ref, table_ref), (base_t_ref, table_t_ref)):
            table[head, 0] = jnp.full((block, block), NEGATIVE, F32)
            table[head, kinds + 1] = jnp.zeros((block, block), F32)
            for kind in range(kinds):
                table[head, kind + 1] = spread(base[head, kind], block)[:, block:]


def bias_tables(rel_bias, block):
    kinds = near_types(block)
    at = np.arange(2 * block)[None, :] - block
    start = np.arange(kinds)[:, None] * block
    base, base_t = bias_of(start - at, rel_bias), bias_of(start + at, rel_bias)
    if block % LANES:
        step = np.arange(block)[None, :] - np.arange(block)[:, None] + block
        masked = jnp.full((HEADS, 1, block, block), NEGATIVE, F32)
        return [jnp.concatenate([masked, v[:, :, step], jnp.zeros_like(masked)], axis=1) for v in (base, base_t)]
    heads = HEADS // 3
    spec = pl.BlockSpec((heads, kinds, 1, 2 * block), lambda h: (h, 0, 0, 0))
    out = pl.BlockSpec((heads, kinds + 2, block, block), lambda h: (h, 0, 0, 0))
    shape = jax.ShapeDtypeStruct((HEADS, kinds + 2, block, block), F32)
    return pl.pallas_call(
        table_kernel,
        grid=(HEADS // heads,),
        in_specs=[spec, spec],
        out_specs=[out, out],
        out_shape=[pltpu.HBM(shape.shape, shape.dtype)] * 2,
        compiler_params=pltpu.CompilerParams(vmem_limit_bytes=VMEM_LIMIT),
        name="bias_tables",
    )(base[:, :, None, :], base_t[:, :, None, :])


def small_parts(block, small):
    return [(r, c, (r - c) // small) for r in range(0, block, small) for c in range(0, block, small)]


def kind_index(step, kind, block, small, kinds):
    return jnp.clip(kind * (block // small) + step + 1, 0, kinds + 1)


def with_bias(s, table_ref, head, kind, turned=False):
    block, small, kinds = s.shape[0], table_ref.shape[2], table_ref.shape[1] - 2
    fixed = isinstance(kind, int)
    if fixed and (kind - 1) * block >= FAR - 1:
        return s
    pieces = {}
    for r, c, step in small_parts(block, small):
        at = (c, r) if turned else (r, c)
        part = s[at[0] : at[0] + small, at[1] : at[1] + small]
        if fixed:
            step = kind * (block // small) + step
            if step < kinds:
                part = part + table_ref[head, step + 1] if step >= 0 else jnp.full(part.shape, NEGATIVE, F32)
        else:
            part = part + table_ref[head, kind_index(step, kind, block, small, kinds)]
        pieces[at] = part
    starts = range(0, block, small)
    return jnp.concatenate([jnp.concatenate([pieces[a, b] for b in starts], axis=1) for a in starts], axis=0)


def add_grad(ds, grad_ref, head, kind):
    block, small, kinds = ds.shape[0], grad_ref.shape[2], grad_ref.shape[1] - 2
    fixed = isinstance(kind, int)
    for r, c, step in small_parts(block, small):
        part = ds[c : c + small, r : r + small]
        if fixed:
            step = kind * (block // small) + step
            if not 0 <= step < kinds:
                continue
            at = step + 1
        else:
            at = kind_index(step, kind, block, small, kinds)
        grad_ref[head, at] = grad_ref[head, at] + part


def fold(table):
    rows, width = table.shape
    while rows > 1:
        rows //= 2
        table = table[:rows] + pltpu.roll(table[rows:], width - rows, 1)
    return table


def fold_kernel(first_ref, rest_ref, cross_ref, ffn_ref, sums_ref):
    kinds = first_ref.shape[1] - 2
    sums_ref[...] = jnp.zeros_like(sums_ref)
    sums_ref[1:2, :], sums_ref[2:3, :] = cross_ref[...], ffn_ref[...]
    for part, ref in enumerate((first_ref, rest_ref)):
        heads = ref.shape[0]
        for head in range(heads):
            for kind in range(kinds):
                table = ref[head, kind + 1]
                width = 2 * table.shape[1]
                wide = jnp.concatenate([table, jnp.zeros_like(table)], axis=1)
                row = FIRST_HEAD_ROW + part * heads + head
                sums_ref[row : row + 1, kind * width : (kind + 1) * width] = fold(wide)


def table_sums(first, rest, cross_grad, ffn_grad):
    kinds, block = first.shape[1] - 2, first.shape[2]
    shape = (SMALL_ROWS, cross_grad.shape[1])
    if block % LANES:
        grad_t = jnp.pad(jnp.concatenate([first, rest])[:, 1 : kinds + 1], ((0, 0), (0, 0), (0, 0), (0, block)))
        place = (np.arange(block)[:, None] + np.arange(2 * block)[None, :]) % (2 * block)
        sums = jnp.sum(grad_t[:, :, np.arange(block)[:, None], place], axis=2).reshape(HEADS, -1)
        small = jnp.zeros(shape, F32).at[1].set(cross_grad[0]).at[2].set(ffn_grad[0])
        return small.at[FIRST_HEAD_ROW : FIRST_HEAD_ROW + HEADS, : sums.shape[1]].set(sums)
    return run(
        fold_kernel,
        "table_sums",
        (1,),
        [(first, None, pltpu.HBM), (rest, None, pltpu.HBM), (cross_grad, None), (ffn_grad, None)],
        [(shape, F32, None)],
    )[0]


def bucket_hot(block):
    kinds = near_types(block)
    at = np.arange(2 * block)[None, :]
    at = np.where(at < block, at, at - 2 * block) + np.arange(kinds)[:, None] * block
    near = (at >= 0) & (at < FAR)
    hot = (rel_bucket(np.maximum(at, 0))[..., None] == np.arange(BUCKETS)) & near[..., None]
    return hot.reshape(-1, BUCKETS).T.astype(np.float32)


def write_kernel(chunks, *refs):
    counts, chunks = chunks
    totals, at = [], 0
    for count in counts:
        parts = [ref[...].astype(F32) for ref in refs[at : at + count]]
        totals.append(sum(parts[1:], parts[0]))
        at += count
    ffn, rest, own = totals
    small, hot = refs[at][...], refs[at + 1][...]
    refs = refs[at + 2 :]
    gains, table_ref, fo_ref, fi_ref, squares = refs[:3], refs[3], refs[4], refs[5], refs[6:]
    for i in range(3):
        gains[i][...] = small[i : i + 1, :]
    sums = small[FIRST_HEAD_ROW : FIRST_HEAD_ROW + HEADS, : hot.shape[1]]
    near = lax.dot_general(
        hot, sums, (((1,), (1,)), ((), ())), precision=lax.Precision.HIGHEST, preferred_element_type=F32
    )
    last = -jnp.sum(near, axis=0, keepdims=True)
    bucket = lax.broadcasted_iota(jnp.int32, near.shape, 0)
    table_ref[...] = jnp.where(bucket == BUCKETS - 1, last, near)
    rows, cols = fo_ref.shape
    fo_ref[...] = ffn[:rows]
    each = fi_ref.shape[0]
    for i in range(chunks):
        fi_ref[:, i * cols : (i + 1) * cols] = ffn[rows + i * each : rows + (i + 1) * each]
    at = 0
    for total in (rest, own):
        for i in range(total.shape[0] // each):
            squares[at][...] = total[i * each : (i + 1) * each]
            at += 1


def write_grads(ffn, rest, own, small, block, width, hidden):
    dp_size, mem_size = lax.axis_size("dp"), lax.axis_size("mem")
    hot = jnp.asarray(bucket_hot(block))
    square = ((width // dp_size, width // mem_size), F32, None)
    return run(
        functools.partial(write_kernel, ([1 + len(s.came) for s in (ffn, rest, own)], hidden // width)),
        "write_grads",
        (1,),
        [(v.reshape(v.shape[-2:]), None) for s in (ffn, rest, own) for v in (s.keep, *s.came)]
        + [(v, None) for v in (small, hot)],
        [((1, width), F32, None)] * 3
        + [
            ((BUCKETS, HEADS), F32, None),
            ((hidden // dp_size, width // mem_size), F32, None),
            ((width // dp_size, hidden // mem_size), F32, None),
        ]
        + [square] * 8,
    )


def nt(a, b):
    return lax.dot_general(a, b, (((1,), (1,)), ((), ())), preferred_element_type=F32)


def nn(a, b):
    return jnp.dot(a, b, preferred_element_type=F32)


def half_of(values, head):
    lane = lax.broadcasted_iota(jnp.int32, values.shape, 1)
    return jnp.where((lane >= HEAD_DIM) == (head == 1), values, jnp.zeros_like(values))


def join_halves(first, second):
    lane = lax.broadcasted_iota(jnp.int32, first.shape, 1)
    return jnp.where(lane < HEAD_DIM, first, second)


def in_three(values):
    high = values.astype(BF16)
    rest = values - high.astype(F32)
    mid = rest.astype(BF16)
    low = (rest - mid.astype(F32)).astype(BF16)
    return high, mid, low


def put_lanes(base, start, values):
    lane = lax.broadcasted_iota(jnp.int32, base.shape, 1)
    for i, value in enumerate(values):
        base = jnp.where(lane == start + i, value, base)
    return base


def with_log_sum(mask_lanes, log_sum):
    pieces = [piece.astype(F32) for piece in in_three(-log_sum)]
    return put_lanes(mask_lanes.astype(F32), 3, pieces).astype(BF16)


def bit_count(axis):
    return lax.axis_size(axis).bit_length() - 1


def swap(values, axis, bit):
    size = lax.axis_size(axis)
    return lax.ppermute(values, axis, [(i, i ^ (1 << bit)) for i in range(size)])


def swap_many(values, names):
    dp_size, mem_size = lax.axis_size("dp"), lax.axis_size("mem")
    flips = {axis: sum(1 << bit for name, bit in names if name == axis) for axis in ("dp", "mem")}
    moves = [
        (dp * mem_size + mem, (dp ^ flips["dp"]) * mem_size + (mem ^ flips["mem"]))
        for dp in range(dp_size)
        for mem in range(mem_size)
    ]
    return lax.ppermute(values, ("dp", "mem"), moves)


def bit_order(order):
    dp_bits, mem_bits = bit_count("dp"), bit_count("mem")
    z_bits = [("dp", b) for b in range(2, dp_bits)]
    groups = {
        "x": [("mem", b) for b in range(mem_bits)],
        "y": [("dp", b) for b in range(1, min(2, dp_bits))],
        "Z": z_bits[:1],
        "z": z_bits[1:] if "Z" in order else z_bits,
    }
    return [step for name in order for step in groups[name]]


def in_pairs(names):
    return [tuple(names[i : i + 2]) for i in range(0, len(names), 2)]


SMALL_ROWS = 16
FIRST_HEAD_ROW = 4


TILE = 256
LIMITS = {
    "own_project": 12,
    "other_project": 12,
    "encoder_project": 12,
    "self_forward": 18,
    "cross_forward": 18,
    "feed_forward": 34,
    "cross_backward": 18,
    "cross_finish": 30,
    "encoder_finish": 18,
    "self_backward": 18,
    "table_sums": 12,
    "query_grad": 12,
    "key_grads": 18,
    "self_finish_back": 18,
    "advance": 24,
    "write_grads": 16,
}


def tn(a, b):
    return lax.dot_general(a, b, (((0,), (0,)), ((), ())), preferred_element_type=F32)


def normed(hidden, gain):
    return hidden * lax.rsqrt(jnp.mean(hidden * hidden, axis=-1, keepdims=True) + EPSILON) * gain


def norm_back(hidden, gain, grad):
    scale = lax.rsqrt(jnp.mean(hidden * hidden, axis=-1, keepdims=True) + EPSILON)
    unit = hidden * scale
    inner = grad * gain
    out = scale * (inner - unit * jnp.mean(inner * unit, axis=-1, keepdims=True))
    return out, jnp.sum(grad * unit, axis=0, keepdims=True)


def whole(array):
    zeros = (0,) * array.ndim
    return pl.BlockSpec(array.shape, lambda *_: zeros)


def run(kernel, name, grid, ins, outs, scratch=(), scalars=(), after=(), flops=0, aliases=None):
    count = len(scalars) + len(ins)
    in_places = [v[2] if len(v) > 2 else None if v[1] is None or v[1] is ANY else pltpu.HBM for v in ins]
    out_places = [v[3] if len(v) > 3 else None if v[2] is None else pltpu.HBM for v in outs]
    ins, outs = [v[:2] for v in ins], [v[:3] for v in outs]

    def body(*refs):
        kernel(*refs[:count], *refs[count + len(after) :])

    out_shape = [jax.ShapeDtypeStruct(shape, dtype) for shape, dtype, _ in outs]
    placed = [o if p is None else p(o.shape, o.dtype) for o, p in zip(out_shape, out_places)]
    arrays = [a if p is None else pltpu.with_memory_space_constraint(a, p) for (a, _), p in zip(ins, in_places)]
    moved = sum(a.size * a.dtype.itemsize for a, _ in ins) + sum(
        math.prod(s) * jnp.dtype(d).itemsize for s, d, _ in outs
    )
    return pl.pallas_call(
        body,
        grid_spec=pltpu.PrefetchScalarGridSpec(
            num_scalar_prefetch=len(scalars),
            grid=grid,
            in_specs=[whole(a) if s is None else s for a, s in ins]
            + [pl.BlockSpec(memory_space=pl.ANY) for _ in after],
            out_specs=[whole(o) if s is None else s for o, (_, _, s) in zip(out_shape, outs)],
            scratch_shapes=list(scratch),
        ),
        out_shape=placed,
        input_output_aliases=aliases or {},
        compiler_params=pltpu.CompilerParams(vmem_limit_bytes=LIMITS[name] << 20),
        cost_estimate=pl.CostEstimate(flops=flops // 16, bytes_accessed=moved // 16, transcendentals=0),
        name=name,
    )(*scalars, *arrays, *after)


ANY = pl.BlockSpec(memory_space=pl.ANY)


def row_spec(tile, width, shift=0):
    return pl.BlockSpec((tile, width), lambda i, *_: (i + shift, 0))


def fits(rows, cols):
    dp_size, mem_size = lax.axis_size("dp"), lax.axis_size("mem")
    return (rows // dp_size) % 16 == 0 and (cols // mem_size) % LANES == 0


def emit(mine, total_ref, keep_ref, send_ref, at, rows):
    mem_size, pairs, _, cols = keep_ref.shape
    chunks = total_ref.shape[1] // cols // mem_size
    for pair in range(pairs):
        keep_at = pl.multiple_of((2 * pair + mine) * rows, 16)
        send_at = pl.multiple_of((2 * pair + 1 - mine) * rows, 16)
        for mem in range(mem_size):
            for chunk in range(chunks):
                lanes = slice((mem * chunks + chunk) * cols, (mem * chunks + chunk + 1) * cols)
                place = slice(at + chunk * rows, at + (chunk + 1) * rows)
                keep_ref[mem, pair, place, :] = total_ref[pl.ds(keep_at, rows), lanes].astype(BF16)
                send_ref[mem, pair, place, :] = total_ref[pl.ds(send_at, rows), lanes].astype(BF16)


def square_outs(count, width):
    dp_size, mem_size = lax.axis_size("dp"), lax.axis_size("mem")
    if fits(width, width):
        shape = (mem_size, dp_size // 2, count * width // dp_size, width // mem_size)
        return [(shape, BF16, None)] * 2
    return [((width, width), BF16, None)] * count


def write_square(mine, index, total, total_ref, out_refs):
    if len(out_refs[0].shape) == 4:
        keep_ref, send_ref = out_refs
        rows = total.shape[0] // (2 * keep_ref.shape[1])
        total_ref[...] = total
        emit(mine, total_ref, keep_ref, send_ref, index * rows, rows)
    else:
        out_refs[index][...] = total.astype(BF16)


def in_order(grads, chunks=1):
    if grads[0].ndim == 4:
        return grads
    dp_size, mem_size = lax.axis_size("dp"), lax.axis_size("mem")
    cuts = []
    for grad in grads:
        rows, cols = grad.shape[0] // dp_size, grad.shape[1] // mem_size // chunks
        cut = grad.reshape(dp_size // 2, 2, rows, mem_size, chunks, cols).transpose(1, 3, 0, 4, 2, 5)
        cuts.append(cut.reshape(2, mem_size, dp_size // 2, chunks * rows, cols))
    cut = jnp.concatenate(cuts, axis=3)
    mine = lax.axis_index("dp") & 1
    return [lax.dynamic_index_in_dim(cut, which, 0, keepdims=False) for which in (mine, 1 - mine)]


class Scatter:
    def __init__(self, grads, order, chunks=1):
        keep, send = in_order(grads, chunks)
        mem_bits, dp_bits = bit_count("mem"), bit_count("dp")
        self.names = [("mem", b) for b in reversed(range(mem_bits))]
        self.names += [("dp", b) for b in reversed(range(1, dp_bits))]
        self.order = []
        for part in order.split("]"):
            single, _, paired = part.partition("[")
            self.order += [(name,) for name in bit_order(single)] + in_pairs(bit_order(paired))
        shape = (2,) * len(self.names) + keep.shape[2:]
        self.keep, self.came = keep.reshape(shape), [swap(send, "dp", 0).reshape(shape)]
        self.span = (0, shape[-2])

    def parts(self, *orders):
        size = self.span[1] // len(orders)
        shares = []
        for i, order in enumerate(orders):
            share = copy.copy(self)
            share.names, share.span = list(self.names), (i * size, size)
            share.order = [(name,) for name in bit_order(order)]
            shares.append(share)
        return shares


def all_bits():
    return [("mem", b) for b in range(bit_count("mem"))] + [("dp", b) for b in range(bit_count("dp"))]


def bit_values():
    return jnp.stack([((lax.axis_index(axis) >> bit) & 1).astype(jnp.int32) for axis, bit in all_bits()])


def level(*group, bits):
    while any(v.order != group[0].order for v in group):
        longest = max(sum(map(len, v.order)) for v in group)
        advance(bits, *[v for v in group if sum(map(len, v.order)) == longest])


def advance_kernel(moves, bits, *refs):
    outs = refs[sum(parts for _, sources in moves for _, _, parts in sources) :]
    ref_at = out_at = 0
    for names, sources in moves:
        flips = [(0,), (1,)] if len(names) == 1 else [(0, 0), (0, 1), (1, 0), (1, 1)]
        start = 0
        for from_row, size, parts in sources:
            ins = refs[ref_at : ref_at + parts]
            ref_at += parts
            for pre in range(ins[0].shape[0]):
                for mid in range(ins[0].shape[2]):
                    for post in range(ins[0].shape[4]):
                        for out, flip in zip(outs[out_at : out_at + len(flips)], flips):
                            place = [bits[name] if f == 0 else 1 - bits[name] for name, f in zip(names, flip)]
                            place = place + [0] if len(place) == 1 else place
                            rows = slice(from_row, from_row + size)
                            values = [ref[pre, place[0], mid, place[1], post, rows, :].astype(F32) for ref in ins]
                            out[pre, mid, post, start : start + size, :] = sum(values[1:], values[0]).astype(BF16)
            start += size
        out_at += len(flips)


def advance(bits, *groups):
    groups = [group if isinstance(group, tuple) else (group,) for group in groups]
    for group in groups:
        lead = group[0]
        assert all(v.names == lead.names and v.order == lead.order for v in group)
        if not lead.order and len(group) > 1:
            sums = [sum(v.came, v.keep.astype(F32))[..., v.span[0] : sum(v.span), :] for v in group]
            lead.keep = jnp.concatenate(sums, axis=-2)
            lead.came, lead.span = [jnp.zeros_like(lead.keep)], (0, lead.keep.shape[-2])
    groups = [group for group in groups if group[0].order]
    if not groups:
        return
    moves, arrays, heads = [], [], []
    for group in groups:
        lead = group[0]
        names = lead.order.pop(0)
        places = [lead.names.index(name) for name in names]
        if places != sorted(places):
            names, places = names[::-1], places[::-1]
        pre = 2 ** places[0]
        mid = 2 ** (places[1] - places[0] - 1) if len(names) == 2 else 1
        post = 2 ** (len(lead.names) - len(names)) // pre // mid
        second = len(names)
        lead.names = [name for name in lead.names if name not in names]
        rows, cols = [v.span for v in group], lead.keep.shape[-1]
        moves.append(([all_bits().index(name) for name in names], [(*r, 1 + len(v.came)) for r, v in zip(rows, group)]))
        arrays.append(
            [v.reshape(pre, 2, mid, second, post, v.shape[-2], cols) for s in group for v in (s.keep, *s.came)]
        )
        heads.append((names, pre, mid, post, sum(size for _, size in rows), cols))
    total = sum(v.size * 2 for group in arrays for v in group)
    steps = 1
    if total > 8 << 20:
        steps = next(n for n in (4, 2, 1) if all(pre % n == 0 or post % n == 0 for _, pre, _, post, _, _ in heads))
    ins, outs = [], []
    for group, (names, pre, mid, post, rows, cols) in zip(arrays, heads):
        by_pre = pre % steps == 0
        own_pre, own_post = (pre // steps, post) if by_pre else (pre, post // steps)
        for array in group:
            block = (own_pre, 2, mid, array.shape[3], own_post) + array.shape[5:]
            place = (lambda i, *_: (i, 0, 0, 0, 0, 0, 0)) if by_pre else (lambda i, *_: (0, 0, 0, 0, i, 0, 0))
            ins.append((array, None if steps == 1 else pl.BlockSpec(block, place)))
        place = (lambda i, *_: (i, 0, 0, 0, 0)) if by_pre else (lambda i, *_: (0, 0, i, 0, 0))
        spec = None if steps == 1 else pl.BlockSpec((own_pre, mid, own_post, rows, cols), place)
        outs += [((pre, mid, post, rows, cols), BF16, spec)] * 2 ** len(names)
    results = run(
        functools.partial(advance_kernel, moves), "advance", (steps,), ins, outs, scalars=(bits,), flops=total
    )
    for group, (names, pre, mid, post, rows, cols) in zip(groups, heads):
        lead = group[0]
        lead.span = (0, rows)
        lead.keep, *sends = [v.reshape((2,) * len(lead.names) + (rows, cols)) for v in results[: 2 ** len(names)]]
        results = results[2 ** len(names) :]
        partners = [names] if len(names) == 1 else [names[1:], names[:1], names]
        lead.came = [swap_many(send, partner) for send, partner in zip(sends, partners)]


def fence(scatters, *values):
    states = [(v.keep, v.came) for v in scatters]
    states, values = lax.optimization_barrier((states, values))
    for scatter, (keep, came) in zip(scatters, states):
        scatter.keep, scatter.came = keep, came
    return values


def head_norms(rows):
    wide = rows.astype(F32)
    shape = (rows.shape[1], LANES)
    head = lax.broadcasted_iota(jnp.int32, shape, 0) // HEAD_DIM == lax.broadcasted_iota(jnp.int32, shape, 1)
    return jnp.max(nn((wide * wide).astype(BF16), head.astype(F32).astype(BF16)), axis=0, keepdims=True)


def put_norms(norm_ref, rows):
    norms = head_norms(rows)

    @pl.when(pl.program_id(0) == 0)
    def _():
        norm_ref[...] = norms

    @pl.when(pl.program_id(0) > 0)
    def _():
        norm_ref[...] = jnp.maximum(norm_ref[...], norms)


def tag_lanes(tags, first):
    lane = lax.broadcasted_iota(jnp.int32, tags.shape, 1)
    tags = tags.astype(F32)
    kept = (tags[:, first : first + 1] == lane.astype(F32)) & (tags[:, first + 1 : first + 2] > 0)
    lanes = jnp.where(lane < 3, jnp.where(kept, 0.0, NEGATIVE), 0.0)
    return jnp.where((lane >= 3) & (lane < 6), 1.0, lanes).astype(BF16)


def own_project_kernel(
    x_ref,
    gain_ref,
    wq_ref,
    wk_ref,
    wv_ref,
    a_ref,
    q_ref,
    k_ref,
    v_ref,
    dec_ref,
    enc_ref,
    q_lanes_ref,
    q_norm_ref,
    k_norm_ref,
):
    width = gain_ref.shape[1]
    a = normed(x_ref[:, :width].astype(F32), gain_ref[...]).astype(BF16)
    a_ref[...] = a
    q = (nn(a, wq_ref[...]) * LOG2E).astype(BF16)
    k = nn(a, wk_ref[...]).astype(BF16)
    q_ref[...], k_ref[...] = q, k
    v_ref[...] = nn(a, wv_ref[...]).astype(BF16)
    put_norms(q_norm_ref, q), put_norms(k_norm_ref, k)
    tags = x_ref[:, width:]
    dec_ref[...], enc_ref[...] = tag_lanes(tags, 0), tag_lanes(tags, 2)
    lane = lax.broadcasted_iota(jnp.int32, tags.shape, 1)
    q_lanes_ref[...] = ((tags[:, 0:1].astype(F32) == lane.astype(F32)) & (lane < 3)).astype(F32).astype(BF16)


def other_project_kernel(
    x_ref,
    gain_ref,
    wk_ref,
    wv_ref,
    k_old,
    v_old,
    dec_old,
    enc_old,
    k_ref,
    v_ref,
    dec_ref,
    enc_ref,
    k_norm_ref,
):
    width = gain_ref.shape[1]
    a = normed(x_ref[:, :width].astype(F32), gain_ref[...]).astype(BF16)
    k = nn(a, wk_ref[...]).astype(BF16)
    k_ref[...] = k
    v_ref[...] = nn(a, wv_ref[...]).astype(BF16)
    put_norms(k_norm_ref, k)
    tags = x_ref[:, width:]
    dec_ref[...], enc_ref[...] = tag_lanes(tags, 0), tag_lanes(tags, 2)


def encoder_project_kernel(x_ref, wk_ref, wv_ref, *refs):
    k_ref, v_ref, k_norm_ref = refs[-3:]
    k = nn(x_ref[...], wk_ref[...]).astype(BF16)
    k_ref[...] = k
    put_norms(k_norm_ref, k)
    v_ref[...] = nn(x_ref[...], wv_ref[...]).astype(BF16)


def own_project(x, gain, wq, wk, wv, keys):
    rows, width = x.shape[0], gain.shape[1]
    tile = min(TILE, rows)
    spec, lanes = row_spec(tile, width), row_spec(tile, LANES)
    return run(
        own_project_kernel,
        "own_project",
        (rows // tile,),
        [(x, row_spec(tile, x.shape[1]), None), (gain, None), (wq, None), (wk, None), (wv, None)],
        [((n, width), BF16, spec) for n in (rows, rows, keys, keys)]
        + [((n, LANES), BF16, lanes) for n in (keys, keys, rows)]
        + [((1, LANES), F32, None)] * 2,
        flops=6 * rows * width * width,
    )


def other_project(x, gain, wk, wv, *so_far):
    rows, width = x.shape[0], gain.shape[1]
    tile = min(TILE, rows)
    shift = (so_far[0].shape[0] - rows) // tile
    spec, lanes = row_spec(tile, width, shift), row_spec(tile, LANES, shift)
    return run(
        other_project_kernel,
        "other_project",
        (rows // tile,),
        [(x, row_spec(tile, x.shape[1]), None), (gain, None), (wk, None), (wv, None)] + [(v, ANY) for v in so_far],
        [(v.shape, BF16, s) for v, s in zip(so_far, (spec, spec, lanes, lanes))] + [((1, LANES), F32, None)],
        aliases={4: 0, 5: 1, 6: 2, 7: 3},
        flops=4 * rows * width * width,
    )


def encoder_project(x, wk, wv, keys, so_far=()):
    rows, width = x.shape
    tile = min(TILE, rows)
    spec = row_spec(tile, width, (keys - rows) // tile if so_far else 0)
    return run(
        encoder_project_kernel,
        "encoder_project",
        (rows // tile,),
        [(x, row_spec(tile, width), None), (wk, None), (wv, None)] + [(v, ANY) for v in so_far],
        [((keys, width), BF16, spec)] * 2 + [((1, LANES), F32, None)],
        aliases={3: 0, 4: 1} if so_far else None,
        flops=4 * rows * width * width,
    )


def self_finish(mixed_ref, hidden_ref, w_out_ref, gain_ref, w_next_ref, hidden_out, norm_out, next_out, next_norm):
    rows = hidden_ref.shape[0]
    tile = min(TILE, rows)
    for at in range(0, rows, tile):
        o = jnp.concatenate([mixed_ref[p, at : at + tile, :] for p in range(PAIRS)], axis=1)
        hidden = hidden_ref[at : at + tile, :].astype(F32) + nn(o, w_out_ref[...])
        hidden_out[at : at + tile, :] = hidden
        b = normed(hidden, gain_ref[...]).astype(BF16)
        norm_out[at : at + tile, :] = b
        if w_next_ref is not None:
            following = (nn(b, w_next_ref[...]) * LOG2E).astype(BF16)
            next_out[at : at + tile, :] = following
            norms = head_norms(following)
            next_norm[...] = norms if at == 0 else jnp.maximum(next_norm[...], norms)


def ffn_kernel(mine_ref, c_ref, og_ref, wi_ref, wo_ref, h2_ref, gain_ref, wco_ref, *refs):
    layer_ref, dh2_ref, dyc_ref, doc_ref, dgain_ref, *grad_refs, y_sum, dc_sum, total_ref, turned_ref = refs
    step, steps = pl.program_id(0), pl.num_programs(0)
    mine = mine_ref[0]
    c, og, wi, wo = c_ref[...], og_ref[...], wi_ref[...], wo_ref[...]

    @pl.when(step == 0)
    def _():
        turned_ref[...] = c.T

    u = nn(c, wi)
    slope = math.sqrt(2.0 / math.pi)
    square = u * u
    bend = jnp.tanh(u * (slope + (slope * 0.044715) * square))
    half = 0.5 + 0.5 * bend
    wide = u * half
    g = wide.astype(BF16)
    rate = half + wide * ((1.0 - bend) * (slope + (slope * 3.0 * 0.044715) * square))
    y = nn(g, wo)
    du = (nt(og, wo) * rate).astype(BF16)
    dc = nt(du, wi)

    @pl.when(step == 0)
    def _():
        y_sum[...] = y
        dc_sum[...] = dc

    @pl.when(step > 0)
    def _():
        y_sum[...] += y
        dc_sum[...] += dc

    out_total, in_total = tn(g, og), nn(turned_ref[...], du)
    if len(grad_refs) == 4:
        total_ref[...] = out_total
        emit(mine, total_ref, grad_refs[0], grad_refs[1], 0, grad_refs[0].shape[2])
        total_ref[...] = in_total
        rows = grad_refs[2].shape[2] * grad_refs[2].shape[3] // total_ref.shape[1]
        emit(mine, total_ref, grad_refs[2], grad_refs[3], 0, rows)
    else:
        grad_refs[0][...] = out_total.astype(BF16)
        grad_refs[1][...] = in_total.astype(BF16)

    @pl.when(step == steps - 1)
    def _():
        rows = h2_ref.shape[0]
        tile = min(TILE, rows)
        dgain = jnp.zeros(dgain_ref.shape, F32)
        for at in range(0, rows, tile):
            part = slice(at, at + tile)
            hidden = h2_ref[part, :]
            layer_ref[part, :] = (hidden + y_sum[part, :]).astype(BF16)
            back, gain_part = norm_back(hidden, gain_ref[...], dc_sum[part, :])
            dgain = dgain + gain_part
            dh2 = og_ref[part, :].astype(F32) + back
            dh2_ref[part, :] = dh2
            dyc = dh2.astype(BF16)
            dyc_ref[part, :] = dyc
            doc_ref[part, :] = nt(dyc, wco_ref[...]).astype(BF16)
        dgain_ref[...] = dgain


def feed_forward(mine, c, og, wi, wo, h2, gain, wco, after=()):
    rows, width = c.shape
    hidden = wi.shape[1]
    dp_size, mem_size = lax.axis_size("dp"), lax.axis_size("mem")
    chunk = width
    steps = hidden // chunk
    direct = fits(width, width) and steps == 2 * mem_size and (chunk * dp_size) % (2 * hidden) == 0
    if direct:
        pairs, rows_o, cols_o = dp_size // 2, hidden // dp_size, width // mem_size
        chunk_rows = width // dp_size * (chunk // cols_o)
        grads = [
            (
                (mem_size, pairs, rows_o, cols_o),
                BF16,
                pl.BlockSpec((mem_size, pairs // steps, rows_o, cols_o), lambda f, *_: (0, f, 0, 0)),
            )
        ] * 2 + [
            (
                (mem_size, pairs, rows_o, cols_o),
                BF16,
                pl.BlockSpec((1, pairs, chunk_rows, cols_o), lambda f, *_: (f // 2, 0, f % 2, 0)),
            )
        ] * 2
    else:
        grads = [
            ((hidden, width), BF16, pl.BlockSpec((chunk, width), lambda f, *_: (f, 0))),
            ((width, hidden), BF16, pl.BlockSpec((width, chunk), lambda f, *_: (0, f))),
        ]
    outs = run(
        ffn_kernel,
        "feed_forward",
        (steps,),
        [
            (c, None),
            (og, None),
            (wi, pl.BlockSpec((width, chunk), lambda f, *_: (0, f))),
            (wo, pl.BlockSpec((chunk, width), lambda f, *_: (f, 0))),
            (h2, None),
            (gain, None),
            (wco, None),
        ],
        [
            (c.shape, BF16, None),
            (c.shape, F32, None),
            (c.shape, BF16, None),
            (c.shape, BF16, None),
            (gain.shape, F32, None),
        ]
        + grads,
        scratch=[
            pltpu.VMEM(c.shape, F32),
            pltpu.VMEM(c.shape, F32),
            pltpu.VMEM((chunk, width), F32),
            pltpu.VMEM((width, rows), BF16),
        ],
        scalars=(mine,),
        after=after,
        flops=12 * rows * width * hidden,
    )
    grads = outs[5:]
    return outs[:5], [grads[0:2], grads[2:4]] if direct else [grads[0:1], grads[1:2]]


def cross_finish_kernel(
    mine_ref, dq0_ref, dq1_ref, wq_ref, h1_ref, gain_ref, dh2_ref, o_ref, oc_ref, dyc_ref, b_ref, wso_ref, *refs
):
    dh1_ref, do_ref, dgain_ref, *grad_refs, dy_ref, total_ref = refs
    mine = mine_ref[0]
    dq = jnp.concatenate([dq0_ref[...], dq1_ref[...]], axis=1)
    rows = h1_ref.shape[0]
    tile = min(TILE, rows)
    write_square(mine, 0, tn(oc_ref[...], dyc_ref[...]), total_ref, grad_refs)
    write_square(mine, 1, tn(b_ref[...], dq), total_ref, grad_refs)
    dgain = jnp.zeros(dgain_ref.shape, F32)
    for at in range(0, rows, tile):
        part = slice(at, at + tile)
        db = nt(dq[part, :], wq_ref[...])
        back, gain_part = norm_back(h1_ref[part, :], gain_ref[...], db)
        dgain = dgain + gain_part
        dh1 = dh2_ref[part, :] + back
        dh1_ref[part, :] = dh1
        dy = dh1.astype(BF16)
        dy_ref[part, :] = dy
        do_ref[part, :] = nt(dy, wso_ref[...]).astype(BF16)
    dgain_ref[...] = dgain
    write_square(mine, 2, tn(o_ref[...], dy_ref[...]), total_ref, grad_refs)


def cross_finish(mine, dq, wq, h1, gain, dh2, o, oc, dyc, b, wso, after=()):
    rows, width = h1.shape
    outs = run(
        cross_finish_kernel,
        "cross_finish",
        (1,),
        [(v, None) for v in (*dq, wq, h1, gain, dh2, o, oc, dyc, b, wso)],
        [(h1.shape, F32, None, pltpu.HBM), (h1.shape, BF16, None), (gain.shape, F32, None)] + square_outs(3, width),
        scratch=[pltpu.VMEM(h1.shape, BF16), pltpu.VMEM((width, width), F32)],
        scalars=(mine,),
        after=after,
        flops=10 * rows * width * width,
    )
    return outs[:3], outs[3:]


def summed(own_refs, came_refs, index):
    return jnp.concatenate(
        [
            (own[index].astype(F32) + came[index].astype(F32)).astype(BF16)
            for own, came in zip(own_refs, came_refs)
        ],
        axis=1,
    )


def encoder_finish_kernel(mine_ref, own0_ref, own1_ref, came0_ref, came1_ref, x_ref, wk_ref, wv_ref, *refs):
    dx_ref, *grad_refs, total_ref = refs
    mine = mine_ref[0]
    dk = summed((own0_ref, own1_ref), (came0_ref, came1_ref), 0)
    dv = summed((own0_ref, own1_ref), (came0_ref, came1_ref), 1)
    x = x_ref[...]
    dx_ref[...] = (nt(dk, wk_ref[...]) + nt(dv, wv_ref[...])).astype(BF16)
    write_square(mine, 0, tn(x, dk), total_ref, grad_refs)
    write_square(mine, 1, tn(x, dv), total_ref, grad_refs)


def encoder_finish(mine, own, came, x, wk, wv, after=()):
    rows, width = x.shape
    outs = run(
        encoder_finish_kernel,
        "encoder_finish",
        (1,),
        [(v, None) for v in (*own, *came, x, wk, wv)],
        [(x.shape, BF16, None)] + square_outs(2, width),
        scratch=[pltpu.VMEM((width, width), F32)],
        scalars=(mine,),
        after=after,
        flops=8 * rows * width * width,
    )
    return outs[0], outs[1:]


def query_grad_kernel(mine_ref, dq0_ref, dq1_ref, a_ref, *refs):
    *grad_refs, total_ref = refs
    dq = jnp.concatenate([dq0_ref[...], dq1_ref[...]], axis=1)
    write_square(mine_ref[0], 0, tn(a_ref[...], dq), total_ref, grad_refs)


def query_grad(mine, dq, a):
    rows, width = a.shape
    return run(
        query_grad_kernel,
        "query_grad",
        (1,),
        [(v, None) for v in (*dq, a)],
        square_outs(1, width),
        scratch=[pltpu.VMEM((width, width), F32)],
        scalars=(mine,),
        flops=2 * rows * width * width,
    )


def key_grads_kernel(mine_ref, own0_ref, own1_ref, came0_ref, came1_ref, a_ref, *refs):
    sums_ref, *grad_refs, total_ref = refs
    a = a_ref[...]
    for i in range(2):
        total = summed((own0_ref, own1_ref), (came0_ref, came1_ref), i)
        sums_ref[i] = total
        write_square(mine_ref[0], i, tn(a, total), total_ref, grad_refs)


def key_grads(mine, own, came, a, after=()):
    rows, width = a.shape
    outs = run(
        key_grads_kernel,
        "key_grads",
        (1,),
        [(v, None) for v in (*own, *came, a)],
        [((2, rows, width), BF16, None)] + square_outs(2, width),
        scratch=[pltpu.VMEM((width, width), F32)],
        scalars=(mine,),
        after=after,
        flops=4 * rows * width * width,
    )
    return outs[0], outs[1:]


def self_finish_back_kernel(
    dq0_ref, dq1_ref, sums_ref, x_ref, gain_ref, dh1_ref, wq_ref, wk_ref, wv_ref, small_ref, dx_ref, small_out
):
    @pl.when(pl.program_id(0) == 0)
    def _():
        small_out[...] = small_ref[...]

    dq = jnp.concatenate([dq0_ref[...], dq1_ref[...]], axis=1)
    da = nt(dq, wq_ref[...]) + nt(sums_ref[0], wk_ref[...]) + nt(sums_ref[1], wv_ref[...])
    back, gain_part = norm_back(x_ref[...].astype(F32), gain_ref[...], da)
    small_out[0:1, :] += gain_part
    dx_ref[...] = (dh1_ref[...] + back).astype(BF16)


def self_finish_back(dq, sums, x, gain, dh1, wq, wk, wv, small):
    rows, width = dh1.shape
    tile = min(TILE, rows)
    spec = row_spec(tile, width)
    return run(
        self_finish_back_kernel,
        "self_finish_back",
        (rows // tile,),
        [
            (dq[0], row_spec(tile, dq[0].shape[1])),
            (dq[1], row_spec(tile, dq[1].shape[1])),
            (sums, pl.BlockSpec((2, tile, width), lambda i, *_: (0, i, 0)), None),
            (x, spec),
            (gain, None),
            (dh1, spec),
            (wq, None),
            (wk, None),
            (wv, None),
            (small, None),
        ],
        [((rows, width), BF16, spec), (small.shape, F32, None)],
        flops=6 * rows * width * width,
    )


SCORE_BOUND = 80.0


def mark_small(small_ref, q_norm_ref, *k_norm_refs):
    @pl.when(pl.program_id(0) == 0)
    def _():
        k_norm = k_norm_refs[0][...]
        for ref in k_norm_refs[1:]:
            k_norm = jnp.maximum(k_norm, ref[...])
        largest = jnp.max(q_norm_ref[...] * k_norm)
        small_ref[0] = (largest <= 0.95 * SCORE_BOUND**2).astype(jnp.int32)


def self_scores(i, head, blocks, q_ref, k_ref, table_ref, q_lanes_ref, k_lanes_ref):
    piece = q_ref.shape[0] // 2
    mem_size = k_ref.shape[0] // q_ref.shape[0]
    q_at = pl.multiple_of(blocks[0, i], piece)
    k_at = pl.multiple_of(blocks[1, i], piece)
    q = half_of(q_ref[pl.ds(q_at, piece), :], head)
    q = jnp.concatenate([q, q_lanes_ref[pl.ds(q_at, piece), :]], axis=1)
    k = jnp.concatenate([k_ref[pl.ds(k_at, piece), :], k_lanes_ref[pl.ds(k_at, piece), :]], axis=1)
    return with_bias(nt(q, k), table_ref, head, 2 * mem_size - i if i >= mem_size else blocks[2, i])


def add_mixed(sums, i, mixed, low, mem_size):
    if i == 0:
        sums[0] = mixed
    elif i < mem_size:
        part = jnp.where(low, mixed, 0.0)
        sums[0] = sums[0] + part
        sums[1] = mixed - part if sums[1] is None else sums[1] + (mixed - part)
    else:
        sums[1] = mixed if sums[1] is None else sums[1] + mixed


def self_forward_kernel(
    blocks,
    q_ref,
    k_ref,
    v_ref,
    table_ref,
    q_lanes_ref,
    k_lanes_ref,
    hidden_ref,
    w_out_ref,
    gain_ref,
    w_next_ref,
    q_norm_ref,
    k_norm0_ref,
    k_norm1_ref,
    o_ref,
    back_lanes_ref,
    hidden_out,
    norm_out,
    next_out,
    next_norm,
    s_ref,
    mixed_ref,
    small_ref,
):
    rows = q_ref.shape[0]
    piece = rows // 2
    mem_size = k_ref.shape[0] // rows
    count = 2 * mem_size + 1
    ones = jnp.ones((piece, LANES), BF16)
    scores = functools.partial(
        self_scores,
        blocks=blocks,
        q_ref=q_ref,
        k_ref=k_ref,
        table_ref=table_ref,
        q_lanes_ref=q_lanes_ref,
        k_lanes_ref=k_lanes_ref,
    )
    mark_small(small_ref, q_norm_ref, k_norm0_ref, k_norm1_ref)

    def mix(i, p):
        k_at = pl.multiple_of(blocks[1, i], piece)
        return nn(p.astype(BF16), jnp.concatenate([v_ref[pl.ds(k_at, piece), :], ones], axis=1))

    def put(outs):
        for i in range(2):
            mixed = join_halves(outs[0][i], outs[1][i]).astype(BF16)
            o_ref[i * piece : (i + 1) * piece, :] = mixed
            mixed_ref[pl.program_id(0), i * piece : (i + 1) * piece, :] = mixed

    def close(head, sums, tops):
        mixed = []
        for at, total, top in ((0, sums[0], tops[0]), (piece, sums[1], tops[1])):
            weight = total[:, LANES:]
            mixed.append(total[:, :LANES] / weight)
            log_sum = jnp.log2(weight) if top is None else top + jnp.log2(weight)
            back_lanes_ref[head, at : at + piece, :] = with_log_sum(q_lanes_ref[at : at + piece, :], log_sum)
        return mixed

    @pl.when(small_ref[0] == 1)
    def _():
        outs = []
        for head in range(2):
            sums = [None, None]
            for i in range(count):
                add_mixed(sums, i, mix(i, jnp.exp2(scores(i, head))), blocks[3, i] == 1, mem_size)
            outs.append(close(head, sums, (None, None)))
        put(outs)

    @pl.when(small_ref[0] == 0)
    def _():
        outs = []
        for head in range(2):
            tops = []
            for i in range(count):
                s = scores(i, head)
                s_ref[i] = s
                tops.append(jnp.max(s, axis=1, keepdims=True))
            top_low, top_high = tops[0], tops[mem_size]
            for i in range(mem_size + 1, count):
                top_high = jnp.maximum(top_high, tops[i])
            for i in range(1, mem_size):
                low = blocks[3, i] == 1
                top_low = jnp.maximum(top_low, jnp.where(low, tops[i], NEGATIVE))
                top_high = jnp.maximum(top_high, jnp.where(low, NEGATIVE, tops[i]))
            sums = [None, None]
            for i in range(count):
                low = blocks[3, i] == 1
                top = top_low if i == 0 else top_high if i >= mem_size else jnp.where(low, top_low, top_high)
                add_mixed(sums, i, mix(i, jnp.exp2(s_ref[i] - top)), low, mem_size)
            outs.append(close(head, sums, (top_low, top_high)))
        put(outs)

    @pl.when(pl.program_id(0) == PAIRS - 1)
    def _():
        self_finish(
            mixed_ref, hidden_ref, w_out_ref, gain_ref, w_next_ref, hidden_out, norm_out, next_out, next_norm
        )


def pair_spec(rows):
    return pl.BlockSpec((rows, LANES), lambda p, *_: (0, p))


def whole_spec(rows):
    return pl.BlockSpec((rows, LANES), lambda p, *_: (0, 0))


def lanes_spec(rows):
    return pl.BlockSpec((2, rows, LANES), lambda p, *_: (p, 0, 0))


def cross_forward_kernel(
    q_ref,
    k_ref,
    v_ref,
    q_lanes_ref,
    k_lanes_ref,
    hidden_ref,
    w_out_ref,
    gain_ref,
    q_norm_ref,
    k_norm0_ref,
    k_norm1_ref,
    o_ref,
    back_lanes_ref,
    hidden_out,
    norm_out,
    mixed_ref,
    small_ref,
):
    rows, keys = q_ref.shape[0], k_ref.shape[0]
    tile, key_tile = min(256, rows), min(256, keys)
    mark_small(small_ref, q_norm_ref, k_norm0_ref, k_norm1_ref)

    def put(part, outs):
        mixed = join_halves(outs[0], outs[1]).astype(BF16)
        o_ref[part, :] = mixed
        mixed_ref[pl.program_id(0), part, :] = mixed

    @pl.when(small_ref[0] == 1)
    def _():
        ones = jnp.ones((key_tile, LANES), BF16)
        outs = []
        for head in range(2):
            q = jnp.concatenate([half_of(q_ref[...], head), q_lanes_ref[...]], axis=1)
            total = None
            for at in range(0, keys, key_tile):
                part = slice(at, at + key_tile)
                k = jnp.concatenate([k_ref[part, :], k_lanes_ref[part, :]], axis=1)
                v = jnp.concatenate([v_ref[part, :], ones], axis=1)
                mixed = nn(jnp.exp2(nt(q, k)).astype(BF16), v)
                total = mixed if total is None else total + mixed
            weight = total[:, LANES:]
            outs.append(total[:, :LANES] / weight)
            back_lanes_ref[head] = with_log_sum(q_lanes_ref[...], jnp.log2(weight))
        put(slice(0, rows), outs)

    @pl.when(small_ref[0] == 0)
    def _():
        k = jnp.concatenate([k_ref[...], k_lanes_ref[...]], axis=1)
        v = jnp.concatenate([v_ref[...], jnp.ones((keys, LANES), BF16)], axis=1)
        for at in range(0, rows, tile):
            part = slice(at, at + tile)
            outs = []
            for head in range(2):
                q = jnp.concatenate([half_of(q_ref[part, :], head), q_lanes_ref[part, :]], axis=1)
                s = nt(q, k)
                top = jnp.max(s, axis=1, keepdims=True)
                total = nn(jnp.exp2(s - top).astype(BF16), v)
                weight = total[:, LANES:]
                outs.append(total[:, :LANES] / weight)
                back_lanes_ref[head, part, :] = with_log_sum(q_lanes_ref[part, :], top + jnp.log2(weight))
            put(part, outs)

    @pl.when(pl.program_id(0) == PAIRS - 1)
    def _():
        self_finish(mixed_ref, hidden_ref, w_out_ref, gain_ref, None, hidden_out, norm_out, None, None)


def grad_lanes(o, do):
    inner = jnp.sum(o.astype(F32) * do.astype(F32), axis=1, keepdims=True)
    pieces = [piece.astype(F32) for piece in in_three(-inner)]
    return put_lanes(jnp.zeros(do.shape, F32), 0, pieces).astype(BF16)


def put_parts(at, dk, dv, own_ref, other_ref):
    rows = own_ref.shape[1]
    ref, start = (own_ref, at) if at < rows else (other_ref, at - rows)
    ref[0, start : start + dk.shape[0], :] = (dk * LN2).astype(BF16)
    ref[1, start : start + dv.shape[0], :] = dv.astype(BF16)


def cross_backward_kernel(
    q_ref, k_ref, v_ref, o_ref, do_ref, back_lanes_ref, k_lanes_ref, dq_ref, own_ref, other_ref
):
    rows, keys = q_ref.shape[0], k_ref.shape[0]
    tile = min(256, rows)
    k_turned = k_ref[...].T
    k_wide = jnp.concatenate([k_ref[...], k_lanes_ref[...]], axis=1)
    v_wide = jnp.concatenate([v_ref[...], jnp.ones((keys, LANES), BF16)], axis=1)
    dk = dv = None
    for at in range(0, rows, tile):
        part = slice(at, at + tile)
        dqs = []
        for head in range(2):
            q, do = half_of(q_ref[part, :], head), half_of(do_ref[part, :], head)
            q_wide = jnp.concatenate([q, back_lanes_ref[head, part, :]], axis=1)
            do_wide = jnp.concatenate([do, grad_lanes(o_ref[part, :], do)], axis=1)
            p = jnp.exp2(nt(k_wide, q_wide))
            ds = (p * nt(v_wide, do_wide)).astype(BF16)
            dv_part, dk_part = nn(p.astype(BF16), do), nn(ds, q)
            dv = dv_part if dv is None else dv + dv_part
            dk = dk_part if dk is None else dk + dk_part
            dqs.append(nn(k_turned[head * HEAD_DIM : (head + 1) * HEAD_DIM, :], ds))
        dq_ref[part, :] = jnp.concatenate(dqs, axis=0).T.astype(BF16)
    for at, size in ((0, rows), (rows, keys - rows)):
        put_parts(at, dk[at : at + size], dv[at : at + size], own_ref, other_ref)


def self_backward_kernel(
    blocks,
    q_ref,
    k_ref,
    v_ref,
    o_ref,
    do_ref,
    back_lanes_ref,
    k_lanes_ref,
    table_ref,
    dq_ref,
    own_ref,
    other_ref,
    grad_ref,
    do_lanes_ref,
    dq_sum,
    dk_sum,
    dv_sum,
):
    rows = q_ref.shape[0]
    piece = rows // 2
    mem_size = k_ref.shape[0] // rows
    count = 2 * mem_size + 1
    ones = jnp.ones((piece, LANES), BF16)
    for head in range(2):
        do_lanes_ref[head] = grad_lanes(o_ref[...], half_of(do_ref[...], head))
    dq_sum[...] = jnp.zeros_like(dq_sum)
    dk_sum[...] = jnp.zeros_like(dk_sum)
    dv_sum[...] = jnp.zeros_like(dv_sum)
    grad_ref[...] = jnp.zeros_like(grad_ref)
    for i in reversed(range(count)):
        q_at = pl.multiple_of(blocks[0, i], piece)
        k_at = pl.multiple_of(blocks[1, i], piece)
        k, v = k_ref[pl.ds(k_at, piece), :], v_ref[pl.ds(k_at, piece), :]
        k_turned = k.T
        k_wide = jnp.concatenate([k, k_lanes_ref[pl.ds(k_at, piece), :]], axis=1)
        v_wide = jnp.concatenate([v, ones], axis=1)
        dk = dv = None
        dqs = []
        for head in range(2):
            q = half_of(q_ref[pl.ds(q_at, piece), :], head)
            do = half_of(do_ref[pl.ds(q_at, piece), :], head)
            q_wide = jnp.concatenate([q, back_lanes_ref[head, pl.ds(q_at, piece), :]], axis=1)
            do_wide = jnp.concatenate([do, do_lanes_ref[head, pl.ds(q_at, piece), :]], axis=1)
            s = nt(k_wide, q_wide)
            kind = 2 * mem_size - i if i >= mem_size else blocks[2, i]
            p = jnp.exp2(with_bias(s, table_ref, head, kind, turned=True))
            ds = p * nt(v_wide, do_wide)
            add_grad(ds, grad_ref, head, kind)
            ds = ds.astype(BF16)
            dv_part, dk_part = nn(p.astype(BF16), do), nn(ds, q)
            dv = dv_part if dv is None else dv + dv_part
            dk = dk_part if dk is None else dk + dk_part
            dqs.append(nn(k_turned[head * HEAD_DIM : (head + 1) * HEAD_DIM, :], ds))
        which = 1 - blocks[3, i]
        dq_sum[which] = dq_sum[which] + jnp.concatenate(dqs, axis=0)
        dk_sum[pl.ds(k_at, piece), :] = dk_sum[pl.ds(k_at, piece), :] + dk
        dv_sum[pl.ds(k_at, piece), :] = dv_sum[pl.ds(k_at, piece), :] + dv
    for i in range(2):
        dq_ref[i * piece : (i + 1) * piece, :] = dq_sum[i].T.astype(BF16)
    for at in (0, rows):
        size = rows if at == 0 else k_ref.shape[0] - rows
        put_parts(at, dk_sum[at : at + size, :], dv_sum[at : at + size, :], own_ref, other_ref)


def table_spec(table):
    return pl.BlockSpec((2,) + table.shape[1:], lambda p, *_: (p, 0, 0, 0))


def attention_flops(scores, matmuls):
    return 2 * HEADS * scores * 256 * matmuls


def self_forward(blocks, q, k, v, table, q_lanes, k_lanes, hidden, w_out, gain, w_next, norms, after=()):
    rows, keys = q.shape[0], k.shape[0]
    piece = rows // 2
    return run(
        self_forward_kernel,
        "self_forward",
        (PAIRS,),
        [
            (q, pair_spec(rows)),
            (k, pair_spec(keys)),
            (v, pair_spec(keys)),
            (table, table_spec(table)),
            (q_lanes, None),
            (k_lanes, None, pltpu.HBM),
            (hidden, pl.BlockSpec((rows, gain.shape[1]), lambda *_: (0, 0))),
            (w_out, None),
            (gain, None),
            (w_next, None),
        ]
        + [(norm, None) for norm in norms],
        [
            (q.shape, BF16, pair_spec(rows)),
            ((HEADS, rows, LANES), BF16, lanes_spec(rows)),
            (q.shape, F32, None),
            (q.shape, BF16, None),
            (q.shape, BF16, None),
            ((1, LANES), F32, None),
        ],
        scratch=[
            pltpu.VMEM((blocks.shape[1], piece, piece), F32),
            pltpu.VMEM((PAIRS, rows, LANES), BF16),
            pltpu.SMEM((1,), jnp.int32),
        ],
        scalars=(blocks,),
        after=after,
        flops=attention_flops(blocks.shape[1] * piece * piece, 2),
    )


def cross_forward(q, k, v, q_lanes, k_lanes, hidden, w_out, gain, norms, after=()):
    rows, keys = q.shape[0], k.shape[0]
    return run(
        cross_forward_kernel,
        "cross_forward",
        (PAIRS,),
        [
            (q, pair_spec(rows)),
            (k, pair_spec(keys)),
            (v, pair_spec(keys)),
            (q_lanes, None),
            (k_lanes, None, pltpu.HBM),
            (hidden, None),
            (w_out, None),
            (gain, None),
        ]
        + [(norm, None) for norm in norms],
        [
            (q.shape, BF16, pair_spec(rows)),
            ((HEADS, rows, LANES), BF16, lanes_spec(rows)),
            (q.shape, F32, None),
            (q.shape, BF16, None),
        ],
        scratch=[pltpu.VMEM((PAIRS, rows, LANES), BF16), pltpu.SMEM((1,), jnp.int32)],
        after=after,
        flops=attention_flops(rows * keys, 2),
    )


def half_spec(rows, start):
    return pl.BlockSpec((rows, LANES), lambda p, *_: (0, p + start))


def cross_backward(q, k, v, o, do, back_lanes, k_lanes, start, count, after=()):
    rows, keys = q.shape[0], k.shape[0]
    width = count * LANES
    parts = pl.BlockSpec((2, rows, LANES), lambda p, *_: (0, 0, p))
    others_spec = pl.BlockSpec((2, keys - rows, LANES), lambda p, *_: (0, 0, p))
    return run(
        cross_backward_kernel,
        "cross_backward",
        (count,),
        [
            (q, half_spec(rows, start)),
            (k, half_spec(keys, start)),
            (v, half_spec(keys, start)),
            (o, half_spec(rows, start)),
            (do, half_spec(rows, start), None),
            (back_lanes, pl.BlockSpec((2, rows, LANES), lambda p, *_: (p + start, 0, 0))),
            (k_lanes, None, pltpu.HBM),
        ],
        [
            ((rows, width), BF16, pair_spec(rows)),
            ((2, rows, width), BF16, parts),
            ((2, keys - rows, width), BF16, others_spec),
        ],
        after=after,
        flops=attention_flops(rows * keys, 5) * count // PAIRS,
    )


def self_backward(blocks, q, k, v, o, do, back_lanes, k_lanes, table_t, start, count, after=()):
    rows, keys = q.shape[0], k.shape[0]
    piece = rows // 2
    width = count * LANES
    parts = pl.BlockSpec((2, rows, LANES), lambda p, *_: (0, 0, p))
    others_spec = pl.BlockSpec((2, keys - rows, LANES), lambda p, *_: (0, 0, p))
    return run(
        self_backward_kernel,
        "self_backward",
        (count,),
        [
            (q, half_spec(rows, start)),
            (k, half_spec(keys, start)),
            (v, half_spec(keys, start)),
            (o, half_spec(rows, start)),
            (do, half_spec(rows, start), None),
            (back_lanes, pl.BlockSpec((2, rows, LANES), lambda p, *_: (p + start, 0, 0))),
            (k_lanes, None, pltpu.HBM),
            (table_t, pl.BlockSpec((2,) + table_t.shape[1:], lambda p, *_: (p + start, 0, 0, 0))),
        ],
        [
            ((rows, width), BF16, pair_spec(rows)),
            ((2, rows, width), BF16, parts),
            ((2, keys - rows, width), BF16, others_spec),
            ((2 * count,) + table_t.shape[1:], F32, table_spec(table_t)),
        ],
        scratch=[
            pltpu.VMEM((2, rows, LANES), BF16),
            pltpu.VMEM((2, LANES, piece), F32),
            pltpu.VMEM((keys, LANES), F32),
            pltpu.VMEM((keys, LANES), F32),
        ],
        scalars=(blocks,),
        after=after,
        flops=attention_flops(blocks.shape[1] * piece * piece, 5) * count // PAIRS,
    )


def on_device(
    decoder_in,
    encoder_out,
    dec_segments,
    dec_mask,
    enc_segments,
    enc_mask,
    self_gain,
    cross_gain,
    ffn_gain,
    rel_bias,
    self_query,
    self_key,
    self_value,
    self_out,
    cross_query,
    cross_key,
    cross_value,
    cross_out,
    ffn_in,
    ffn_out,
    out_grad,
):
    mem_size = lax.axis_size("mem")
    rows, width = decoder_in.shape[1:]
    keys = rows * mem_size
    dp_index = lax.axis_index("dp")
    mine = (dp_index % 2).astype(jnp.int32)[None]
    group = group_of(dp_index, lax.axis_index("mem"), mem_size)
    odd = group % 2 == 1
    blocks = block_list(group, mem_size, rows)
    bits = bit_values()
    gain_self, gain_cross, gain_ffn = (g[None, :] for g in (self_gain, cross_gain, ffn_gain))
    first, rest = PAIRS // 2, PAIRS - PAIRS // 2

    lane = jnp.arange(LANES, dtype=jnp.int32)[None, :]
    tags = jnp.zeros((rows, LANES), jnp.int32)
    for i, tag in enumerate((dec_segments, dec_mask, enc_segments, enc_mask)):
        tags = jnp.where(lane == i, tag[0][:, None], tags)
    pieces = to_rows(jnp.concatenate([decoder_in[0], tags.astype(BF16)], axis=1))
    table, table_t = bias_tables(rel_bias, small_block(rows // 2))
    pair_in = jnp.stack([encoder_out[0], out_grad[0]])
    pieces, table, table_t, pair_in = fence([], pieces, table, table_t, pair_in)
    hidden_own = arranged(pieces, odd)

    hidden_others = jnp.concatenate(others(hidden_own))
    pair_pieces = to_rows(pair_in, axis=1)
    self_in, query_rows, *so_far, q_lanes, q_norm, k_norm0 = own_project(
        hidden_own, gain_self, self_query, self_key, self_value, keys
    )
    hidden_others, so_far = fence([], hidden_others, so_far)
    key_all, value_all, dec_lanes, enc_lanes, k_norm1 = other_project(hidden_others, gain_self, self_key, self_value, *so_far)
    self_mixed, self_lanes, hidden_one, cross_in, cross_rows, cross_norm = self_forward(
        blocks,
        query_rows,
        key_all,
        value_all,
        table,
        q_lanes,
        dec_lanes,
        hidden_own,
        self_out,
        gain_cross,
        cross_query,
        (q_norm, k_norm0, k_norm1),
    )
    pair_pieces, cross_rows = fence([], pair_pieces, cross_rows)

    encoder_own, cotangent = arranged(pair_pieces, odd, axis=1)
    encoder_others = jnp.concatenate(others(encoder_own))
    *so_far, k_norm0 = encoder_project(encoder_own, cross_key, cross_value, keys)
    encoder_others, so_far = fence([], encoder_others, so_far)

    cross_key_all, cross_value_all, k_norm1 = encoder_project(encoder_others, cross_key, cross_value, keys, so_far)
    cross_mixed, cross_lanes, hidden_two, ffn_input = cross_forward(
        cross_rows,
        cross_key_all,
        cross_value_all,
        q_lanes,
        enc_lanes,
        hidden_one,
        cross_out,
        gain_ffn,
        (cross_norm, k_norm0, k_norm1),
    )
    (layer_out, hidden_two_grad, cross_branch_grad, cross_mixed_grad, ffn_gain_grad), ffn_grads = feed_forward(
        mine, ffn_input, cotangent, ffn_in, ffn_out, hidden_two, gain_ffn, cross_out
    )

    ffn_a, ffn_b = Scatter(ffn_grads[0], "xyz"), Scatter(ffn_grads[1], "yxz", ffn_in.shape[1] // width)
    layer_out = from_rows(layer_out, odd)

    def cross_half(start, count, do):
        return cross_backward(
            cross_rows, cross_key_all, cross_value_all, cross_mixed, do, cross_lanes, enc_lanes, start, count
        )

    cross_q0, cross_own0, cross_other0 = cross_half(0, first, cross_mixed_grad)
    layer_out, cross_q0, cross_own0, cross_other0, cross_mixed_grad = fence(
        [ffn_a, ffn_b], layer_out, cross_q0, cross_own0, cross_other0, cross_mixed_grad
    )

    advance(bits, ffn_a, ffn_b)
    came0 = came_parts(cross_other0, rows)
    cross_q1, cross_own1, cross_other1 = cross_half(first, rest, cross_mixed_grad)
    came0, cross_q1, cross_own1, cross_other1 = fence([], came0, cross_q1, cross_own1, cross_other1)

    came1 = came_parts(cross_other1, rows)
    (hidden_one_grad, self_mixed_grad, cross_gain_grad), grads = cross_finish(
        mine,
        (cross_q0, cross_q1),
        cross_query,
        hidden_one,
        gain_cross,
        hidden_two_grad,
        self_mixed,
        cross_mixed,
        cross_branch_grad,
        cross_in,
        self_out,
    )
    came1, hidden_one_grad, self_mixed_grad, grads = fence(
        [ffn_a, ffn_b], came1, hidden_one_grad, self_mixed_grad, grads
    )

    advance(bits, ffn_a, ffn_b)
    rest_a = Scatter(grads, "xyz")
    encoder_out_grad, grads = encoder_finish(
        mine, (cross_own0, cross_own1), (came0, came1), encoder_own, cross_key, cross_value, after=[ffn_a.keep]
    )
    encoder_out_grad, grads, self_mixed_grad = fence([rest_a], encoder_out_grad, grads, self_mixed_grad)

    rest_b = Scatter(grads, "yxz")
    encoder_out_grad = from_rows(encoder_out_grad, odd)

    def self_half(start, count, do):
        return self_backward(
            blocks, query_rows, key_all, value_all, self_mixed, do, self_lanes, dec_lanes, table_t, start, count
        )

    self_q0, self_own0, self_other0, table_grad0 = self_half(0, first, self_mixed_grad)
    encoder_out_grad, self_q0, self_own0, self_other0, self_mixed_grad = fence(
        [ffn_a, ffn_b, rest_a, rest_b], encoder_out_grad, self_q0, self_own0, self_other0, self_mixed_grad
    )

    level(ffn_a, ffn_b, bits=bits)
    advance(bits, (ffn_a, ffn_b), rest_a, rest_b)
    came0 = came_parts(self_other0, rows)
    self_q1, self_own1, self_other1, table_grad1 = self_half(first, rest, self_mixed_grad)
    came0, self_q1, self_own1, self_other1, table_grad1 = fence(
        [ffn_a, rest_b], came0, self_q1, self_own1, self_other1, table_grad1
    )

    came1 = came_parts(self_other1, rows)
    query_grads = query_grad(mine, (self_q0, self_q1), self_in)
    (query_grads,) = fence([], query_grads)

    own_q = Scatter(query_grads, "yxz")
    small = table_sums(table_grad0, table_grad1, cross_gain_grad, ffn_gain_grad)
    came1, small = fence([ffn_a, rest_a, rest_b, own_q], came1, small)

    advance(bits, ffn_a, rest_a, rest_b, own_q)
    sums, grads = key_grads(mine, (self_own0, self_own1), (came0, came1), self_in, after=[rest_a.keep])
    sums, grads = fence([], sums, grads)

    own = Scatter(grads, "yxz")
    decoder_in_grad, small = self_finish_back(
        (self_q0, self_q1),
        sums,
        hidden_own,
        gain_self,
        hidden_one_grad,
        self_query,
        self_key,
        self_value,
        small,
    )
    decoder_in_grad, small = fence([ffn_a, rest_a, rest_b, own_q, own], decoder_in_grad, small)

    small_bits = [("dp", 0), ("dp", 2), ("mem", 0), ("dp", 1), ("dp", 3)]
    small_bits = [name for name in small_bits if name in all_bits()]
    small_bits += [name for name in all_bits() if name not in small_bits]

    def add_small(small, rounds=1):
        for _ in range(min(rounds, len(small_bits))):
            small = small + swap_many(small, (small_bits.pop(0),))
        return small

    own_k, own_v = own.parts("yxz", "xyz")
    level(rest_a, rest_b, bits=bits)
    advance(bits, own_k, own_v, own_q, (rest_a, rest_b))
    (small,) = fence([own_k, own_v, own_q, rest_a], add_small(small, 2))

    advance(bits, own_k, own_v)
    decoder_in_grad = from_rows(decoder_in_grad, odd)
    (small,) = fence([own_k, own_v], add_small(small))

    level(own_k, own_v, own_q, bits=bits)
    advance(bits, (own_k, own_v, own_q), rest_a)
    (small,) = fence([own_k], add_small(small))
    small = add_small(small, len(small_bits))
    for scatter in (own_k, ffn_a, rest_a):
        while scatter.order:
            advance(bits, scatter)
    parts = small
    self_gain_sum, cross_gain_sum, ffn_gain_sum, table_sum, grad_fo, grad_fi, *squares = write_grads(
        ffn_a, rest_a, own_k, parts, small_block(rows // 2), width, ffn_in.shape[1]
    )
    self_gain_sum, cross_gain_sum, ffn_gain_sum = self_gain_sum[0], cross_gain_sum[0], ffn_gain_sum[0]
    grad_co, grad_cq, grad_so, grad_ck, grad_cv, grad_sk, grad_sv, grad_sq = squares
    return (
        layer_out[None],
        decoder_in_grad[None],
        encoder_out_grad[None],
        self_gain_sum,
        cross_gain_sum,
        ffn_gain_sum,
        table_sum,
        grad_sq,
        grad_sk,
        grad_sv,
        grad_so,
        grad_cq,
        grad_ck,
        grad_cv,
        grad_co,
        grad_fi,
        grad_fo,
    )


def solution(mesh):
    in_specs = (
        P("dp", "mem", None),
        P("dp", "mem", None),
        P("dp", "mem"),
        P("dp", "mem"),
        P("dp", "mem"),
        P("dp", "mem"),
        P(),
        P(),
        P(),
        P(),
        P(),
        P(),
        P(),
        P(),
        P(),
        P(),
        P(),
        P(),
        P(),
        P(),
        P("dp", "mem", None),
    )
    out_specs = (
        P("dp", "mem", None),
        P("dp", "mem", None),
        P("dp", "mem", None),
        P(),
        P(),
        P(),
        P(),
        P("dp", "mem"),
        P("dp", "mem"),
        P("dp", "mem"),
        P("dp", "mem"),
        P("dp", "mem"),
        P("dp", "mem"),
        P("dp", "mem"),
        P("dp", "mem"),
        P("dp", "mem"),
        P("dp", "mem"),
    )
    return jax.shard_map(
        on_device, mesh=mesh, in_specs=in_specs, out_specs=out_specs, check_vma=False
    )
```

```python
import copy
import functools
import math

import jax
import jax.numpy as jnp
import numpy as np
from jax import lax
from jax.experimental import pallas as pl
from jax.experimental.pallas import tpu as pltpu
from jax.sharding import PartitionSpec as P

HEADS = 12
HEAD_DIM = 64
BUCKETS = 32
MAX_DIST = 128
PAIRS = HEADS // 2
LANES = 128

EPSILON = 1e-06
NEGATIVE = -(2.0**30)
LOG2E = math.log2(math.e)
LN2 = math.log(2.0)
VMEM_LIMIT = 12 * 1024 * 1024
BF16 = jnp.bfloat16
F32 = jnp.float32


def bucket_edges():
    exact_max = BUCKETS // 2
    return [
        math.ceil(exact_max * (MAX_DIST / exact_max) ** (degree / exact_max))
        for degree in range(1, exact_max)
    ]


def rel_bucket(distance):
    exact_max = BUCKETS // 2
    log_bucket = exact_max + sum(
        (distance >= edge).astype(np.int32) for edge in bucket_edges()
    )
    return np.where(distance < exact_max, distance, log_bucket)


FAR = bucket_edges()[-1]


def near_types(block):
    return (FAR - 1 + block - 1) // block + 1


def group_of(dp, mem, mem_size):
    half = mem_size // 2
    return (dp % 2) * half + mem % half


def row_moves(dp_size, mem_size):
    half = mem_size // 2
    moves = ([], [])
    for dp in range(dp_size):
        for mem in range(mem_size):
            for piece in range(2):
                chunk = 2 * mem + piece
                group = chunk if chunk < mem_size else 2 * mem_size - 1 - chunk
                to_dp = dp - dp % 2 + group // half
                to_mem = (dp % 2) * half + group % half
                moves[piece].append((dp * mem_size + mem, to_dp * mem_size + to_mem))
    return moves


def to_rows(values, axis=0):
    moves = row_moves(lax.axis_size("dp"), lax.axis_size("mem"))
    return tuple(
        lax.ppermute(piece, ("dp", "mem"), move) for piece, move in zip(jnp.split(values, 2, axis=axis), moves)
    )


def arranged(pieces, odd, axis=0):
    first, second = pieces
    return jnp.concatenate(
        [jnp.where(odd, second, first), jnp.where(odd, first, second)], axis=axis
    )


def from_rows(values, odd, axis=0):
    moves = row_moves(lax.axis_size("dp"), lax.axis_size("mem"))
    low, high = jnp.split(values, 2, axis=axis)
    first, second = jnp.where(odd, high, low), jnp.where(odd, low, high)
    back = [[(there, here) for here, there in move] for move in moves]
    first = lax.ppermute(first, ("dp", "mem"), back[0])
    second = lax.ppermute(second, ("dp", "mem"), back[1])
    return jnp.concatenate([first, second], axis=axis)


def group_shift(values, step):
    dp_size, mem_size = lax.axis_size("dp"), lax.axis_size("mem")
    half = mem_size // 2
    moves = []
    for dp in range(dp_size):
        for mem in range(mem_size):
            group = (group_of(dp, mem, mem_size) + step) % mem_size
            to_dp = dp - dp % 2 + group // half
            to_mem = mem - mem % half + group % half
            moves.append((dp * mem_size + mem, to_dp * mem_size + to_mem))
    return lax.ppermute(values, ("dp", "mem"), moves)


def others(values):
    return [group_shift(values, step) for step in range(1, lax.axis_size("mem"))]


def came_parts(parts, rows):
    came = [
        group_shift(parts[:, (step - 1) * rows : step * rows], -step) for step in range(1, lax.axis_size("mem"))
    ]
    return came[0] if len(came) == 1 else sum(part.astype(F32) for part in came)


def block_list(group, mem_size, rows):
    piece = rows // 2
    q_at, k_at, kinds, is_low = [], [], [], []
    for i in range(2 * mem_size + 1):
        low = i <= group
        chunk = jnp.where(low, i, i - (group + 1))
        owner = jnp.where(chunk < mem_size, chunk, 2 * mem_size - 1 - chunk)
        slot = (group - owner) % mem_size
        q_at.append(jnp.where(low, 0, piece))
        k_at.append(slot * rows + jnp.where(chunk < mem_size, 0, piece))
        kinds.append(jnp.where(low, group - i, 2 * mem_size - i))
        is_low.append(low.astype(jnp.int32))
    return jnp.stack([jnp.stack(v).astype(jnp.int32) for v in (q_at, k_at, kinds, is_low)])


def bias_of(distance, rel_bias):
    hot = (rel_bucket(np.maximum(distance, 0))[..., None] == np.arange(BUCKETS)).astype(np.float32)
    values = jnp.einsum(
        "...b,bh->h...", jnp.asarray(hot), rel_bias - rel_bias[BUCKETS - 1], precision=lax.Precision.HIGHEST
    )
    return jnp.where(jnp.asarray(distance >= 0), values * LOG2E, NEGATIVE)


def spread(row, rows):
    width = row.shape[1]
    table = jnp.broadcast_to(row, (8, width))
    place = lax.broadcasted_iota(jnp.int32, (8, width), 0)
    for bit in range(3):
        moved = pltpu.roll(table, 1 << bit, 1)
        table = jnp.where((place >> bit) & 1 == 1, moved, table)
    size = 8
    while size < rows:
        table = jnp.concatenate([table, pltpu.roll(table, size, 1)], axis=0)
        size *= 2
    return table


def small_block(block):
    return min(LANES, block)


def table_kernel(base_ref, base_t_ref, table_ref, table_t_ref):
    heads, kinds, block = table_ref.shape[0], table_ref.shape[1] - 2, table_ref.shape[2]
    for head in range(heads):
        for base, table in ((base_ref, table_ref), (base_t_ref, table_t_ref)):
            table[head, 0] = jnp.full((block, block), NEGATIVE, F32)
            table[head, kinds + 1] = jnp.zeros((block, block), F32)
            for kind in range(kinds):
                table[head, kind + 1] = spread(base[head, kind], block)[:, block:]


def bias_tables(rel_bias, block):
    kinds = near_types(block)
    at = np.arange(2 * block)[None, :] - block
    start = np.arange(kinds)[:, None] * block
    base, base_t = bias_of(start - at, rel_bias), bias_of(start + at, rel_bias)
    if block % LANES:
        step = np.arange(block)[None, :] - np.arange(block)[:, None] + block
        masked = jnp.full((HEADS, 1, block, block), NEGATIVE, F32)
        return [jnp.concatenate([masked, v[:, :, step], jnp.zeros_like(masked)], axis=1) for v in (base, base_t)]
    heads = HEADS // 3
    spec = pl.BlockSpec((heads, kinds, 1, 2 * block), lambda h: (h, 0, 0, 0))
    out = pl.BlockSpec((heads, kinds + 2, block, block), lambda h: (h, 0, 0, 0))
    shape = jax.ShapeDtypeStruct((HEADS, kinds + 2, block, block), F32)
    return pl.pallas_call(
        table_kernel,
        grid=(HEADS // heads,),
        in_specs=[spec, spec],
        out_specs=[out, out],
        out_shape=[pltpu.HBM(shape.shape, shape.dtype)] * 2,
        compiler_params=pltpu.CompilerParams(vmem_limit_bytes=VMEM_LIMIT),
        name="bias_tables",
    )(base[:, :, None, :], base_t[:, :, None, :])


def small_parts(block, small):
    return [(r, c, (r - c) // small) for r in range(0, block, small) for c in range(0, block, small)]


def kind_index(step, kind, block, small, kinds):
    return jnp.clip(kind * (block // small) + step + 1, 0, kinds + 1)


def with_bias(s, table_ref, head, kind, turned=False):
    block, small, kinds = s.shape[0], table_ref.shape[2], table_ref.shape[1] - 2
    fixed = isinstance(kind, int)
    if fixed and (kind - 1) * block >= FAR - 1:
        return s
    pieces = {}
    for r, c, step in small_parts(block, small):
        at = (c, r) if turned else (r, c)
        part = s[at[0] : at[0] + small, at[1] : at[1] + small]
        if fixed:
            step = kind * (block // small) + step
            if step < kinds:
                part = part + table_ref[head, step + 1] if step >= 0 else jnp.full(part.shape, NEGATIVE, F32)
        else:
            part = part + table_ref[head, kind_index(step, kind, block, small, kinds)]
        pieces[at] = part
    starts = range(0, block, small)
    return jnp.concatenate([jnp.concatenate([pieces[a, b] for b in starts], axis=1) for a in starts], axis=0)


def add_grad(ds, grad_ref, head, kind):
    block, small, kinds = ds.shape[0], grad_ref.shape[2], grad_ref.shape[1] - 2
    fixed = isinstance(kind, int)
    for r, c, step in small_parts(block, small):
        part = ds[c : c + small, r : r + small]
        if fixed:
            step = kind * (block // small) + step
            if not 0 <= step < kinds:
                continue
            at = step + 1
        else:
            at = kind_index(step, kind, block, small, kinds)
        grad_ref[head, at] = grad_ref[head, at] + part


def fold(table):
    rows, width = table.shape
    while rows > 1:
        rows //= 2
        table = table[:rows] + pltpu.roll(table[rows:], width - rows, 1)
    return table


def fold_kernel(first_ref, rest_ref, cross_ref, ffn_ref, sums_ref):
    kinds = first_ref.shape[1] - 2
    sums_ref[...] = jnp.zeros_like(sums_ref)
    sums_ref[1:2, :], sums_ref[2:3, :] = cross_ref[...], ffn_ref[...]
    for part, ref in enumerate((first_ref, rest_ref)):
        heads = ref.shape[0]
        for head in range(heads):
            for kind in range(kinds):
                table = ref[head, kind + 1]
                width = 2 * table.shape[1]
                wide = jnp.concatenate([table, jnp.zeros_like(table)], axis=1)
                row = FIRST_HEAD_ROW + part * heads + head
                sums_ref[row : row + 1, kind * width : (kind + 1) * width] = fold(wide)


def table_sums(first, rest, cross_grad, ffn_grad):
    kinds, block = first.shape[1] - 2, first.shape[2]
    shape = (SMALL_ROWS, cross_grad.shape[1])
    if block % LANES:
        grad_t = jnp.pad(jnp.concatenate([first, rest])[:, 1 : kinds + 1], ((0, 0), (0, 0), (0, 0), (0, block)))
        place = (np.arange(block)[:, None] + np.arange(2 * block)[None, :]) % (2 * block)
        sums = jnp.sum(grad_t[:, :, np.arange(block)[:, None], place], axis=2).reshape(HEADS, -1)
        small = jnp.zeros(shape, F32).at[1].set(cross_grad[0]).at[2].set(ffn_grad[0])
        return small.at[FIRST_HEAD_ROW : FIRST_HEAD_ROW + HEADS, : sums.shape[1]].set(sums)
    return run(
        fold_kernel,
        "table_sums",
        (1,),
        [(first, None, pltpu.HBM), (rest, None, pltpu.HBM), (cross_grad, None), (ffn_grad, None)],
        [(shape, F32, None)],
    )[0]


def bucket_hot(block):
    kinds = near_types(block)
    at = np.arange(2 * block)[None, :]
    at = np.where(at < block, at, at - 2 * block) + np.arange(kinds)[:, None] * block
    near = (at >= 0) & (at < FAR)
    hot = (rel_bucket(np.maximum(at, 0))[..., None] == np.arange(BUCKETS)) & near[..., None]
    return hot.reshape(-1, BUCKETS).T.astype(np.float32)


def write_kernel(chunks, *refs):
    counts, chunks = chunks
    totals, at = [], 0
    for count in counts:
        parts = [ref[...].astype(F32) for ref in refs[at : at + count]]
        totals.append(sum(parts[1:], parts[0]))
        at += count
    first, second, rest, own = totals
    ffn = jnp.concatenate([first, second], axis=0)
    small, hot = refs[at][...], refs[at + 1][...]
    refs = refs[at + 2 :]
    gains, table_ref, fo_ref, fi_ref, squares = refs[:3], refs[3], refs[4], refs[5], refs[6:]
    for i in range(3):
        gains[i][...] = small[i : i + 1, :]
    sums = small[FIRST_HEAD_ROW : FIRST_HEAD_ROW + HEADS, : hot.shape[1]]
    near = lax.dot_general(
        hot, sums, (((1,), (1,)), ((), ())), precision=lax.Precision.HIGHEST, preferred_element_type=F32
    )
    last = -jnp.sum(near, axis=0, keepdims=True)
    bucket = lax.broadcasted_iota(jnp.int32, near.shape, 0)
    table_ref[...] = jnp.where(bucket == BUCKETS - 1, last, near)
    rows, cols = fo_ref.shape
    fo_ref[...] = ffn[:rows]
    each = fi_ref.shape[0]
    for i in range(chunks):
        fi_ref[:, i * cols : (i + 1) * cols] = ffn[rows + i * each : rows + (i + 1) * each]
    at = 0
    for total in (rest, own):
        for i in range(total.shape[0] // each):
            squares[at][...] = total[i * each : (i + 1) * each]
            at += 1


def write_grads(ffn, rest, own, small, block, width, hidden):
    dp_size, mem_size = lax.axis_size("dp"), lax.axis_size("mem")
    hot = jnp.asarray(bucket_hot(block))
    square = ((width // dp_size, width // mem_size), F32, None)
    return run(
        functools.partial(write_kernel, ([1 + len(s.came) for s in (*ffn, rest, own)], hidden // width)),
        "write_grads",
        (1,),
        [(v.reshape(v.shape[-2:]), None) for s in (*ffn, rest, own) for v in (s.keep, *s.came)]
        + [(v, None) for v in (small, hot)],
        [((1, width), F32, None)] * 3
        + [
            ((BUCKETS, HEADS), F32, None),
            ((hidden // dp_size, width // mem_size), F32, None),
            ((width // dp_size, hidden // mem_size), F32, None),
        ]
        + [square] * 8,
    )


def nt(a, b):
    return lax.dot_general(a, b, (((1,), (1,)), ((), ())), preferred_element_type=F32)


def nn(a, b):
    return jnp.dot(a, b, preferred_element_type=F32)


def half_of(values, head):
    lane = lax.broadcasted_iota(jnp.int32, values.shape, 1)
    return jnp.where((lane >= HEAD_DIM) == (head == 1), values, jnp.zeros_like(values))


def join_halves(first, second):
    lane = lax.broadcasted_iota(jnp.int32, first.shape, 1)
    return jnp.where(lane < HEAD_DIM, first, second)


def in_three(values):
    high = values.astype(BF16)
    rest = values - high.astype(F32)
    mid = rest.astype(BF16)
    low = (rest - mid.astype(F32)).astype(BF16)
    return high, mid, low


def put_lanes(base, start, values):
    lane = lax.broadcasted_iota(jnp.int32, base.shape, 1)
    for i, value in enumerate(values):
        base = jnp.where(lane == start + i, value, base)
    return base


def with_log_sum(mask_lanes, log_sum):
    pieces = [piece.astype(F32) for piece in in_three(-log_sum)]
    return put_lanes(mask_lanes.astype(F32), 3, pieces).astype(BF16)


def bit_count(axis):
    return lax.axis_size(axis).bit_length() - 1


def swap(values, axis, bit):
    size = lax.axis_size(axis)
    return lax.ppermute(values, axis, [(i, i ^ (1 << bit)) for i in range(size)])


def swap_many(values, names):
    dp_size, mem_size = lax.axis_size("dp"), lax.axis_size("mem")
    flips = {axis: sum(1 << bit for name, bit in names if name == axis) for axis in ("dp", "mem")}
    moves = [
        (dp * mem_size + mem, (dp ^ flips["dp"]) * mem_size + (mem ^ flips["mem"]))
        for dp in range(dp_size)
        for mem in range(mem_size)
    ]
    return lax.ppermute(values, ("dp", "mem"), moves)


def bit_order(order):
    dp_bits, mem_bits = bit_count("dp"), bit_count("mem")
    z_bits = [("dp", b) for b in range(2, dp_bits)]
    groups = {
        "x": [("mem", b) for b in range(mem_bits)],
        "y": [("dp", b) for b in range(1, min(2, dp_bits))],
        "Z": z_bits[:1],
        "z": z_bits[1:] if "Z" in order else z_bits,
    }
    return [step for name in order for step in groups[name]]


def in_pairs(names):
    return [tuple(names[i : i + 2]) for i in range(0, len(names), 2)]


SMALL_ROWS = 16
FIRST_HEAD_ROW = 4


TILE = 256
LIMITS = {
    "own_project": 12,
    "other_project": 12,
    "encoder_project": 12,
    "self_forward": 18,
    "cross_forward": 18,
    "feed_forward": 34,
    "cross_backward": 18,
    "cross_finish": 30,
    "encoder_finish": 18,
    "self_backward": 18,
    "table_sums": 12,
    "query_grad": 12,
    "key_grads": 18,
    "self_finish_back": 18,
    "advance": 24,
    "write_grads": 16,
}


def tn(a, b):
    return lax.dot_general(a, b, (((0,), (0,)), ((), ())), preferred_element_type=F32)


def normed(hidden, gain):
    return hidden * lax.rsqrt(jnp.mean(hidden * hidden, axis=-1, keepdims=True) + EPSILON) * gain


def norm_back(hidden, gain, grad):
    scale = lax.rsqrt(jnp.mean(hidden * hidden, axis=-1, keepdims=True) + EPSILON)
    unit = hidden * scale
    inner = grad * gain
    out = scale * (inner - unit * jnp.mean(inner * unit, axis=-1, keepdims=True))
    return out, jnp.sum(grad * unit, axis=0, keepdims=True)


def whole(array):
    zeros = (0,) * array.ndim
    return pl.BlockSpec(array.shape, lambda *_: zeros)


def run(kernel, name, grid, ins, outs, scratch=(), scalars=(), after=(), flops=0, aliases=None):
    count = len(scalars) + len(ins)
    in_places = [v[2] if len(v) > 2 else None if v[1] is None or v[1] is ANY else pltpu.HBM for v in ins]
    out_places = [v[3] if len(v) > 3 else None if v[2] is None else pltpu.HBM for v in outs]
    ins, outs = [v[:2] for v in ins], [v[:3] for v in outs]

    def body(*refs):
        kernel(*refs[:count], *refs[count + len(after) :])

    out_shape = [jax.ShapeDtypeStruct(shape, dtype) for shape, dtype, _ in outs]
    placed = [o if p is None else p(o.shape, o.dtype) for o, p in zip(out_shape, out_places)]
    arrays = [a if p is None else pltpu.with_memory_space_constraint(a, p) for (a, _), p in zip(ins, in_places)]
    moved = sum(a.size * a.dtype.itemsize for a, _ in ins) + sum(
        math.prod(s) * jnp.dtype(d).itemsize for s, d, _ in outs
    )
    return pl.pallas_call(
        body,
        grid_spec=pltpu.PrefetchScalarGridSpec(
            num_scalar_prefetch=len(scalars),
            grid=grid,
            in_specs=[whole(a) if s is None else s for a, s in ins]
            + [pl.BlockSpec(memory_space=pl.ANY) for _ in after],
            out_specs=[whole(o) if s is None else s for o, (_, _, s) in zip(out_shape, outs)],
            scratch_shapes=list(scratch),
        ),
        out_shape=placed,
        input_output_aliases=aliases or {},
        compiler_params=pltpu.CompilerParams(vmem_limit_bytes=LIMITS[name] << 20),
        cost_estimate=pl.CostEstimate(flops=flops // 16, bytes_accessed=moved // 16, transcendentals=0),
        name=name,
    )(*scalars, *arrays, *after)


ANY = pl.BlockSpec(memory_space=pl.ANY)


def row_spec(tile, width, shift=0):
    return pl.BlockSpec((tile, width), lambda i, *_: (i + shift, 0))


def fits(rows, cols):
    dp_size, mem_size = lax.axis_size("dp"), lax.axis_size("mem")
    return (rows // dp_size) % 16 == 0 and (cols // mem_size) % LANES == 0


def emit(mine, total_ref, keep_ref, send_ref, at, rows):
    mem_size, pairs, _, cols = keep_ref.shape
    chunks = total_ref.shape[1] // cols // mem_size
    for pair in range(pairs):
        keep_at = pl.multiple_of((2 * pair + mine) * rows, 16)
        send_at = pl.multiple_of((2 * pair + 1 - mine) * rows, 16)
        for mem in range(mem_size):
            for chunk in range(chunks):
                lanes = slice((mem * chunks + chunk) * cols, (mem * chunks + chunk + 1) * cols)
                place = slice(at + chunk * rows, at + (chunk + 1) * rows)
                keep_ref[mem, pair, place, :] = total_ref[pl.ds(keep_at, rows), lanes].astype(BF16)
                send_ref[mem, pair, place, :] = total_ref[pl.ds(send_at, rows), lanes].astype(BF16)


def square_outs(count, width):
    dp_size, mem_size = lax.axis_size("dp"), lax.axis_size("mem")
    if fits(width, width):
        shape = (mem_size, dp_size // 2, count * width // dp_size, width // mem_size)
        return [(shape, BF16, None)] * 2
    return [((width, width), BF16, None)] * count


def write_square(mine, index, total, total_ref, out_refs):
    if len(out_refs[0].shape) == 4:
        keep_ref, send_ref = out_refs
        rows = total.shape[0] // (2 * keep_ref.shape[1])
        total_ref[...] = total
        emit(mine, total_ref, keep_ref, send_ref, index * rows, rows)
    else:
        out_refs[index][...] = total.astype(BF16)


def in_order(grads, chunks=1):
    if grads[0].ndim == 4:
        return grads
    dp_size, mem_size = lax.axis_size("dp"), lax.axis_size("mem")
    cuts = []
    for grad in grads:
        rows, cols = grad.shape[0] // dp_size, grad.shape[1] // mem_size // chunks
        cut = grad.reshape(dp_size // 2, 2, rows, mem_size, chunks, cols).transpose(1, 3, 0, 4, 2, 5)
        cuts.append(cut.reshape(2, mem_size, dp_size // 2, chunks * rows, cols))
    cut = jnp.concatenate(cuts, axis=3)
    mine = lax.axis_index("dp") & 1
    return [lax.dynamic_index_in_dim(cut, which, 0, keepdims=False) for which in (mine, 1 - mine)]


class Scatter:
    def __init__(self, grads, order, chunks=1):
        keep, send = in_order(grads, chunks)
        mem_bits, dp_bits = bit_count("mem"), bit_count("dp")
        self.names = [("mem", b) for b in reversed(range(mem_bits))]
        self.names += [("dp", b) for b in reversed(range(1, dp_bits))]
        self.order = []
        for part in order.split("]"):
            single, _, paired = part.partition("[")
            self.order += [(name,) for name in bit_order(single)] + in_pairs(bit_order(paired))
        shape = (2,) * len(self.names) + keep.shape[2:]
        self.keep, self.came = keep.reshape(shape), [swap(send, "dp", 0).reshape(shape)]
        self.span = (0, shape[-2])

    def part(self, start, size, order):
        share = copy.copy(self)
        share.names, share.span = list(self.names), (self.span[0] + start, size)
        share.order = [(name,) for name in bit_order(order)]
        return share


def all_bits():
    return [("mem", b) for b in range(bit_count("mem"))] + [("dp", b) for b in range(bit_count("dp"))]


def bit_values():
    return jnp.stack([((lax.axis_index(axis) >> bit) & 1).astype(jnp.int32) for axis, bit in all_bits()])


def level(*group, bits):
    while any(v.order != group[0].order for v in group):
        longest = max(sum(map(len, v.order)) for v in group)
        advance(bits, *[v for v in group if sum(map(len, v.order)) == longest])


def advance_kernel(moves, bits, *refs):
    outs = refs[sum(parts for _, sources in moves for _, _, parts in sources) :]
    ref_at = out_at = 0
    for names, sources in moves:
        flips = [(0,), (1,)] if len(names) == 1 else [(0, 0), (0, 1), (1, 0), (1, 1)]
        start = 0
        for from_row, size, parts in sources:
            ins = refs[ref_at : ref_at + parts]
            ref_at += parts
            for pre in range(ins[0].shape[0]):
                for mid in range(ins[0].shape[2]):
                    for post in range(ins[0].shape[4]):
                        for out, flip in zip(outs[out_at : out_at + len(flips)], flips):
                            place = [bits[name] if f == 0 else 1 - bits[name] for name, f in zip(names, flip)]
                            place = place + [0] if len(place) == 1 else place
                            rows = slice(from_row, from_row + size)
                            values = [ref[pre, place[0], mid, place[1], post, rows, :].astype(F32) for ref in ins]
                            out[pre, mid, post, start : start + size, :] = sum(values[1:], values[0]).astype(BF16)
            start += size
        out_at += len(flips)


def advance(bits, *groups):
    groups = [group if isinstance(group, tuple) else (group,) for group in groups]
    for group in groups:
        lead = group[0]
        assert all(v.names == lead.names and v.order == lead.order for v in group)
        if not lead.order and len(group) > 1:
            sums = [sum(v.came, v.keep.astype(F32))[..., v.span[0] : sum(v.span), :] for v in group]
            lead.keep = jnp.concatenate(sums, axis=-2)
            lead.came, lead.span = [jnp.zeros_like(lead.keep)], (0, lead.keep.shape[-2])
    groups = [group for group in groups if group[0].order]
    if not groups:
        return
    moves, arrays, heads = [], [], []
    for group in groups:
        lead = group[0]
        names = lead.order.pop(0)
        places = [lead.names.index(name) for name in names]
        if places != sorted(places):
            names, places = names[::-1], places[::-1]
        pre = 2 ** places[0]
        mid = 2 ** (places[1] - places[0] - 1) if len(names) == 2 else 1
        post = 2 ** (len(lead.names) - len(names)) // pre // mid
        second = len(names)
        lead.names = [name for name in lead.names if name not in names]
        rows, cols = [v.span for v in group], lead.keep.shape[-1]
        moves.append(([all_bits().index(name) for name in names], [(*r, 1 + len(v.came)) for r, v in zip(rows, group)]))
        arrays.append(
            [v.reshape(pre, 2, mid, second, post, v.shape[-2], cols) for s in group for v in (s.keep, *s.came)]
        )
        heads.append((names, pre, mid, post, sum(size for _, size in rows), cols))
    total = sum(v.size * 2 for group in arrays for v in group)
    steps = 1
    if total > 8 << 20:
        steps = next(n for n in (4, 2, 1) if all(pre % n == 0 or post % n == 0 for _, pre, _, post, _, _ in heads))
    ins, outs = [], []
    for group, (names, pre, mid, post, rows, cols) in zip(arrays, heads):
        by_pre = pre % steps == 0
        own_pre, own_post = (pre // steps, post) if by_pre else (pre, post // steps)
        for array in group:
            block = (own_pre, 2, mid, array.shape[3], own_post) + array.shape[5:]
            place = (lambda i, *_: (i, 0, 0, 0, 0, 0, 0)) if by_pre else (lambda i, *_: (0, 0, 0, 0, i, 0, 0))
            ins.append((array, None if steps == 1 else pl.BlockSpec(block, place)))
        place = (lambda i, *_: (i, 0, 0, 0, 0)) if by_pre else (lambda i, *_: (0, 0, i, 0, 0))
        spec = None if steps == 1 else pl.BlockSpec((own_pre, mid, own_post, rows, cols), place)
        outs += [((pre, mid, post, rows, cols), BF16, spec)] * 2 ** len(names)
    results = run(
        functools.partial(advance_kernel, moves), "advance", (steps,), ins, outs, scalars=(bits,), flops=total
    )
    for group, (names, pre, mid, post, rows, cols) in zip(groups, heads):
        lead = group[0]
        lead.span = (0, rows)
        lead.keep, *sends = [v.reshape((2,) * len(lead.names) + (rows, cols)) for v in results[: 2 ** len(names)]]
        results = results[2 ** len(names) :]
        partners = [names] if len(names) == 1 else [names[1:], names[:1], names]
        lead.came = [swap_many(send, partner) for send, partner in zip(sends, partners)]


def fence(scatters, *values):
    states = [(v.keep, v.came) for v in scatters]
    states, values = lax.optimization_barrier((states, values))
    for scatter, (keep, came) in zip(scatters, states):
        scatter.keep, scatter.came = keep, came
    return values


def head_norms(rows):
    wide = rows.astype(F32)
    shape = (rows.shape[1], LANES)
    head = lax.broadcasted_iota(jnp.int32, shape, 0) // HEAD_DIM == lax.broadcasted_iota(jnp.int32, shape, 1)
    return jnp.max(nn((wide * wide).astype(BF16), head.astype(F32).astype(BF16)), axis=0, keepdims=True)


def put_norms(norm_ref, rows):
    norms = head_norms(rows)

    @pl.when(pl.program_id(0) == 0)
    def _():
        norm_ref[...] = norms

    @pl.when(pl.program_id(0) > 0)
    def _():
        norm_ref[...] = jnp.maximum(norm_ref[...], norms)


def tag_lanes(tags, first):
    lane = lax.broadcasted_iota(jnp.int32, tags.shape, 1)
    tags = tags.astype(F32)
    kept = (tags[:, first : first + 1] == lane.astype(F32)) & (tags[:, first + 1 : first + 2] > 0)
    lanes = jnp.where(lane < 3, jnp.where(kept, 0.0, NEGATIVE), 0.0)
    return jnp.where((lane >= 3) & (lane < 6), 1.0, lanes).astype(BF16)


def own_project_kernel(
    x_ref,
    gain_ref,
    wq_ref,
    wk_ref,
    wv_ref,
    a_ref,
    q_ref,
    k_ref,
    v_ref,
    dec_ref,
    enc_ref,
    q_lanes_ref,
    q_norm_ref,
    k_norm_ref,
):
    width = gain_ref.shape[1]
    a = normed(x_ref[:, :width].astype(F32), gain_ref[...]).astype(BF16)
    a_ref[...] = a
    q = (nn(a, wq_ref[...]) * LOG2E).astype(BF16)
    k = nn(a, wk_ref[...]).astype(BF16)
    q_ref[...], k_ref[...] = q, k
    v_ref[...] = nn(a, wv_ref[...]).astype(BF16)
    put_norms(q_norm_ref, q), put_norms(k_norm_ref, k)
    tags = x_ref[:, width:]
    dec_ref[...], enc_ref[...] = tag_lanes(tags, 0), tag_lanes(tags, 2)
    lane = lax.broadcasted_iota(jnp.int32, tags.shape, 1)
    q_lanes_ref[...] = ((tags[:, 0:1].astype(F32) == lane.astype(F32)) & (lane < 3)).astype(F32).astype(BF16)


def other_project_kernel(
    x_ref,
    gain_ref,
    wk_ref,
    wv_ref,
    k_old,
    v_old,
    dec_old,
    enc_old,
    k_ref,
    v_ref,
    dec_ref,
    enc_ref,
    k_norm_ref,
):
    width = gain_ref.shape[1]
    a = normed(x_ref[:, :width].astype(F32), gain_ref[...]).astype(BF16)
    k = nn(a, wk_ref[...]).astype(BF16)
    k_ref[...] = k
    v_ref[...] = nn(a, wv_ref[...]).astype(BF16)
    put_norms(k_norm_ref, k)
    tags = x_ref[:, width:]
    dec_ref[...], enc_ref[...] = tag_lanes(tags, 0), tag_lanes(tags, 2)


def encoder_project_kernel(x_ref, wk_ref, wv_ref, *refs):
    k_ref, v_ref, k_norm_ref = refs[-3:]
    k = nn(x_ref[...], wk_ref[...]).astype(BF16)
    k_ref[...] = k
    put_norms(k_norm_ref, k)
    v_ref[...] = nn(x_ref[...], wv_ref[...]).astype(BF16)


def own_project(x, gain, wq, wk, wv, keys):
    rows, width = x.shape[0], gain.shape[1]
    tile = min(TILE, rows)
    spec, lanes = row_spec(tile, width), row_spec(tile, LANES)
    return run(
        own_project_kernel,
        "own_project",
        (rows // tile,),
        [(x, row_spec(tile, x.shape[1]), None), (gain, None), (wq, None), (wk, None), (wv, None)],
        [((n, width), BF16, spec) for n in (rows, rows, keys, keys)]
        + [((n, LANES), BF16, lanes) for n in (keys, keys, rows)]
        + [((1, LANES), F32, None)] * 2,
        flops=6 * rows * width * width,
    )


def other_project(x, gain, wk, wv, *so_far):
    rows, width = x.shape[0], gain.shape[1]
    tile = min(TILE, rows)
    shift = (so_far[0].shape[0] - rows) // tile
    spec, lanes = row_spec(tile, width, shift), row_spec(tile, LANES, shift)
    return run(
        other_project_kernel,
        "other_project",
        (rows // tile,),
        [(x, row_spec(tile, x.shape[1]), None), (gain, None), (wk, None), (wv, None)] + [(v, ANY) for v in so_far],
        [(v.shape, BF16, s) for v, s in zip(so_far, (spec, spec, lanes, lanes))] + [((1, LANES), F32, None)],
        aliases={4: 0, 5: 1, 6: 2, 7: 3},
        flops=4 * rows * width * width,
    )


def encoder_project(x, wk, wv, keys, so_far=()):
    rows, width = x.shape
    tile = min(TILE, rows)
    spec = row_spec(tile, width, (keys - rows) // tile if so_far else 0)
    return run(
        encoder_project_kernel,
        "encoder_project",
        (rows // tile,),
        [(x, row_spec(tile, width), None), (wk, None), (wv, None)] + [(v, ANY) for v in so_far],
        [((keys, width), BF16, spec)] * 2 + [((1, LANES), F32, None)],
        aliases={3: 0, 4: 1} if so_far else None,
        flops=4 * rows * width * width,
    )


def self_finish(mixed_ref, hidden_ref, w_out_ref, gain_ref, w_next_ref, hidden_out, norm_out, next_out, next_norm):
    rows = hidden_ref.shape[0]
    tile = min(TILE, rows)
    for at in range(0, rows, tile):
        o = jnp.concatenate([mixed_ref[p, at : at + tile, :] for p in range(PAIRS)], axis=1)
        hidden = hidden_ref[at : at + tile, :].astype(F32) + nn(o, w_out_ref[...])
        hidden_out[at : at + tile, :] = hidden
        b = normed(hidden, gain_ref[...]).astype(BF16)
        norm_out[at : at + tile, :] = b
        if w_next_ref is not None:
            following = (nn(b, w_next_ref[...]) * LOG2E).astype(BF16)
            next_out[at : at + tile, :] = following
            norms = head_norms(following)
            next_norm[...] = norms if at == 0 else jnp.maximum(next_norm[...], norms)


def ffn_kernel(mine_ref, c_ref, og_ref, wi_ref, wo_ref, h2_ref, gain_ref, wco_ref, *refs):
    layer_ref, dh2_ref, dyc_ref, doc_ref, dgain_ref, *grad_refs, y_sum, dc_sum, total_ref, turned_ref = refs
    step, steps = pl.program_id(0), pl.num_programs(0)
    mine = mine_ref[0]
    c, og, wi, wo = c_ref[...], og_ref[...], wi_ref[...], wo_ref[...]

    @pl.when(step == 0)
    def _():
        turned_ref[...] = c.T

    u = nn(c, wi)
    slope = math.sqrt(2.0 / math.pi)
    square = u * u
    bend = jnp.tanh(u * (slope + (slope * 0.044715) * square))
    half = 0.5 + 0.5 * bend
    wide = u * half
    g = wide.astype(BF16)
    rate = half + wide * ((1.0 - bend) * (slope + (slope * 3.0 * 0.044715) * square))
    y = nn(g, wo)
    du = (nt(og, wo) * rate).astype(BF16)
    dc = nt(du, wi)

    @pl.when(step == 0)
    def _():
        y_sum[...] = y
        dc_sum[...] = dc

    @pl.when(step > 0)
    def _():
        y_sum[...] += y
        dc_sum[...] += dc

    out_total, in_total = tn(g, og), nn(turned_ref[...], du)
    if len(grad_refs) == 4:
        total_ref[...] = out_total
        emit(mine, total_ref, grad_refs[0], grad_refs[1], 0, grad_refs[0].shape[2])
        total_ref[...] = in_total
        rows = grad_refs[2].shape[2] * grad_refs[2].shape[3] // total_ref.shape[1]
        emit(mine, total_ref, grad_refs[2], grad_refs[3], 0, rows)
    else:
        grad_refs[0][...] = out_total.astype(BF16)
        grad_refs[1][...] = in_total.astype(BF16)

    @pl.when(step == steps - 1)
    def _():
        rows = h2_ref.shape[0]
        tile = min(TILE, rows)
        dgain = jnp.zeros(dgain_ref.shape, F32)
        for at in range(0, rows, tile):
            part = slice(at, at + tile)
            hidden = h2_ref[part, :]
            layer_ref[part, :] = (hidden + y_sum[part, :]).astype(BF16)
            back, gain_part = norm_back(hidden, gain_ref[...], dc_sum[part, :])
            dgain = dgain + gain_part
            dh2 = og_ref[part, :].astype(F32) + back
            dh2_ref[part, :] = dh2
            dyc = dh2.astype(BF16)
            dyc_ref[part, :] = dyc
            doc_ref[part, :] = nt(dyc, wco_ref[...]).astype(BF16)
        dgain_ref[...] = dgain


def feed_forward(mine, c, og, wi, wo, h2, gain, wco, after=()):
    rows, width = c.shape
    hidden = wi.shape[1]
    dp_size, mem_size = lax.axis_size("dp"), lax.axis_size("mem")
    chunk = width
    steps = hidden // chunk
    direct = fits(width, width) and steps == 2 * mem_size and (chunk * dp_size) % (2 * hidden) == 0
    if direct:
        pairs, rows_o, cols_o = dp_size // 2, hidden // dp_size, width // mem_size
        chunk_rows = width // dp_size * (chunk // cols_o)
        grads = [
            (
                (mem_size, pairs, rows_o, cols_o),
                BF16,
                pl.BlockSpec((mem_size, pairs // steps, rows_o, cols_o), lambda f, *_: (0, f, 0, 0)),
            )
        ] * 2 + [
            (
                (mem_size, pairs, rows_o, cols_o),
                BF16,
                pl.BlockSpec((1, pairs, chunk_rows, cols_o), lambda f, *_: (f // 2, 0, f % 2, 0)),
            )
        ] * 2
    else:
        grads = [
            ((hidden, width), BF16, pl.BlockSpec((chunk, width), lambda f, *_: (f, 0))),
            ((width, hidden), BF16, pl.BlockSpec((width, chunk), lambda f, *_: (0, f))),
        ]
    outs = run(
        ffn_kernel,
        "feed_forward",
        (steps,),
        [
            (c, None),
            (og, None),
            (wi, pl.BlockSpec((width, chunk), lambda f, *_: (0, f))),
            (wo, pl.BlockSpec((chunk, width), lambda f, *_: (f, 0))),
            (h2, None),
            (gain, None),
            (wco, None),
        ],
        [
            (c.shape, BF16, None),
            (c.shape, F32, None),
            (c.shape, BF16, None),
            (c.shape, BF16, None),
            (gain.shape, F32, None),
        ]
        + grads,
        scratch=[
            pltpu.VMEM(c.shape, F32),
            pltpu.VMEM(c.shape, F32),
            pltpu.VMEM((chunk, width), F32),
            pltpu.VMEM((width, rows), BF16),
        ],
        scalars=(mine,),
        after=after,
        flops=12 * rows * width * hidden,
    )
    grads = outs[5:]
    return outs[:5], [grads[0:2], grads[2:4]] if direct else [grads[0:1], grads[1:2]]


def cross_finish_kernel(
    mine_ref, dq0_ref, dq1_ref, wq_ref, h1_ref, gain_ref, dh2_ref, o_ref, oc_ref, dyc_ref, b_ref, wso_ref, *refs
):
    dh1_ref, do_ref, dgain_ref, *grad_refs, dy_ref, total_ref = refs
    mine = mine_ref[0]
    dq = jnp.concatenate([dq0_ref[...], dq1_ref[...]], axis=1)
    rows = h1_ref.shape[0]
    tile = min(TILE, rows)
    write_square(mine, 0, tn(oc_ref[...], dyc_ref[...]), total_ref, grad_refs)
    write_square(mine, 1, tn(b_ref[...], dq), total_ref, grad_refs)
    dgain = jnp.zeros(dgain_ref.shape, F32)
    for at in range(0, rows, tile):
        part = slice(at, at + tile)
        db = nt(dq[part, :], wq_ref[...])
        back, gain_part = norm_back(h1_ref[part, :], gain_ref[...], db)
        dgain = dgain + gain_part
        dh1 = dh2_ref[part, :] + back
        dh1_ref[part, :] = dh1
        dy = dh1.astype(BF16)
        dy_ref[part, :] = dy
        do_ref[part, :] = nt(dy, wso_ref[...]).astype(BF16)
    dgain_ref[...] = dgain
    write_square(mine, 2, tn(o_ref[...], dy_ref[...]), total_ref, grad_refs)


def cross_finish(mine, dq, wq, h1, gain, dh2, o, oc, dyc, b, wso, after=()):
    rows, width = h1.shape
    outs = run(
        cross_finish_kernel,
        "cross_finish",
        (1,),
        [(v, None) for v in (*dq, wq, h1, gain, dh2, o, oc, dyc, b, wso)],
        [(h1.shape, F32, None, pltpu.HBM), (h1.shape, BF16, None), (gain.shape, F32, None)] + square_outs(3, width),
        scratch=[pltpu.VMEM(h1.shape, BF16), pltpu.VMEM((width, width), F32)],
        scalars=(mine,),
        after=after,
        flops=10 * rows * width * width,
    )
    return outs[:3], outs[3:]


def summed(own_refs, came_refs, index):
    return jnp.concatenate(
        [
            (own[index].astype(F32) + came[index].astype(F32)).astype(BF16)
            for own, came in zip(own_refs, came_refs)
        ],
        axis=1,
    )


def encoder_finish_kernel(mine_ref, own0_ref, own1_ref, came0_ref, came1_ref, x_ref, wk_ref, wv_ref, *refs):
    dx_ref, *grad_refs, total_ref = refs
    mine = mine_ref[0]
    dk = summed((own0_ref, own1_ref), (came0_ref, came1_ref), 0)
    dv = summed((own0_ref, own1_ref), (came0_ref, came1_ref), 1)
    x = x_ref[...]
    dx_ref[...] = (nt(dk, wk_ref[...]) + nt(dv, wv_ref[...])).astype(BF16)
    write_square(mine, 0, tn(x, dk), total_ref, grad_refs)
    write_square(mine, 1, tn(x, dv), total_ref, grad_refs)


def encoder_finish(mine, own, came, x, wk, wv, after=()):
    rows, width = x.shape
    outs = run(
        encoder_finish_kernel,
        "encoder_finish",
        (1,),
        [(v, None) for v in (*own, *came, x, wk, wv)],
        [(x.shape, BF16, None)] + square_outs(2, width),
        scratch=[pltpu.VMEM((width, width), F32)],
        scalars=(mine,),
        after=after,
        flops=8 * rows * width * width,
    )
    return outs[0], outs[1:]


def query_grad_kernel(mine_ref, dq0_ref, dq1_ref, a_ref, *refs):
    *grad_refs, total_ref = refs
    dq = jnp.concatenate([dq0_ref[...], dq1_ref[...]], axis=1)
    write_square(mine_ref[0], 0, tn(a_ref[...], dq), total_ref, grad_refs)


def query_grad(mine, dq, a):
    rows, width = a.shape
    return run(
        query_grad_kernel,
        "query_grad",
        (1,),
        [(v, None) for v in (*dq, a)],
        square_outs(1, width),
        scratch=[pltpu.VMEM((width, width), F32)],
        scalars=(mine,),
        flops=2 * rows * width * width,
    )


def key_grads_kernel(mine_ref, own0_ref, own1_ref, came0_ref, came1_ref, a_ref, *refs):
    sums_ref, *grad_refs, total_ref = refs
    a = a_ref[...]
    for i in range(2):
        total = summed((own0_ref, own1_ref), (came0_ref, came1_ref), i)
        sums_ref[i] = total
        write_square(mine_ref[0], i, tn(a, total), total_ref, grad_refs)


def key_grads(mine, own, came, a, after=()):
    rows, width = a.shape
    outs = run(
        key_grads_kernel,
        "key_grads",
        (1,),
        [(v, None) for v in (*own, *came, a)],
        [((2, rows, width), BF16, None)] + square_outs(2, width),
        scratch=[pltpu.VMEM((width, width), F32)],
        scalars=(mine,),
        after=after,
        flops=4 * rows * width * width,
    )
    return outs[0], outs[1:]


def self_finish_back_kernel(
    dq0_ref, dq1_ref, sums_ref, x_ref, gain_ref, dh1_ref, wq_ref, wk_ref, wv_ref, small_ref, dx_ref, small_out
):
    @pl.when(pl.program_id(0) == 0)
    def _():
        small_out[...] = small_ref[...]

    dq = jnp.concatenate([dq0_ref[...], dq1_ref[...]], axis=1)
    da = nt(dq, wq_ref[...]) + nt(sums_ref[0], wk_ref[...]) + nt(sums_ref[1], wv_ref[...])
    back, gain_part = norm_back(x_ref[...].astype(F32), gain_ref[...], da)
    small_out[0:1, :] += gain_part
    dx_ref[...] = (dh1_ref[...] + back).astype(BF16)


def self_finish_back(dq, sums, x, gain, dh1, wq, wk, wv, small):
    rows, width = dh1.shape
    tile = min(TILE, rows)
    spec = row_spec(tile, width)
    return run(
        self_finish_back_kernel,
        "self_finish_back",
        (rows // tile,),
        [
            (dq[0], row_spec(tile, dq[0].shape[1])),
            (dq[1], row_spec(tile, dq[1].shape[1])),
            (sums, pl.BlockSpec((2, tile, width), lambda i, *_: (0, i, 0)), None),
            (x, spec),
            (gain, None),
            (dh1, spec),
            (wq, None),
            (wk, None),
            (wv, None),
            (small, None),
        ],
        [((rows, width), BF16, spec), (small.shape, F32, None)],
        flops=6 * rows * width * width,
    )


SCORE_BOUND = 80.0


def mark_small(small_ref, q_norm_ref, *k_norm_refs):
    @pl.when(pl.program_id(0) == 0)
    def _():
        k_norm = k_norm_refs[0][...]
        for ref in k_norm_refs[1:]:
            k_norm = jnp.maximum(k_norm, ref[...])
        largest = jnp.max(q_norm_ref[...] * k_norm)
        small_ref[0] = (largest <= 0.95 * SCORE_BOUND**2).astype(jnp.int32)


def self_scores(i, head, blocks, q_ref, k_ref, table_ref, q_lanes_ref, k_lanes_ref):
    piece = q_ref.shape[0] // 2
    mem_size = k_ref.shape[0] // q_ref.shape[0]
    q_at = pl.multiple_of(blocks[0, i], piece)
    k_at = pl.multiple_of(blocks[1, i], piece)
    q = half_of(q_ref[pl.ds(q_at, piece), :], head)
    q = jnp.concatenate([q, q_lanes_ref[pl.ds(q_at, piece), :]], axis=1)
    k = jnp.concatenate([k_ref[pl.ds(k_at, piece), :], k_lanes_ref[pl.ds(k_at, piece), :]], axis=1)
    return with_bias(nt(q, k), table_ref, head, 2 * mem_size - i if i >= mem_size else blocks[2, i])


def add_mixed(sums, i, mixed, low, mem_size):
    if i == 0:
        sums[0] = mixed
    elif i < mem_size:
        part = jnp.where(low, mixed, 0.0)
        sums[0] = sums[0] + part
        sums[1] = mixed - part if sums[1] is None else sums[1] + (mixed - part)
    else:
        sums[1] = mixed if sums[1] is None else sums[1] + mixed


def self_forward_kernel(
    blocks,
    q_ref,
    k_ref,
    v_ref,
    table_ref,
    q_lanes_ref,
    k_lanes_ref,
    hidden_ref,
    w_out_ref,
    gain_ref,
    w_next_ref,
    q_norm_ref,
    k_norm0_ref,
    k_norm1_ref,
    o_ref,
    back_lanes_ref,
    hidden_out,
    norm_out,
    next_out,
    next_norm,
    s_ref,
    mixed_ref,
    small_ref,
):
    rows = q_ref.shape[0]
    piece = rows // 2
    mem_size = k_ref.shape[0] // rows
    count = 2 * mem_size + 1
    ones = jnp.ones((piece, LANES), BF16)
    scores = functools.partial(
        self_scores,
        blocks=blocks,
        q_ref=q_ref,
        k_ref=k_ref,
        table_ref=table_ref,
        q_lanes_ref=q_lanes_ref,
        k_lanes_ref=k_lanes_ref,
    )
    mark_small(small_ref, q_norm_ref, k_norm0_ref, k_norm1_ref)

    def mix(i, p):
        k_at = pl.multiple_of(blocks[1, i], piece)
        return nn(p.astype(BF16), jnp.concatenate([v_ref[pl.ds(k_at, piece), :], ones], axis=1))

    def put(outs):
        for i in range(2):
            mixed = join_halves(outs[0][i], outs[1][i]).astype(BF16)
            o_ref[i * piece : (i + 1) * piece, :] = mixed
            mixed_ref[pl.program_id(0), i * piece : (i + 1) * piece, :] = mixed

    def close(head, sums, tops):
        mixed = []
        for at, total, top in ((0, sums[0], tops[0]), (piece, sums[1], tops[1])):
            weight = total[:, LANES:]
            mixed.append(total[:, :LANES] / weight)
            log_sum = jnp.log2(weight) if top is None else top + jnp.log2(weight)
            back_lanes_ref[head, at : at + piece, :] = with_log_sum(q_lanes_ref[at : at + piece, :], log_sum)
        return mixed

    @pl.when(small_ref[0] == 1)
    def _():
        outs = []
        for head in range(2):
            sums = [None, None]
            for i in range(count):
                add_mixed(sums, i, mix(i, jnp.exp2(scores(i, head))), blocks[3, i] == 1, mem_size)
            outs.append(close(head, sums, (None, None)))
        put(outs)

    @pl.when(small_ref[0] == 0)
    def _():
        outs = []
        for head in range(2):
            tops = []
            for i in range(count):
                s = scores(i, head)
                s_ref[i] = s
                tops.append(jnp.max(s, axis=1, keepdims=True))
            top_low, top_high = tops[0], tops[mem_size]
            for i in range(mem_size + 1, count):
                top_high = jnp.maximum(top_high, tops[i])
            for i in range(1, mem_size):
                low = blocks[3, i] == 1
                top_low = jnp.maximum(top_low, jnp.where(low, tops[i], NEGATIVE))
                top_high = jnp.maximum(top_high, jnp.where(low, NEGATIVE, tops[i]))
            sums = [None, None]
            for i in range(count):
                low = blocks[3, i] == 1
                top = top_low if i == 0 else top_high if i >= mem_size else jnp.where(low, top_low, top_high)
                add_mixed(sums, i, mix(i, jnp.exp2(s_ref[i] - top)), low, mem_size)
            outs.append(close(head, sums, (top_low, top_high)))
        put(outs)

    @pl.when(pl.program_id(0) == PAIRS - 1)
    def _():
        self_finish(
            mixed_ref, hidden_ref, w_out_ref, gain_ref, w_next_ref, hidden_out, norm_out, next_out, next_norm
        )


def pair_spec(rows):
    return pl.BlockSpec((rows, LANES), lambda p, *_: (0, p))


def whole_spec(rows):
    return pl.BlockSpec((rows, LANES), lambda p, *_: (0, 0))


def lanes_spec(rows):
    return pl.BlockSpec((2, rows, LANES), lambda p, *_: (p, 0, 0))


def cross_forward_kernel(
    q_ref,
    k_ref,
    v_ref,
    q_lanes_ref,
    k_lanes_ref,
    hidden_ref,
    w_out_ref,
    gain_ref,
    q_norm_ref,
    k_norm0_ref,
    k_norm1_ref,
    o_ref,
    back_lanes_ref,
    hidden_out,
    norm_out,
    mixed_ref,
    small_ref,
):
    rows, keys = q_ref.shape[0], k_ref.shape[0]
    tile, key_tile = min(256, rows), min(256, keys)
    mark_small(small_ref, q_norm_ref, k_norm0_ref, k_norm1_ref)

    def put(part, outs):
        mixed = join_halves(outs[0], outs[1]).astype(BF16)
        o_ref[part, :] = mixed
        mixed_ref[pl.program_id(0), part, :] = mixed

    @pl.when(small_ref[0] == 1)
    def _():
        ones = jnp.ones((key_tile, LANES), BF16)
        outs = []
        for head in range(2):
            q = jnp.concatenate([half_of(q_ref[...], head), q_lanes_ref[...]], axis=1)
            total = None
            for at in range(0, keys, key_tile):
                part = slice(at, at + key_tile)
                k = jnp.concatenate([k_ref[part, :], k_lanes_ref[part, :]], axis=1)
                v = jnp.concatenate([v_ref[part, :], ones], axis=1)
                mixed = nn(jnp.exp2(nt(q, k)).astype(BF16), v)
                total = mixed if total is None else total + mixed
            weight = total[:, LANES:]
            outs.append(total[:, :LANES] / weight)
            back_lanes_ref[head] = with_log_sum(q_lanes_ref[...], jnp.log2(weight))
        put(slice(0, rows), outs)

    @pl.when(small_ref[0] == 0)
    def _():
        k = jnp.concatenate([k_ref[...], k_lanes_ref[...]], axis=1)
        v = jnp.concatenate([v_ref[...], jnp.ones((keys, LANES), BF16)], axis=1)
        for at in range(0, rows, tile):
            part = slice(at, at + tile)
            outs = []
            for head in range(2):
                q = jnp.concatenate([half_of(q_ref[part, :], head), q_lanes_ref[part, :]], axis=1)
                s = nt(q, k)
                top = jnp.max(s, axis=1, keepdims=True)
                total = nn(jnp.exp2(s - top).astype(BF16), v)
                weight = total[:, LANES:]
                outs.append(total[:, :LANES] / weight)
                back_lanes_ref[head, part, :] = with_log_sum(q_lanes_ref[part, :], top + jnp.log2(weight))
            put(part, outs)

    @pl.when(pl.program_id(0) == PAIRS - 1)
    def _():
        self_finish(mixed_ref, hidden_ref, w_out_ref, gain_ref, None, hidden_out, norm_out, None, None)


def grad_lanes(o, do):
    inner = jnp.sum(o.astype(F32) * do.astype(F32), axis=1, keepdims=True)
    pieces = [piece.astype(F32) for piece in in_three(-inner)]
    return put_lanes(jnp.zeros(do.shape, F32), 0, pieces).astype(BF16)


def put_parts(at, dk, dv, own_ref, other_ref):
    rows = own_ref.shape[1]
    ref, start = (own_ref, at) if at < rows else (other_ref, at - rows)
    ref[0, start : start + dk.shape[0], :] = (dk * LN2).astype(BF16)
    ref[1, start : start + dv.shape[0], :] = dv.astype(BF16)


def cross_backward_kernel(
    q_ref, k_ref, v_ref, o_ref, do_ref, back_lanes_ref, k_lanes_ref, dq_ref, own_ref, other_ref
):
    rows, keys = q_ref.shape[0], k_ref.shape[0]
    tile = min(256, rows)
    k_turned = k_ref[...].T
    k_wide = jnp.concatenate([k_ref[...], k_lanes_ref[...]], axis=1)
    v_wide = jnp.concatenate([v_ref[...], jnp.ones((keys, LANES), BF16)], axis=1)
    dk = dv = None
    for at in range(0, rows, tile):
        part = slice(at, at + tile)
        dqs = []
        for head in range(2):
            q, do = half_of(q_ref[part, :], head), half_of(do_ref[part, :], head)
            q_wide = jnp.concatenate([q, back_lanes_ref[head, part, :]], axis=1)
            do_wide = jnp.concatenate([do, grad_lanes(o_ref[part, :], do)], axis=1)
            p = jnp.exp2(nt(k_wide, q_wide))
            ds = (p * nt(v_wide, do_wide)).astype(BF16)
            dv_part, dk_part = nn(p.astype(BF16), do), nn(ds, q)
            dv = dv_part if dv is None else dv + dv_part
            dk = dk_part if dk is None else dk + dk_part
            dqs.append(nn(k_turned[head * HEAD_DIM : (head + 1) * HEAD_DIM, :], ds))
        dq_ref[part, :] = jnp.concatenate(dqs, axis=0).T.astype(BF16)
    for at, size in ((0, rows), (rows, keys - rows)):
        put_parts(at, dk[at : at + size], dv[at : at + size], own_ref, other_ref)


def self_backward_kernel(
    blocks,
    q_ref,
    k_ref,
    v_ref,
    o_ref,
    do_ref,
    back_lanes_ref,
    k_lanes_ref,
    table_ref,
    dq_ref,
    own_ref,
    other_ref,
    grad_ref,
    do_lanes_ref,
    dq_sum,
    dk_sum,
    dv_sum,
):
    rows = q_ref.shape[0]
    piece = rows // 2
    mem_size = k_ref.shape[0] // rows
    count = 2 * mem_size + 1
    ones = jnp.ones((piece, LANES), BF16)
    for head in range(2):
        do_lanes_ref[head] = grad_lanes(o_ref[...], half_of(do_ref[...], head))
    dq_sum[...] = jnp.zeros_like(dq_sum)
    dk_sum[...] = jnp.zeros_like(dk_sum)
    dv_sum[...] = jnp.zeros_like(dv_sum)
    grad_ref[...] = jnp.zeros_like(grad_ref)
    for i in reversed(range(count)):
        q_at = pl.multiple_of(blocks[0, i], piece)
        k_at = pl.multiple_of(blocks[1, i], piece)
        k, v = k_ref[pl.ds(k_at, piece), :], v_ref[pl.ds(k_at, piece), :]
        k_turned = k.T
        k_wide = jnp.concatenate([k, k_lanes_ref[pl.ds(k_at, piece), :]], axis=1)
        v_wide = jnp.concatenate([v, ones], axis=1)
        dk = dv = None
        dqs = []
        for head in range(2):
            q = half_of(q_ref[pl.ds(q_at, piece), :], head)
            do = half_of(do_ref[pl.ds(q_at, piece), :], head)
            q_wide = jnp.concatenate([q, back_lanes_ref[head, pl.ds(q_at, piece), :]], axis=1)
            do_wide = jnp.concatenate([do, do_lanes_ref[head, pl.ds(q_at, piece), :]], axis=1)
            s = nt(k_wide, q_wide)
            kind = 2 * mem_size - i if i >= mem_size else blocks[2, i]
            p = jnp.exp2(with_bias(s, table_ref, head, kind, turned=True))
            ds = p * nt(v_wide, do_wide)
            add_grad(ds, grad_ref, head, kind)
            ds = ds.astype(BF16)
            dv_part, dk_part = nn(p.astype(BF16), do), nn(ds, q)
            dv = dv_part if dv is None else dv + dv_part
            dk = dk_part if dk is None else dk + dk_part
            dqs.append(nn(k_turned[head * HEAD_DIM : (head + 1) * HEAD_DIM, :], ds))
        which = 1 - blocks[3, i]
        dq_sum[which] = dq_sum[which] + jnp.concatenate(dqs, axis=0)
        dk_sum[pl.ds(k_at, piece), :] = dk_sum[pl.ds(k_at, piece), :] + dk
        dv_sum[pl.ds(k_at, piece), :] = dv_sum[pl.ds(k_at, piece), :] + dv
    for i in range(2):
        dq_ref[i * piece : (i + 1) * piece, :] = dq_sum[i].T.astype(BF16)
    for at in (0, rows):
        size = rows if at == 0 else k_ref.shape[0] - rows
        put_parts(at, dk_sum[at : at + size, :], dv_sum[at : at + size, :], own_ref, other_ref)


def table_spec(table):
    return pl.BlockSpec((2,) + table.shape[1:], lambda p, *_: (p, 0, 0, 0))


def attention_flops(scores, matmuls):
    return 2 * HEADS * scores * 256 * matmuls


def self_forward(blocks, q, k, v, table, q_lanes, k_lanes, hidden, w_out, gain, w_next, norms, after=()):
    rows, keys = q.shape[0], k.shape[0]
    piece = rows // 2
    return run(
        self_forward_kernel,
        "self_forward",
        (PAIRS,),
        [
            (q, pair_spec(rows)),
            (k, pair_spec(keys)),
            (v, pair_spec(keys)),
            (table, table_spec(table)),
            (q_lanes, None),
            (k_lanes, None, pltpu.HBM),
            (hidden, pl.BlockSpec((rows, gain.shape[1]), lambda *_: (0, 0))),
            (w_out, None),
            (gain, None),
            (w_next, None),
        ]
        + [(norm, None) for norm in norms],
        [
            (q.shape, BF16, pair_spec(rows)),
            ((HEADS, rows, LANES), BF16, lanes_spec(rows)),
            (q.shape, F32, None),
            (q.shape, BF16, None),
            (q.shape, BF16, None),
            ((1, LANES), F32, None),
        ],
        scratch=[
            pltpu.VMEM((blocks.shape[1], piece, piece), F32),
            pltpu.VMEM((PAIRS, rows, LANES), BF16),
            pltpu.SMEM((1,), jnp.int32),
        ],
        scalars=(blocks,),
        after=after,
        flops=attention_flops(blocks.shape[1] * piece * piece, 2),
    )


def cross_forward(q, k, v, q_lanes, k_lanes, hidden, w_out, gain, norms, after=()):
    rows, keys = q.shape[0], k.shape[0]
    return run(
        cross_forward_kernel,
        "cross_forward",
        (PAIRS,),
        [
            (q, pair_spec(rows)),
            (k, pair_spec(keys)),
            (v, pair_spec(keys)),
            (q_lanes, None),
            (k_lanes, None, pltpu.HBM),
            (hidden, None),
            (w_out, None),
            (gain, None),
        ]
        + [(norm, None) for norm in norms],
        [
            (q.shape, BF16, pair_spec(rows)),
            ((HEADS, rows, LANES), BF16, lanes_spec(rows)),
            (q.shape, F32, None),
            (q.shape, BF16, None),
        ],
        scratch=[pltpu.VMEM((PAIRS, rows, LANES), BF16), pltpu.SMEM((1,), jnp.int32)],
        after=after,
        flops=attention_flops(rows * keys, 2),
    )


def half_spec(rows, start):
    return pl.BlockSpec((rows, LANES), lambda p, *_: (0, p + start))


def cross_backward(q, k, v, o, do, back_lanes, k_lanes, start, count, after=()):
    rows, keys = q.shape[0], k.shape[0]
    width = count * LANES
    parts = pl.BlockSpec((2, rows, LANES), lambda p, *_: (0, 0, p))
    others_spec = pl.BlockSpec((2, keys - rows, LANES), lambda p, *_: (0, 0, p))
    return run(
        cross_backward_kernel,
        "cross_backward",
        (count,),
        [
            (q, half_spec(rows, start)),
            (k, half_spec(keys, start)),
            (v, half_spec(keys, start)),
            (o, half_spec(rows, start)),
            (do, half_spec(rows, start), None),
            (back_lanes, pl.BlockSpec((2, rows, LANES), lambda p, *_: (p + start, 0, 0))),
            (k_lanes, None, pltpu.HBM),
        ],
        [
            ((rows, width), BF16, pair_spec(rows)),
            ((2, rows, width), BF16, parts),
            ((2, keys - rows, width), BF16, others_spec),
        ],
        after=after,
        flops=attention_flops(rows * keys, 5) * count // PAIRS,
    )


def self_backward(blocks, q, k, v, o, do, back_lanes, k_lanes, table_t, start, count, after=()):
    rows, keys = q.shape[0], k.shape[0]
    piece = rows // 2
    width = count * LANES
    parts = pl.BlockSpec((2, rows, LANES), lambda p, *_: (0, 0, p))
    others_spec = pl.BlockSpec((2, keys - rows, LANES), lambda p, *_: (0, 0, p))
    return run(
        self_backward_kernel,
        "self_backward",
        (count,),
        [
            (q, half_spec(rows, start)),
            (k, half_spec(keys, start)),
            (v, half_spec(keys, start)),
            (o, half_spec(rows, start)),
            (do, half_spec(rows, start), None),
            (back_lanes, pl.BlockSpec((2, rows, LANES), lambda p, *_: (p + start, 0, 0))),
            (k_lanes, None, pltpu.HBM),
            (table_t, pl.BlockSpec((2,) + table_t.shape[1:], lambda p, *_: (p + start, 0, 0, 0))),
        ],
        [
            ((rows, width), BF16, pair_spec(rows)),
            ((2, rows, width), BF16, parts),
            ((2, keys - rows, width), BF16, others_spec),
            ((2 * count,) + table_t.shape[1:], F32, table_spec(table_t)),
        ],
        scratch=[
            pltpu.VMEM((2, rows, LANES), BF16),
            pltpu.VMEM((2, LANES, piece), F32),
            pltpu.VMEM((keys, LANES), F32),
            pltpu.VMEM((keys, LANES), F32),
        ],
        scalars=(blocks,),
        after=after,
        flops=attention_flops(blocks.shape[1] * piece * piece, 5) * count // PAIRS,
    )


def on_device(
    decoder_in,
    encoder_out,
    dec_segments,
    dec_mask,
    enc_segments,
    enc_mask,
    self_gain,
    cross_gain,
    ffn_gain,
    rel_bias,
    self_query,
    self_key,
    self_value,
    self_out,
    cross_query,
    cross_key,
    cross_value,
    cross_out,
    ffn_in,
    ffn_out,
    out_grad,
):
    mem_size = lax.axis_size("mem")
    rows, width = decoder_in.shape[1:]
    keys = rows * mem_size
    dp_index = lax.axis_index("dp")
    mine = (dp_index % 2).astype(jnp.int32)[None]
    group = group_of(dp_index, lax.axis_index("mem"), mem_size)
    odd = group % 2 == 1
    blocks = block_list(group, mem_size, rows)
    bits = bit_values()
    gain_self, gain_cross, gain_ffn = (g[None, :] for g in (self_gain, cross_gain, ffn_gain))
    first, rest = PAIRS // 2, PAIRS - PAIRS // 2

    lane = jnp.arange(LANES, dtype=jnp.int32)[None, :]
    tags = jnp.zeros((rows, LANES), jnp.int32)
    for i, tag in enumerate((dec_segments, dec_mask, enc_segments, enc_mask)):
        tags = jnp.where(lane == i, tag[0][:, None], tags)
    pieces = to_rows(jnp.concatenate([decoder_in[0], tags.astype(BF16)], axis=1))
    table, table_t = bias_tables(rel_bias, small_block(rows // 2))
    pair_in = jnp.stack([encoder_out[0], out_grad[0]])
    pieces, table, table_t, pair_in = fence([], pieces, table, table_t, pair_in)
    hidden_own = arranged(pieces, odd)

    hidden_others = jnp.concatenate(others(hidden_own))
    pair_pieces = to_rows(pair_in, axis=1)
    self_in, query_rows, *so_far, q_lanes, q_norm, k_norm0 = own_project(
        hidden_own, gain_self, self_query, self_key, self_value, keys
    )
    hidden_others, so_far = fence([], hidden_others, so_far)
    key_all, value_all, dec_lanes, enc_lanes, k_norm1 = other_project(hidden_others, gain_self, self_key, self_value, *so_far)
    self_mixed, self_lanes, hidden_one, cross_in, cross_rows, cross_norm = self_forward(
        blocks,
        query_rows,
        key_all,
        value_all,
        table,
        q_lanes,
        dec_lanes,
        hidden_own,
        self_out,
        gain_cross,
        cross_query,
        (q_norm, k_norm0, k_norm1),
    )
    pair_pieces, cross_rows = fence([], pair_pieces, cross_rows)

    encoder_own, cotangent = arranged(pair_pieces, odd, axis=1)
    encoder_others = jnp.concatenate(others(encoder_own))
    *so_far, k_norm0 = encoder_project(encoder_own, cross_key, cross_value, keys)
    encoder_others, so_far = fence([], encoder_others, so_far)

    cross_key_all, cross_value_all, k_norm1 = encoder_project(encoder_others, cross_key, cross_value, keys, so_far)
    cross_mixed, cross_lanes, hidden_two, ffn_input = cross_forward(
        cross_rows,
        cross_key_all,
        cross_value_all,
        q_lanes,
        enc_lanes,
        hidden_one,
        cross_out,
        gain_ffn,
        (cross_norm, k_norm0, k_norm1),
    )
    (layer_out, hidden_two_grad, cross_branch_grad, cross_mixed_grad, ffn_gain_grad), ffn_grads = feed_forward(
        mine, ffn_input, cotangent, ffn_in, ffn_out, hidden_two, gain_ffn, cross_out
    )

    ffn_a, ffn_b = Scatter(ffn_grads[0], "xyz"), Scatter(ffn_grads[1], "yxz", ffn_in.shape[1] // width)
    layer_out = from_rows(layer_out, odd)

    def cross_half(start, count, do):
        return cross_backward(
            cross_rows, cross_key_all, cross_value_all, cross_mixed, do, cross_lanes, enc_lanes, start, count
        )

    cross_q0, cross_own0, cross_other0 = cross_half(0, first, cross_mixed_grad)
    layer_out, cross_q0, cross_own0, cross_other0, cross_mixed_grad = fence(
        [ffn_a, ffn_b], layer_out, cross_q0, cross_own0, cross_other0, cross_mixed_grad
    )

    third = (ffn_a.span[1] + ffn_b.span[1]) // 3
    left = ffn_a.span[1] - third
    ffn_mid = (ffn_a.part(third, left, "yxz"), ffn_b.part(0, third - left, "yxz"))
    ffn_a, ffn_b, ffn_c = ffn_a.part(0, third, "xyz"), ffn_mid[0], ffn_b.part(third - left, third, "zxy")
    advance(bits, ffn_a, ffn_mid, ffn_c)
    came0 = came_parts(cross_other0, rows)
    cross_q1, cross_own1, cross_other1 = cross_half(first, rest, cross_mixed_grad)
    came0, cross_q1, cross_own1, cross_other1 = fence([], came0, cross_q1, cross_own1, cross_other1)

    came1 = came_parts(cross_other1, rows)
    (hidden_one_grad, self_mixed_grad, cross_gain_grad), grads = cross_finish(
        mine,
        (cross_q0, cross_q1),
        cross_query,
        hidden_one,
        gain_cross,
        hidden_two_grad,
        self_mixed,
        cross_mixed,
        cross_branch_grad,
        cross_in,
        self_out,
    )
    came1, hidden_one_grad, self_mixed_grad, grads = fence(
        [ffn_a, ffn_b, ffn_c], came1, hidden_one_grad, self_mixed_grad, grads
    )

    advance(bits, ffn_a, ffn_b)
    rest_a = Scatter(grads, "xyz")
    encoder_out_grad, grads = encoder_finish(
        mine, (cross_own0, cross_own1), (came0, came1), encoder_own, cross_key, cross_value, after=[ffn_a.keep]
    )
    encoder_out_grad, grads, self_mixed_grad = fence([rest_a], encoder_out_grad, grads, self_mixed_grad)

    rest_b = Scatter(grads, "yxz")
    encoder_out_grad = from_rows(encoder_out_grad, odd)

    def self_half(start, count, do):
        return self_backward(
            blocks, query_rows, key_all, value_all, self_mixed, do, self_lanes, dec_lanes, table_t, start, count
        )

    self_q0, self_own0, self_other0, table_grad0 = self_half(0, first, self_mixed_grad)
    encoder_out_grad, self_q0, self_own0, self_other0, self_mixed_grad = fence(
        [ffn_a, ffn_b, rest_a, rest_b], encoder_out_grad, self_q0, self_own0, self_other0, self_mixed_grad
    )

    level(ffn_a, ffn_b, bits=bits)
    advance(bits, (ffn_a, ffn_b), ffn_c, rest_a, rest_b)
    came0 = came_parts(self_other0, rows)
    self_q1, self_own1, self_other1, table_grad1 = self_half(first, rest, self_mixed_grad)
    came0, self_q1, self_own1, self_other1, table_grad1 = fence(
        [ffn_a, ffn_c, rest_b], came0, self_q1, self_own1, self_other1, table_grad1
    )

    came1 = came_parts(self_other1, rows)
    query_grads = query_grad(mine, (self_q0, self_q1), self_in)
    (query_grads,) = fence([], query_grads)

    own_q = Scatter(query_grads, "xyz")
    small = table_sums(table_grad0, table_grad1, cross_gain_grad, ffn_gain_grad)
    came1, small = fence([ffn_a, rest_a, rest_b, own_q], came1, small)

    advance(bits, ffn_a, ffn_c, rest_a, rest_b, own_q)
    sums, grads = key_grads(mine, (self_own0, self_own1), (came0, came1), self_in, after=[rest_a.keep])
    sums, grads = fence([], sums, grads)

    own = Scatter(grads, "yxz")
    decoder_in_grad, small = self_finish_back(
        (self_q0, self_q1),
        sums,
        hidden_own,
        gain_self,
        hidden_one_grad,
        self_query,
        self_key,
        self_value,
        small,
    )
    decoder_in_grad, small = fence([ffn_a, ffn_c, rest_a, rest_b, own_q, own], decoder_in_grad, small)

    small_bits = [("dp", 0), ("dp", 2), ("dp", 1), ("mem", 0), ("dp", 3)]
    small_bits = [name for name in small_bits if name in all_bits()]
    small_bits += [name for name in all_bits() if name not in small_bits]

    def add_small(small, rounds=1):
        for _ in range(min(rounds, len(small_bits))):
            small = small + swap_many(small, (small_bits.pop(0),))
        return small

    half = own.span[1] // 2
    own_k, own_v = own.part(0, half, "yxz"), own.part(half, half, "xyz")
    level(rest_a, rest_b, bits=bits)
    advance(bits, own_k, own_v, own_q, (rest_a, rest_b))
    (small,) = fence([own_k, own_v, own_q, rest_a], add_small(small, 2))

    advance(bits, own_k, own_v, ffn_c)
    decoder_in_grad = from_rows(decoder_in_grad, odd)
    (small,) = fence([own_k, own_v], add_small(small))

    level(own_k, own_v, own_q, bits=bits)
    advance(bits, (own_k, own_v, own_q), rest_a)
    (small,) = fence([own_k], add_small(small))
    small = add_small(small, len(small_bits))
    for scatter in (own_k, ffn_a, ffn_c, rest_a):
        while scatter.order:
            advance(bits, scatter)
    parts = small
    self_gain_sum, cross_gain_sum, ffn_gain_sum, table_sum, grad_fo, grad_fi, *squares = write_grads(
        (ffn_a, ffn_c), rest_a, own_k, parts, small_block(rows // 2), width, ffn_in.shape[1]
    )
    self_gain_sum, cross_gain_sum, ffn_gain_sum = self_gain_sum[0], cross_gain_sum[0], ffn_gain_sum[0]
    grad_co, grad_cq, grad_so, grad_ck, grad_cv, grad_sk, grad_sv, grad_sq = squares
    return (
        layer_out[None],
        decoder_in_grad[None],
        encoder_out_grad[None],
        self_gain_sum,
        cross_gain_sum,
        ffn_gain_sum,
        table_sum,
        grad_sq,
        grad_sk,
        grad_sv,
        grad_so,
        grad_cq,
        grad_ck,
        grad_cv,
        grad_co,
        grad_fi,
        grad_fo,
    )


def solution(mesh):
    in_specs = (
        P("dp", "mem", None),
        P("dp", "mem", None),
        P("dp", "mem"),
        P("dp", "mem"),
        P("dp", "mem"),
        P("dp", "mem"),
        P(),
        P(),
        P(),
        P(),
        P(),
        P(),
        P(),
        P(),
        P(),
        P(),
        P(),
        P(),
        P(),
        P(),
        P("dp", "mem", None),
    )
    out_specs = (
        P("dp", "mem", None),
        P("dp", "mem", None),
        P("dp", "mem", None),
        P(),
        P(),
        P(),
        P(),
        P("dp", "mem"),
        P("dp", "mem"),
        P("dp", "mem"),
        P("dp", "mem"),
        P("dp", "mem"),
        P("dp", "mem"),
        P("dp", "mem"),
        P("dp", "mem"),
        P("dp", "mem"),
        P("dp", "mem"),
    )
    return jax.shard_map(
        on_device, mesh=mesh, in_specs=in_specs, out_specs=out_specs, check_vma=False
    )
```

```python
import copy
import functools
import itertools
import math

import jax
import jax.numpy as jnp
import numpy as np
from jax import lax
from jax.experimental import pallas as pl
from jax.experimental.pallas import tpu as pltpu
from jax.sharding import PartitionSpec as P

HEADS = 12
HEAD_DIM = 64
BUCKETS = 32
MAX_DIST = 128
PAIRS = HEADS // 2
LANES = 128

EPSILON = 1e-06
NEGATIVE = -(2.0**30)
LOG2E = math.log2(math.e)
LN2 = math.log(2.0)
VMEM_LIMIT = 12 * 1024 * 1024
BF16 = jnp.bfloat16
F32 = jnp.float32


def bucket_edges():
    exact_max = BUCKETS // 2
    return [
        math.ceil(exact_max * (MAX_DIST / exact_max) ** (degree / exact_max))
        for degree in range(1, exact_max)
    ]


def rel_bucket(distance):
    exact_max = BUCKETS // 2
    log_bucket = exact_max + sum(
        (distance >= edge).astype(np.int32) for edge in bucket_edges()
    )
    return np.where(distance < exact_max, distance, log_bucket)


FAR = bucket_edges()[-1]


def near_types(block):
    return (FAR - 1 + block - 1) // block + 1


def group_of(dp, mem, mem_size):
    half = mem_size // 2
    return (dp % 2) * half + mem % half


def row_moves(dp_size, mem_size):
    half = mem_size // 2
    moves = ([], [])
    for dp in range(dp_size):
        for mem in range(mem_size):
            for piece in range(2):
                chunk = 2 * mem + piece
                group = chunk if chunk < mem_size else 2 * mem_size - 1 - chunk
                to_dp = dp - dp % 2 + group // half
                to_mem = (dp % 2) * half + group % half
                moves[piece].append((dp * mem_size + mem, to_dp * mem_size + to_mem))
    return moves


def to_rows(values, axis=0):
    moves = row_moves(lax.axis_size("dp"), lax.axis_size("mem"))
    return tuple(
        lax.ppermute(piece, ("dp", "mem"), move) for piece, move in zip(jnp.split(values, 2, axis=axis), moves)
    )


def arranged(pieces, odd, axis=0):
    first, second = pieces
    return jnp.concatenate(
        [jnp.where(odd, second, first), jnp.where(odd, first, second)], axis=axis
    )


def from_rows(values, odd, axis=0):
    moves = row_moves(lax.axis_size("dp"), lax.axis_size("mem"))
    low, high = jnp.split(values, 2, axis=axis)
    first, second = jnp.where(odd, high, low), jnp.where(odd, low, high)
    back = [[(there, here) for here, there in move] for move in moves]
    first = lax.ppermute(first, ("dp", "mem"), back[0])
    second = lax.ppermute(second, ("dp", "mem"), back[1])
    return jnp.concatenate([first, second], axis=axis)


def group_shift(values, step):
    dp_size, mem_size = lax.axis_size("dp"), lax.axis_size("mem")
    half = mem_size // 2
    moves = []
    for dp in range(dp_size):
        for mem in range(mem_size):
            group = (group_of(dp, mem, mem_size) + step) % mem_size
            to_dp = dp - dp % 2 + group // half
            to_mem = mem - mem % half + group % half
            moves.append((dp * mem_size + mem, to_dp * mem_size + to_mem))
    return lax.ppermute(values, ("dp", "mem"), moves)


def others(values):
    return [group_shift(values, step) for step in range(1, lax.axis_size("mem"))]


def came_parts(parts, rows):
    came = [
        group_shift(parts[:, (step - 1) * rows : step * rows], -step) for step in range(1, lax.axis_size("mem"))
    ]
    return came[0] if len(came) == 1 else sum(part.astype(F32) for part in came)


def block_list(group, mem_size, rows):
    piece = rows // 2
    q_at, k_at, kinds, is_low = [], [], [], []
    for i in range(2 * mem_size + 1):
        low = i <= group
        chunk = jnp.where(low, i, i - (group + 1))
        owner = jnp.where(chunk < mem_size, chunk, 2 * mem_size - 1 - chunk)
        slot = (group - owner) % mem_size
        q_at.append(jnp.where(low, 0, piece))
        k_at.append(slot * rows + jnp.where(chunk < mem_size, 0, piece))
        kinds.append(jnp.where(low, group - i, 2 * mem_size - i))
        is_low.append(low.astype(jnp.int32))
    return jnp.stack([jnp.stack(v).astype(jnp.int32) for v in (q_at, k_at, kinds, is_low)])


def bias_of(distance, rel_bias):
    hot = (rel_bucket(np.maximum(distance, 0))[..., None] == np.arange(BUCKETS)).astype(np.float32)
    values = jnp.einsum(
        "...b,bh->h...", jnp.asarray(hot), rel_bias - rel_bias[BUCKETS - 1], precision=lax.Precision.HIGHEST
    )
    return jnp.where(jnp.asarray(distance >= 0), values * LOG2E, NEGATIVE)


def spread(row, rows):
    width = row.shape[1]
    table = jnp.broadcast_to(row, (8, width))
    place = lax.broadcasted_iota(jnp.int32, (8, width), 0)
    for bit in range(3):
        moved = pltpu.roll(table, 1 << bit, 1)
        table = jnp.where((place >> bit) & 1 == 1, moved, table)
    size = 8
    while size < rows:
        table = jnp.concatenate([table, pltpu.roll(table, size, 1)], axis=0)
        size *= 2
    return table


def small_block(block):
    return min(LANES, block)


def table_kernel(base_ref, base_t_ref, table_ref, table_t_ref):
    heads, kinds, block = table_ref.shape[0], table_ref.shape[1] - 2, table_ref.shape[2]
    for head in range(heads):
        for base, table in ((base_ref, table_ref), (base_t_ref, table_t_ref)):
            table[head, 0] = jnp.full((block, block), NEGATIVE, F32)
            table[head, kinds + 1] = jnp.zeros((block, block), F32)
            for kind in range(kinds):
                table[head, kind + 1] = spread(base[head, kind], block)[:, block:]


def bias_tables(rel_bias, block):
    kinds = near_types(block)
    at = np.arange(2 * block)[None, :] - block
    start = np.arange(kinds)[:, None] * block
    base, base_t = bias_of(start - at, rel_bias), bias_of(start + at, rel_bias)
    if block % LANES:
        step = np.arange(block)[None, :] - np.arange(block)[:, None] + block
        masked = jnp.full((HEADS, 1, block, block), NEGATIVE, F32)
        return [jnp.concatenate([masked, v[:, :, step], jnp.zeros_like(masked)], axis=1) for v in (base, base_t)]
    heads = HEADS // 3
    spec = pl.BlockSpec((heads, kinds, 1, 2 * block), lambda h: (h, 0, 0, 0))
    out = pl.BlockSpec((heads, kinds + 2, block, block), lambda h: (h, 0, 0, 0))
    shape = jax.ShapeDtypeStruct((HEADS, kinds + 2, block, block), F32)
    return pl.pallas_call(
        table_kernel,
        grid=(HEADS // heads,),
        in_specs=[spec, spec],
        out_specs=[out, out],
        out_shape=[pltpu.HBM(shape.shape, shape.dtype)] * 2,
        compiler_params=pltpu.CompilerParams(vmem_limit_bytes=VMEM_LIMIT),
        name="bias_tables",
    )(base[:, :, None, :], base_t[:, :, None, :])


def small_parts(block, small):
    return [(r, c, (r - c) // small) for r in range(0, block, small) for c in range(0, block, small)]


def kind_index(step, kind, block, small, kinds):
    return jnp.clip(kind * (block // small) + step + 1, 0, kinds + 1)


def with_bias(s, table_ref, head, kind, turned=False):
    block, small, kinds = s.shape[0], table_ref.shape[2], table_ref.shape[1] - 2
    fixed = isinstance(kind, int)
    if fixed and (kind - 1) * block >= FAR - 1:
        return s
    pieces = {}
    for r, c, step in small_parts(block, small):
        at = (c, r) if turned else (r, c)
        part = s[at[0] : at[0] + small, at[1] : at[1] + small]
        if fixed:
            step = kind * (block // small) + step
            if step < kinds:
                part = part + table_ref[head, step + 1] if step >= 0 else jnp.full(part.shape, NEGATIVE, F32)
        else:
            part = part + table_ref[head, kind_index(step, kind, block, small, kinds)]
        pieces[at] = part
    starts = range(0, block, small)
    return jnp.concatenate([jnp.concatenate([pieces[a, b] for b in starts], axis=1) for a in starts], axis=0)


def add_grad(ds, grad_ref, head, kind):
    block, small, kinds = ds.shape[0], grad_ref.shape[2], grad_ref.shape[1] - 2
    fixed = isinstance(kind, int)
    for r, c, step in small_parts(block, small):
        part = ds[c : c + small, r : r + small]
        if fixed:
            step = kind * (block // small) + step
            if not 0 <= step < kinds:
                continue
            at = step + 1
        else:
            at = kind_index(step, kind, block, small, kinds)
        grad_ref[head, at] = grad_ref[head, at] + part


def fold(table):
    rows, width = table.shape
    while rows > 1:
        rows //= 2
        table = table[:rows] + pltpu.roll(table[rows:], width - rows, 1)
    return table


def fold_kernel(first_ref, rest_ref, cross_ref, ffn_ref, sums_ref):
    kinds = first_ref.shape[1] - 2
    sums_ref[...] = jnp.zeros_like(sums_ref)
    sums_ref[1:2, :], sums_ref[2:3, :] = cross_ref[...], ffn_ref[...]
    for part, ref in enumerate((first_ref, rest_ref)):
        heads = ref.shape[0]
        for head in range(heads):
            for kind in range(kinds):
                table = ref[head, kind + 1]
                width = 2 * table.shape[1]
                wide = jnp.concatenate([table, jnp.zeros_like(table)], axis=1)
                row = FIRST_HEAD_ROW + part * heads + head
                sums_ref[row : row + 1, kind * width : (kind + 1) * width] = fold(wide)


def table_sums(first, rest, cross_grad, ffn_grad):
    kinds, block = first.shape[1] - 2, first.shape[2]
    shape = (SMALL_ROWS, cross_grad.shape[1])
    if block % LANES:
        grad_t = jnp.pad(jnp.concatenate([first, rest])[:, 1 : kinds + 1], ((0, 0), (0, 0), (0, 0), (0, block)))
        place = (np.arange(block)[:, None] + np.arange(2 * block)[None, :]) % (2 * block)
        sums = jnp.sum(grad_t[:, :, np.arange(block)[:, None], place], axis=2).reshape(HEADS, -1)
        small = jnp.zeros(shape, F32).at[1].set(cross_grad[0]).at[2].set(ffn_grad[0])
        return small.at[FIRST_HEAD_ROW : FIRST_HEAD_ROW + HEADS, : sums.shape[1]].set(sums)
    return run(
        fold_kernel,
        "table_sums",
        (1,),
        [(first, None, pltpu.HBM), (rest, None, pltpu.HBM), (cross_grad, None), (ffn_grad, None)],
        [(shape, F32, None)],
    )[0]


def bucket_hot(block):
    kinds = near_types(block)
    at = np.arange(2 * block)[None, :]
    at = np.where(at < block, at, at - 2 * block) + np.arange(kinds)[:, None] * block
    near = (at >= 0) & (at < FAR)
    hot = (rel_bucket(np.maximum(at, 0))[..., None] == np.arange(BUCKETS)) & near[..., None]
    return hot.reshape(-1, BUCKETS).T.astype(np.float32)


def write_kernel(chunks, *refs):
    counts, chunks = chunks
    totals, at = [], 0
    for count in counts:
        parts = [ref[...].astype(F32) for ref in refs[at : at + count]]
        totals.append(sum(parts[1:], parts[0]))
        at += count
    first, second, rest, own = totals
    ffn = jnp.concatenate([first, second], axis=0)
    small, hot = refs[at][...], refs[at + 1][...]
    refs = refs[at + 2 :]
    gains, table_ref, fo_ref, fi_ref, squares = refs[:3], refs[3], refs[4], refs[5], refs[6:]
    for i in range(3):
        gains[i][...] = small[i : i + 1, :]
    sums = small[FIRST_HEAD_ROW : FIRST_HEAD_ROW + HEADS, : hot.shape[1]]
    near = lax.dot_general(
        hot, sums, (((1,), (1,)), ((), ())), precision=lax.Precision.HIGHEST, preferred_element_type=F32
    )
    last = -jnp.sum(near, axis=0, keepdims=True)
    bucket = lax.broadcasted_iota(jnp.int32, near.shape, 0)
    table_ref[...] = jnp.where(bucket == BUCKETS - 1, last, near)
    rows, cols = fo_ref.shape
    fo_ref[...] = ffn[:rows]
    each = fi_ref.shape[0]
    for i in range(chunks):
        fi_ref[:, i * cols : (i + 1) * cols] = ffn[rows + i * each : rows + (i + 1) * each]
    at = 0
    for total in (rest, own):
        for i in range(total.shape[0] // each):
            squares[at][...] = total[i * each : (i + 1) * each]
            at += 1


def write_grads(ffn, rest, own, small, block, width, hidden):
    dp_size, mem_size = lax.axis_size("dp"), lax.axis_size("mem")
    hot = jnp.asarray(bucket_hot(block))
    square = ((width // dp_size, width // mem_size), F32, None)
    return run(
        functools.partial(write_kernel, ([1 + len(s.came) for s in (*ffn, rest, own)], hidden // width)),
        "write_grads",
        (1,),
        [(v.reshape(v.shape[-2:]), None) for s in (*ffn, rest, own) for v in (s.keep, *s.came)]
        + [(v, None) for v in (small, hot)],
        [((1, width), F32, None)] * 3
        + [
            ((BUCKETS, HEADS), F32, None),
            ((hidden // dp_size, width // mem_size), F32, None),
            ((width // dp_size, hidden // mem_size), F32, None),
        ]
        + [square] * 8,
    )


def nt(a, b):
    return lax.dot_general(a, b, (((1,), (1,)), ((), ())), preferred_element_type=F32)


def nn(a, b):
    return jnp.dot(a, b, preferred_element_type=F32)


def half_of(values, head):
    lane = lax.broadcasted_iota(jnp.int32, values.shape, 1)
    return jnp.where((lane >= HEAD_DIM) == (head == 1), values, jnp.zeros_like(values))


def join_halves(first, second):
    lane = lax.broadcasted_iota(jnp.int32, first.shape, 1)
    return jnp.where(lane < HEAD_DIM, first, second)


def in_three(values):
    high = values.astype(BF16)
    rest = values - high.astype(F32)
    mid = rest.astype(BF16)
    low = (rest - mid.astype(F32)).astype(BF16)
    return high, mid, low


def put_lanes(base, start, values):
    lane = lax.broadcasted_iota(jnp.int32, base.shape, 1)
    for i, value in enumerate(values):
        base = jnp.where(lane == start + i, value, base)
    return base


def with_log_sum(mask_lanes, log_sum):
    pieces = [piece.astype(F32) for piece in in_three(-log_sum)]
    return put_lanes(mask_lanes.astype(F32), 3, pieces).astype(BF16)


def bit_count(axis):
    return lax.axis_size(axis).bit_length() - 1


def swap(values, axis, bit):
    size = lax.axis_size(axis)
    return lax.ppermute(values, axis, [(i, i ^ (1 << bit)) for i in range(size)])


def swap_many(values, names):
    dp_size, mem_size = lax.axis_size("dp"), lax.axis_size("mem")
    flips = {axis: sum(1 << bit for name, bit in names if name == axis) for axis in ("dp", "mem")}
    moves = [
        (dp * mem_size + mem, (dp ^ flips["dp"]) * mem_size + (mem ^ flips["mem"]))
        for dp in range(dp_size)
        for mem in range(mem_size)
    ]
    return lax.ppermute(values, ("dp", "mem"), moves)


def bit_order(order):
    dp_bits, mem_bits = bit_count("dp"), bit_count("mem")
    z_bits = [("dp", b) for b in range(2, dp_bits)]
    groups = {
        "x": [("mem", b) for b in range(mem_bits)],
        "y": [("dp", b) for b in range(1, min(2, dp_bits))],
        "Z": z_bits[:1],
        "z": z_bits[1:] if "Z" in order else z_bits,
    }
    return [step for name in order for step in groups[name]]


def in_pairs(names):
    return [tuple(names[i : i + 2]) for i in range(0, len(names), 2)]


SMALL_ROWS = 16
FIRST_HEAD_ROW = 4


TILE = 256
LIMITS = {
    "own_project": 12,
    "other_project": 12,
    "encoder_project": 12,
    "self_forward": 18,
    "cross_forward": 18,
    "feed_forward": 34,
    "cross_backward": 18,
    "cross_finish": 30,
    "encoder_finish": 18,
    "self_backward": 18,
    "table_sums": 12,
    "query_grad": 12,
    "key_grads": 18,
    "self_finish_back": 18,
    "advance": 24,
    "write_grads": 16,
}


def tn(a, b):
    return lax.dot_general(a, b, (((0,), (0,)), ((), ())), preferred_element_type=F32)


def normed(hidden, gain):
    return hidden * lax.rsqrt(jnp.mean(hidden * hidden, axis=-1, keepdims=True) + EPSILON) * gain


def norm_back(hidden, gain, grad):
    scale = lax.rsqrt(jnp.mean(hidden * hidden, axis=-1, keepdims=True) + EPSILON)
    unit = hidden * scale
    inner = grad * gain
    out = scale * (inner - unit * jnp.mean(inner * unit, axis=-1, keepdims=True))
    return out, jnp.sum(grad * unit, axis=0, keepdims=True)


def whole(array):
    zeros = (0,) * array.ndim
    return pl.BlockSpec(array.shape, lambda *_: zeros)


def run(kernel, name, grid, ins, outs, scratch=(), scalars=(), after=(), flops=0, aliases=None):
    count = len(scalars) + len(ins)
    in_places = [v[2] if len(v) > 2 else None if v[1] is None or v[1] is ANY else pltpu.HBM for v in ins]
    out_places = [v[3] if len(v) > 3 else None if v[2] is None else pltpu.HBM for v in outs]
    ins, outs = [v[:2] for v in ins], [v[:3] for v in outs]

    def body(*refs):
        kernel(*refs[:count], *refs[count + len(after) :])

    out_shape = [jax.ShapeDtypeStruct(shape, dtype) for shape, dtype, _ in outs]
    placed = [o if p is None else p(o.shape, o.dtype) for o, p in zip(out_shape, out_places)]
    arrays = [a if p is None else pltpu.with_memory_space_constraint(a, p) for (a, _), p in zip(ins, in_places)]
    moved = sum(a.size * a.dtype.itemsize for a, _ in ins) + sum(
        math.prod(s) * jnp.dtype(d).itemsize for s, d, _ in outs
    )
    return pl.pallas_call(
        body,
        grid_spec=pltpu.PrefetchScalarGridSpec(
            num_scalar_prefetch=len(scalars),
            grid=grid,
            in_specs=[whole(a) if s is None else s for a, s in ins]
            + [pl.BlockSpec(memory_space=pl.ANY) for _ in after],
            out_specs=[whole(o) if s is None else s for o, (_, _, s) in zip(out_shape, outs)],
            scratch_shapes=list(scratch),
        ),
        out_shape=placed,
        input_output_aliases=aliases or {},
        compiler_params=pltpu.CompilerParams(vmem_limit_bytes=LIMITS[name] << 20),
        cost_estimate=pl.CostEstimate(flops=flops // 16, bytes_accessed=moved // 16, transcendentals=0),
        name=name,
    )(*scalars, *arrays, *after)


ANY = pl.BlockSpec(memory_space=pl.ANY)


def row_spec(tile, width, shift=0):
    return pl.BlockSpec((tile, width), lambda i, *_: (i + shift, 0))


def fits(rows, cols):
    dp_size, mem_size = lax.axis_size("dp"), lax.axis_size("mem")
    return (rows // dp_size) % 16 == 0 and (cols // mem_size) % LANES == 0


def emit(mine, total_ref, keep_ref, send_ref, at, rows):
    mem_size, pairs, _, cols = keep_ref.shape
    chunks = total_ref.shape[1] // cols // mem_size
    for pair in range(pairs):
        keep_at = pl.multiple_of((2 * pair + mine) * rows, 16)
        send_at = pl.multiple_of((2 * pair + 1 - mine) * rows, 16)
        for mem in range(mem_size):
            for chunk in range(chunks):
                lanes = slice((mem * chunks + chunk) * cols, (mem * chunks + chunk + 1) * cols)
                place = slice(at + chunk * rows, at + (chunk + 1) * rows)
                keep_ref[mem, pair, place, :] = total_ref[pl.ds(keep_at, rows), lanes].astype(BF16)
                send_ref[mem, pair, place, :] = total_ref[pl.ds(send_at, rows), lanes].astype(BF16)


def square_outs(count, width):
    dp_size, mem_size = lax.axis_size("dp"), lax.axis_size("mem")
    if fits(width, width):
        shape = (mem_size, dp_size // 2, count * width // dp_size, width // mem_size)
        return [(shape, BF16, None)] * 2
    return [((width, width), BF16, None)] * count


def write_square(mine, index, total, total_ref, out_refs):
    if len(out_refs[0].shape) == 4:
        keep_ref, send_ref = out_refs
        rows = total.shape[0] // (2 * keep_ref.shape[1])
        total_ref[...] = total
        emit(mine, total_ref, keep_ref, send_ref, index * rows, rows)
    else:
        out_refs[index][...] = total.astype(BF16)


def in_order(grads, chunks=1):
    if grads[0].ndim == 4:
        return grads
    dp_size, mem_size = lax.axis_size("dp"), lax.axis_size("mem")
    cuts = []
    for grad in grads:
        rows, cols = grad.shape[0] // dp_size, grad.shape[1] // mem_size // chunks
        cut = grad.reshape(dp_size // 2, 2, rows, mem_size, chunks, cols).transpose(1, 3, 0, 4, 2, 5)
        cuts.append(cut.reshape(2, mem_size, dp_size // 2, chunks * rows, cols))
    cut = jnp.concatenate(cuts, axis=3)
    mine = lax.axis_index("dp") & 1
    return [lax.dynamic_index_in_dim(cut, which, 0, keepdims=False) for which in (mine, 1 - mine)]


class Scatter:
    def __init__(self, grads, order, chunks=1):
        keep, send = in_order(grads, chunks)
        mem_bits, dp_bits = bit_count("mem"), bit_count("dp")
        self.names = [("mem", b) for b in reversed(range(mem_bits))]
        self.names += [("dp", b) for b in reversed(range(1, dp_bits))]
        self.order = []
        for part in order.split("]"):
            single, _, paired = part.partition("[")
            self.order += [(name,) for name in bit_order(single)] + in_pairs(bit_order(paired))
        shape = (2,) * len(self.names) + keep.shape[2:]
        self.keep, self.came = keep.reshape(shape), [swap(send, "dp", 0).reshape(shape)]
        self.span = (0, shape[-2])

    def part(self, start, size, order):
        share = copy.copy(self)
        share.names, share.span = list(self.names), (self.span[0] + start, size)
        share.order = [(name,) for name in bit_order(order)]
        return share


def all_bits():
    return [("mem", b) for b in range(bit_count("mem"))] + [("dp", b) for b in range(bit_count("dp"))]


def bit_values():
    return jnp.stack([((lax.axis_index(axis) >> bit) & 1).astype(jnp.int32) for axis, bit in all_bits()])


def level(*group, bits):
    while any(v.order != group[0].order for v in group):
        longest = max(sum(map(len, v.order)) for v in group)
        advance(bits, *[v for v in group if sum(map(len, v.order)) == longest])


def advance_kernel(moves, count, bits, *refs):
    ins, outs = refs[:count], refs[count:]
    at = 0
    for names, places, left, sources in moves:
        flips = [(0,), (1,)] if len(names) == 1 else [(0, 0), (0, 1), (1, 0), (1, 1)]
        for out, flip in zip(outs[at : at + len(flips)], flips):
            halves = [bits[name] if f == 0 else 1 - bits[name] for name, f in zip(names, flip)]
            for kept in itertools.product((0, 1), repeat=left):
                place = list(kept)
                for where, half in zip(places, halves):
                    place.insert(where, half)
                start = 0
                for parts, from_row, size in sources:
                    rows = slice(from_row, from_row + size)
                    values = [ins[part][(*place, rows, slice(None))].astype(F32) for part in parts]
                    out[(*kept, slice(start, start + size), slice(None))] = sum(values[1:], values[0]).astype(BF16)
                    start += size
        at += len(flips)


def advance(bits, *groups):
    groups = [group if isinstance(group, tuple) else (group,) for group in groups]
    for group in groups:
        lead = group[0]
        assert all(v.names == lead.names and v.order == lead.order for v in group)
        if not lead.order and len(group) > 1:
            sums = [sum(v.came, v.keep.astype(F32))[..., v.span[0] : sum(v.span), :] for v in group]
            lead.keep = jnp.concatenate(sums, axis=-2)
            lead.came, lead.span = [jnp.zeros_like(lead.keep)], (0, lead.keep.shape[-2])
    groups = [group for group in groups if group[0].order]
    if not groups:
        return
    moves, arrays, shapes, heads = [], [], [], []

    def index_of(array):
        for i, known in enumerate(arrays):
            if known is array:
                return i
        arrays.append(array)
        return len(arrays) - 1

    for group in groups:
        lead = group[0]
        names = tuple(sorted(lead.order.pop(0), key=lead.names.index))
        places = [lead.names.index(name) for name in names]
        lead.names = [name for name in lead.names if name not in names]
        sources = [([index_of(a) for a in (v.keep, *v.came)], *v.span) for v in group]
        moves.append(([all_bits().index(name) for name in names], places, len(lead.names), sources))
        rows = sum(v.span[1] for v in group)
        shapes += [(2,) * len(lead.names) + (rows, lead.keep.shape[-1])] * 2 ** len(names)
        heads.append((names, rows))
    total = sum(v.size * 2 for v in arrays)
    cols = arrays[0].shape[-1]
    if total >= 9 << 20 and all(v.shape[-1] == cols for v in arrays) and cols % LANES == 0:
        steps = cols // LANES

        def spec(shape):
            zeros = (0,) * (len(shape) - 1)
            return pl.BlockSpec(shape[:-1] + (LANES,), lambda i, *_: (*zeros, i))

    else:
        steps = 1

        def spec(shape):
            return None

    results = run(
        functools.partial(advance_kernel, moves, len(arrays)),
        "advance",
        (steps,),
        [(v, spec(v.shape)) for v in arrays],
        [(shape, BF16, spec(shape)) for shape in shapes],
        scalars=(bits,),
        flops=total,
    )
    for group, (names, rows) in zip(groups, heads):
        lead = group[0]
        lead.keep, *sends = results[: 2 ** len(names)]
        lead.span = (0, rows)
        results = results[2 ** len(names) :]
        partners = [names] if len(names) == 1 else [names[1:], names[:1], names]
        lead.came = [swap_many(send, partner) for send, partner in zip(sends, partners)]


def fence(scatters, *values):
    states = [(v.keep, v.came) for v in scatters]
    states, values = lax.optimization_barrier((states, values))
    for scatter, (keep, came) in zip(scatters, states):
        scatter.keep, scatter.came = keep, came
    return values


def head_norms(rows):
    wide = rows.astype(F32)
    shape = (rows.shape[1], LANES)
    head = lax.broadcasted_iota(jnp.int32, shape, 0) // HEAD_DIM == lax.broadcasted_iota(jnp.int32, shape, 1)
    return jnp.max(nn((wide * wide).astype(BF16), head.astype(F32).astype(BF16)), axis=0, keepdims=True)


def put_norms(norm_ref, rows):
    norms = head_norms(rows)

    @pl.when(pl.program_id(0) == 0)
    def _():
        norm_ref[...] = norms

    @pl.when(pl.program_id(0) > 0)
    def _():
        norm_ref[...] = jnp.maximum(norm_ref[...], norms)


def tag_lanes(tags, first):
    lane = lax.broadcasted_iota(jnp.int32, tags.shape, 1)
    tags = tags.astype(F32)
    kept = (tags[:, first : first + 1] == lane.astype(F32)) & (tags[:, first + 1 : first + 2] > 0)
    lanes = jnp.where(lane < 3, jnp.where(kept, 0.0, NEGATIVE), 0.0)
    return jnp.where((lane >= 3) & (lane < 6), 1.0, lanes).astype(BF16)


def own_project_kernel(
    x_ref,
    gain_ref,
    wq_ref,
    wk_ref,
    wv_ref,
    a_ref,
    q_ref,
    k_ref,
    v_ref,
    dec_ref,
    enc_ref,
    q_lanes_ref,
    q_norm_ref,
    k_norm_ref,
):
    width = gain_ref.shape[1]
    a = normed(x_ref[:, :width].astype(F32), gain_ref[...]).astype(BF16)
    a_ref[...] = a
    q = (nn(a, wq_ref[...]) * LOG2E).astype(BF16)
    k = nn(a, wk_ref[...]).astype(BF16)
    q_ref[...], k_ref[...] = q, k
    v_ref[...] = nn(a, wv_ref[...]).astype(BF16)
    put_norms(q_norm_ref, q), put_norms(k_norm_ref, k)
    tags = x_ref[:, width:]
    dec_ref[...], enc_ref[...] = tag_lanes(tags, 0), tag_lanes(tags, 2)
    lane = lax.broadcasted_iota(jnp.int32, tags.shape, 1)
    q_lanes_ref[...] = ((tags[:, 0:1].astype(F32) == lane.astype(F32)) & (lane < 3)).astype(F32).astype(BF16)


def other_project_kernel(
    x_ref,
    gain_ref,
    wk_ref,
    wv_ref,
    k_old,
    v_old,
    dec_old,
    enc_old,
    k_ref,
    v_ref,
    dec_ref,
    enc_ref,
    k_norm_ref,
):
    width = gain_ref.shape[1]
    a = normed(x_ref[:, :width].astype(F32), gain_ref[...]).astype(BF16)
    k = nn(a, wk_ref[...]).astype(BF16)
    k_ref[...] = k
    v_ref[...] = nn(a, wv_ref[...]).astype(BF16)
    put_norms(k_norm_ref, k)
    tags = x_ref[:, width:]
    dec_ref[...], enc_ref[...] = tag_lanes(tags, 0), tag_lanes(tags, 2)


def encoder_project_kernel(x_ref, wk_ref, wv_ref, *refs):
    k_ref, v_ref, k_norm_ref = refs[-3:]
    k = nn(x_ref[...], wk_ref[...]).astype(BF16)
    k_ref[...] = k
    put_norms(k_norm_ref, k)
    v_ref[...] = nn(x_ref[...], wv_ref[...]).astype(BF16)


def own_project(x, gain, wq, wk, wv, keys):
    rows, width = x.shape[0], gain.shape[1]
    tile = min(TILE, rows)
    spec, lanes = row_spec(tile, width), row_spec(tile, LANES)
    return run(
        own_project_kernel,
        "own_project",
        (rows // tile,),
        [(x, row_spec(tile, x.shape[1]), None), (gain, None), (wq, None), (wk, None), (wv, None)],
        [((n, width), BF16, spec) for n in (rows, rows, keys, keys)]
        + [((n, LANES), BF16, lanes) for n in (keys, keys, rows)]
        + [((1, LANES), F32, None)] * 2,
        flops=6 * rows * width * width,
    )


def other_project(x, gain, wk, wv, *so_far):
    rows, width = x.shape[0], gain.shape[1]
    tile = min(TILE, rows)
    shift = (so_far[0].shape[0] - rows) // tile
    spec, lanes = row_spec(tile, width, shift), row_spec(tile, LANES, shift)
    return run(
        other_project_kernel,
        "other_project",
        (rows // tile,),
        [(x, row_spec(tile, x.shape[1]), None), (gain, None), (wk, None), (wv, None)] + [(v, ANY) for v in so_far],
        [(v.shape, BF16, s) for v, s in zip(so_far, (spec, spec, lanes, lanes))] + [((1, LANES), F32, None)],
        aliases={4: 0, 5: 1, 6: 2, 7: 3},
        flops=4 * rows * width * width,
    )


def encoder_project(x, wk, wv, keys, so_far=()):
    rows, width = x.shape
    tile = min(TILE, rows)
    spec = row_spec(tile, width, (keys - rows) // tile if so_far else 0)
    return run(
        encoder_project_kernel,
        "encoder_project",
        (rows // tile,),
        [(x, row_spec(tile, width), None), (wk, None), (wv, None)] + [(v, ANY) for v in so_far],
        [((keys, width), BF16, spec)] * 2 + [((1, LANES), F32, None)],
        aliases={3: 0, 4: 1} if so_far else None,
        flops=4 * rows * width * width,
    )


def self_finish(mixed_ref, hidden_ref, w_out_ref, gain_ref, w_next_ref, hidden_out, norm_out, next_out, next_norm):
    rows = hidden_ref.shape[0]
    tile = min(TILE, rows)
    for at in range(0, rows, tile):
        o = jnp.concatenate([mixed_ref[p, at : at + tile, :] for p in range(PAIRS)], axis=1)
        hidden = hidden_ref[at : at + tile, :].astype(F32) + nn(o, w_out_ref[...])
        hidden_out[at : at + tile, :] = hidden
        b = normed(hidden, gain_ref[...]).astype(BF16)
        norm_out[at : at + tile, :] = b
        if w_next_ref is not None:
            following = (nn(b, w_next_ref[...]) * LOG2E).astype(BF16)
            next_out[at : at + tile, :] = following
            norms = head_norms(following)
            next_norm[...] = norms if at == 0 else jnp.maximum(next_norm[...], norms)


def ffn_kernel(mine_ref, c_ref, og_ref, wi_ref, wo_ref, h2_ref, gain_ref, wco_ref, *refs):
    layer_ref, dh2_ref, dyc_ref, doc_ref, dgain_ref, *grad_refs, y_sum, dc_sum, total_ref, turned_ref = refs
    step, steps = pl.program_id(0), pl.num_programs(0)
    mine = mine_ref[0]
    c, og, wi, wo = c_ref[...], og_ref[...], wi_ref[...], wo_ref[...]

    @pl.when(step == 0)
    def _():
        turned_ref[...] = c.T

    u = nn(c, wi)
    slope = math.sqrt(2.0 / math.pi)
    square = u * u
    bend = jnp.tanh(u * (slope + (slope * 0.044715) * square))
    half = 0.5 + 0.5 * bend
    wide = u * half
    g = wide.astype(BF16)
    rate = half + wide * ((1.0 - bend) * (slope + (slope * 3.0 * 0.044715) * square))
    y = nn(g, wo)
    du = (nt(og, wo) * rate).astype(BF16)
    dc = nt(du, wi)

    @pl.when(step == 0)
    def _():
        y_sum[...] = y
        dc_sum[...] = dc

    @pl.when(step > 0)
    def _():
        y_sum[...] += y
        dc_sum[...] += dc

    out_total, in_total = tn(g, og), nn(turned_ref[...], du)
    if len(grad_refs) == 4:
        total_ref[...] = out_total
        emit(mine, total_ref, grad_refs[0], grad_refs[1], 0, grad_refs[0].shape[2])
        total_ref[...] = in_total
        rows = grad_refs[2].shape[2] * grad_refs[2].shape[3] // total_ref.shape[1]
        emit(mine, total_ref, grad_refs[2], grad_refs[3], 0, rows)
    else:
        grad_refs[0][...] = out_total.astype(BF16)
        grad_refs[1][...] = in_total.astype(BF16)

    @pl.when(step == steps - 1)
    def _():
        rows = h2_ref.shape[0]
        tile = min(TILE, rows)
        dgain = jnp.zeros(dgain_ref.shape, F32)
        for at in range(0, rows, tile):
            part = slice(at, at + tile)
            hidden = h2_ref[part, :]
            layer_ref[part, :] = (hidden + y_sum[part, :]).astype(BF16)
            back, gain_part = norm_back(hidden, gain_ref[...], dc_sum[part, :])
            dgain = dgain + gain_part
            dh2 = og_ref[part, :].astype(F32) + back
            dh2_ref[part, :] = dh2
            dyc = dh2.astype(BF16)
            dyc_ref[part, :] = dyc
            doc_ref[part, :] = nt(dyc, wco_ref[...]).astype(BF16)
        dgain_ref[...] = dgain


def feed_forward(mine, c, og, wi, wo, h2, gain, wco, after=()):
    rows, width = c.shape
    hidden = wi.shape[1]
    dp_size, mem_size = lax.axis_size("dp"), lax.axis_size("mem")
    chunk = width
    steps = hidden // chunk
    direct = fits(width, width) and steps == 2 * mem_size and (chunk * dp_size) % (2 * hidden) == 0
    if direct:
        pairs, rows_o, cols_o = dp_size // 2, hidden // dp_size, width // mem_size
        chunk_rows = width // dp_size * (chunk // cols_o)
        grads = [
            (
                (mem_size, pairs, rows_o, cols_o),
                BF16,
                pl.BlockSpec((mem_size, pairs // steps, rows_o, cols_o), lambda f, *_: (0, f, 0, 0)),
            )
        ] * 2 + [
            (
                (mem_size, pairs, rows_o, cols_o),
                BF16,
                pl.BlockSpec((1, pairs, chunk_rows, cols_o), lambda f, *_: (f // 2, 0, f % 2, 0)),
            )
        ] * 2
    else:
        grads = [
            ((hidden, width), BF16, pl.BlockSpec((chunk, width), lambda f, *_: (f, 0))),
            ((width, hidden), BF16, pl.BlockSpec((width, chunk), lambda f, *_: (0, f))),
        ]
    outs = run(
        ffn_kernel,
        "feed_forward",
        (steps,),
        [
            (c, None),
            (og, None),
            (wi, pl.BlockSpec((width, chunk), lambda f, *_: (0, f))),
            (wo, pl.BlockSpec((chunk, width), lambda f, *_: (f, 0))),
            (h2, None),
            (gain, None),
            (wco, None),
        ],
        [
            (c.shape, BF16, None),
            (c.shape, F32, None),
            (c.shape, BF16, None),
            (c.shape, BF16, None),
            (gain.shape, F32, None),
        ]
        + grads,
        scratch=[
            pltpu.VMEM(c.shape, F32),
            pltpu.VMEM(c.shape, F32),
            pltpu.VMEM((chunk, width), F32),
            pltpu.VMEM((width, rows), BF16),
        ],
        scalars=(mine,),
        after=after,
        flops=12 * rows * width * hidden,
    )
    grads = outs[5:]
    return outs[:5], [grads[0:2], grads[2:4]] if direct else [grads[0:1], grads[1:2]]


def cross_finish_kernel(
    mine_ref, dq0_ref, dq1_ref, wq_ref, h1_ref, gain_ref, dh2_ref, o_ref, oc_ref, dyc_ref, b_ref, wso_ref, *refs
):
    dh1_ref, do_ref, dgain_ref, *grad_refs, dy_ref, total_ref = refs
    mine = mine_ref[0]
    dq = jnp.concatenate([dq0_ref[...], dq1_ref[...]], axis=1)
    rows = h1_ref.shape[0]
    tile = min(TILE, rows)
    write_square(mine, 0, tn(oc_ref[...], dyc_ref[...]), total_ref, grad_refs)
    write_square(mine, 1, tn(b_ref[...], dq), total_ref, grad_refs)
    dgain = jnp.zeros(dgain_ref.shape, F32)
    for at in range(0, rows, tile):
        part = slice(at, at + tile)
        db = nt(dq[part, :], wq_ref[...])
        back, gain_part = norm_back(h1_ref[part, :], gain_ref[...], db)
        dgain = dgain + gain_part
        dh1 = dh2_ref[part, :] + back
        dh1_ref[part, :] = dh1
        dy = dh1.astype(BF16)
        dy_ref[part, :] = dy
        do_ref[part, :] = nt(dy, wso_ref[...]).astype(BF16)
    dgain_ref[...] = dgain
    write_square(mine, 2, tn(o_ref[...], dy_ref[...]), total_ref, grad_refs)


def cross_finish(mine, dq, wq, h1, gain, dh2, o, oc, dyc, b, wso, after=()):
    rows, width = h1.shape
    outs = run(
        cross_finish_kernel,
        "cross_finish",
        (1,),
        [(v, None) for v in (*dq, wq, h1, gain, dh2, o, oc, dyc, b, wso)],
        [(h1.shape, F32, None, pltpu.HBM), (h1.shape, BF16, None), (gain.shape, F32, None)] + square_outs(3, width),
        scratch=[pltpu.VMEM(h1.shape, BF16), pltpu.VMEM((width, width), F32)],
        scalars=(mine,),
        after=after,
        flops=10 * rows * width * width,
    )
    return outs[:3], outs[3:]


def summed(own_refs, came_refs, index):
    return jnp.concatenate(
        [
            (own[index].astype(F32) + came[index].astype(F32)).astype(BF16)
            for own, came in zip(own_refs, came_refs)
        ],
        axis=1,
    )


def encoder_finish_kernel(mine_ref, own0_ref, own1_ref, came0_ref, came1_ref, x_ref, wk_ref, wv_ref, *refs):
    dx_ref, *grad_refs, total_ref = refs
    mine = mine_ref[0]
    dk = summed((own0_ref, own1_ref), (came0_ref, came1_ref), 0)
    dv = summed((own0_ref, own1_ref), (came0_ref, came1_ref), 1)
    x = x_ref[...]
    dx_ref[...] = (nt(dk, wk_ref[...]) + nt(dv, wv_ref[...])).astype(BF16)
    write_square(mine, 0, tn(x, dk), total_ref, grad_refs)
    write_square(mine, 1, tn(x, dv), total_ref, grad_refs)


def encoder_finish(mine, own, came, x, wk, wv, after=()):
    rows, width = x.shape
    outs = run(
        encoder_finish_kernel,
        "encoder_finish",
        (1,),
        [(v, None) for v in (*own, *came, x, wk, wv)],
        [(x.shape, BF16, None)] + square_outs(2, width),
        scratch=[pltpu.VMEM((width, width), F32)],
        scalars=(mine,),
        after=after,
        flops=8 * rows * width * width,
    )
    return outs[0], outs[1:]


def query_grad_kernel(mine_ref, dq0_ref, dq1_ref, a_ref, *refs):
    *grad_refs, total_ref = refs
    dq = jnp.concatenate([dq0_ref[...], dq1_ref[...]], axis=1)
    write_square(mine_ref[0], 0, tn(a_ref[...], dq), total_ref, grad_refs)


def query_grad(mine, dq, a):
    rows, width = a.shape
    return run(
        query_grad_kernel,
        "query_grad",
        (1,),
        [(v, None) for v in (*dq, a)],
        square_outs(1, width),
        scratch=[pltpu.VMEM((width, width), F32)],
        scalars=(mine,),
        flops=2 * rows * width * width,
    )


def key_grads_kernel(mine_ref, own0_ref, own1_ref, came0_ref, came1_ref, a_ref, *refs):
    sums_ref, *grad_refs, total_ref = refs
    a = a_ref[...]
    for i in range(2):
        total = summed((own0_ref, own1_ref), (came0_ref, came1_ref), i)
        sums_ref[i] = total
        write_square(mine_ref[0], i, tn(a, total), total_ref, grad_refs)


def key_grads(mine, own, came, a, after=()):
    rows, width = a.shape
    outs = run(
        key_grads_kernel,
        "key_grads",
        (1,),
        [(v, None) for v in (*own, *came, a)],
        [((2, rows, width), BF16, None)] + square_outs(2, width),
        scratch=[pltpu.VMEM((width, width), F32)],
        scalars=(mine,),
        after=after,
        flops=4 * rows * width * width,
    )
    return outs[0], outs[1:]


def self_finish_back_kernel(
    dq0_ref, dq1_ref, sums_ref, x_ref, gain_ref, dh1_ref, wq_ref, wk_ref, wv_ref, small_ref, dx_ref, small_out
):
    @pl.when(pl.program_id(0) == 0)
    def _():
        small_out[...] = small_ref[...]

    dq = jnp.concatenate([dq0_ref[...], dq1_ref[...]], axis=1)
    da = nt(dq, wq_ref[...]) + nt(sums_ref[0], wk_ref[...]) + nt(sums_ref[1], wv_ref[...])
    back, gain_part = norm_back(x_ref[...].astype(F32), gain_ref[...], da)
    small_out[0:1, :] += gain_part
    dx_ref[...] = (dh1_ref[...] + back).astype(BF16)


def self_finish_back(dq, sums, x, gain, dh1, wq, wk, wv, small):
    rows, width = dh1.shape
    tile = min(TILE, rows)
    spec = row_spec(tile, width)
    return run(
        self_finish_back_kernel,
        "self_finish_back",
        (rows // tile,),
        [
            (dq[0], row_spec(tile, dq[0].shape[1])),
            (dq[1], row_spec(tile, dq[1].shape[1])),
            (sums, pl.BlockSpec((2, tile, width), lambda i, *_: (0, i, 0)), None),
            (x, spec),
            (gain, None),
            (dh1, spec),
            (wq, None),
            (wk, None),
            (wv, None),
            (small, None),
        ],
        [((rows, width), BF16, spec), (small.shape, F32, None)],
        flops=6 * rows * width * width,
    )


SCORE_BOUND = 80.0


def mark_small(small_ref, q_norm_ref, *k_norm_refs):
    @pl.when(pl.program_id(0) == 0)
    def _():
        k_norm = k_norm_refs[0][...]
        for ref in k_norm_refs[1:]:
            k_norm = jnp.maximum(k_norm, ref[...])
        largest = jnp.max(q_norm_ref[...] * k_norm)
        small_ref[0] = (largest <= 0.95 * SCORE_BOUND**2).astype(jnp.int32)


def self_scores(i, head, blocks, q_ref, k_ref, table_ref, q_lanes_ref, k_lanes_ref):
    piece = q_ref.shape[0] // 2
    mem_size = k_ref.shape[0] // q_ref.shape[0]
    q_at = pl.multiple_of(blocks[0, i], piece)
    k_at = pl.multiple_of(blocks[1, i], piece)
    q = half_of(q_ref[pl.ds(q_at, piece), :], head)
    q = jnp.concatenate([q, q_lanes_ref[pl.ds(q_at, piece), :]], axis=1)
    k = jnp.concatenate([k_ref[pl.ds(k_at, piece), :], k_lanes_ref[pl.ds(k_at, piece), :]], axis=1)
    return with_bias(nt(q, k), table_ref, head, 2 * mem_size - i if i >= mem_size else blocks[2, i])


def add_mixed(sums, i, mixed, low, mem_size):
    if i == 0:
        sums[0] = mixed
    elif i < mem_size:
        part = jnp.where(low, mixed, 0.0)
        sums[0] = sums[0] + part
        sums[1] = mixed - part if sums[1] is None else sums[1] + (mixed - part)
    else:
        sums[1] = mixed if sums[1] is None else sums[1] + mixed


def self_forward_kernel(
    blocks,
    q_ref,
    k_ref,
    v_ref,
    table_ref,
    q_lanes_ref,
    k_lanes_ref,
    hidden_ref,
    w_out_ref,
    gain_ref,
    w_next_ref,
    q_norm_ref,
    k_norm0_ref,
    k_norm1_ref,
    o_ref,
    back_lanes_ref,
    hidden_out,
    norm_out,
    next_out,
    next_norm,
    s_ref,
    mixed_ref,
    small_ref,
):
    rows = q_ref.shape[0]
    piece = rows // 2
    mem_size = k_ref.shape[0] // rows
    count = 2 * mem_size + 1
    ones = jnp.ones((piece, LANES), BF16)
    scores = functools.partial(
        self_scores,
        blocks=blocks,
        q_ref=q_ref,
        k_ref=k_ref,
        table_ref=table_ref,
        q_lanes_ref=q_lanes_ref,
        k_lanes_ref=k_lanes_ref,
    )
    mark_small(small_ref, q_norm_ref, k_norm0_ref, k_norm1_ref)

    def mix(i, p):
        k_at = pl.multiple_of(blocks[1, i], piece)
        return nn(p.astype(BF16), jnp.concatenate([v_ref[pl.ds(k_at, piece), :], ones], axis=1))

    def put(outs):
        for i in range(2):
            mixed = join_halves(outs[0][i], outs[1][i]).astype(BF16)
            o_ref[i * piece : (i + 1) * piece, :] = mixed
            mixed_ref[pl.program_id(0), i * piece : (i + 1) * piece, :] = mixed

    def close(head, sums, tops):
        mixed = []
        for at, total, top in ((0, sums[0], tops[0]), (piece, sums[1], tops[1])):
            weight = total[:, LANES:]
            mixed.append(total[:, :LANES] / weight)
            log_sum = jnp.log2(weight) if top is None else top + jnp.log2(weight)
            back_lanes_ref[head, at : at + piece, :] = with_log_sum(q_lanes_ref[at : at + piece, :], log_sum)
        return mixed

    @pl.when(small_ref[0] == 1)
    def _():
        outs = []
        for head in range(2):
            sums = [None, None]
            for i in range(count):
                add_mixed(sums, i, mix(i, jnp.exp2(scores(i, head))), blocks[3, i] == 1, mem_size)
            outs.append(close(head, sums, (None, None)))
        put(outs)

    @pl.when(small_ref[0] == 0)
    def _():
        outs = []
        for head in range(2):
            tops = []
            for i in range(count):
                s = scores(i, head)
                s_ref[i] = s
                tops.append(jnp.max(s, axis=1, keepdims=True))
            top_low, top_high = tops[0], tops[mem_size]
            for i in range(mem_size + 1, count):
                top_high = jnp.maximum(top_high, tops[i])
            for i in range(1, mem_size):
                low = blocks[3, i] == 1
                top_low = jnp.maximum(top_low, jnp.where(low, tops[i], NEGATIVE))
                top_high = jnp.maximum(top_high, jnp.where(low, NEGATIVE, tops[i]))
            sums = [None, None]
            for i in range(count):
                low = blocks[3, i] == 1
                top = top_low if i == 0 else top_high if i >= mem_size else jnp.where(low, top_low, top_high)
                add_mixed(sums, i, mix(i, jnp.exp2(s_ref[i] - top)), low, mem_size)
            outs.append(close(head, sums, (top_low, top_high)))
        put(outs)

    @pl.when(pl.program_id(0) == PAIRS - 1)
    def _():
        self_finish(
            mixed_ref, hidden_ref, w_out_ref, gain_ref, w_next_ref, hidden_out, norm_out, next_out, next_norm
        )


def pair_spec(rows):
    return pl.BlockSpec((rows, LANES), lambda p, *_: (0, p))


def whole_spec(rows):
    return pl.BlockSpec((rows, LANES), lambda p, *_: (0, 0))


def lanes_spec(rows):
    return pl.BlockSpec((2, rows, LANES), lambda p, *_: (p, 0, 0))


def cross_forward_kernel(
    q_ref,
    k_ref,
    v_ref,
    q_lanes_ref,
    k_lanes_ref,
    hidden_ref,
    w_out_ref,
    gain_ref,
    q_norm_ref,
    k_norm0_ref,
    k_norm1_ref,
    o_ref,
    back_lanes_ref,
    hidden_out,
    norm_out,
    mixed_ref,
    small_ref,
):
    rows, keys = q_ref.shape[0], k_ref.shape[0]
    tile, key_tile = min(256, rows), min(256, keys)
    mark_small(small_ref, q_norm_ref, k_norm0_ref, k_norm1_ref)

    def put(part, outs):
        mixed = join_halves(outs[0], outs[1]).astype(BF16)
        o_ref[part, :] = mixed
        mixed_ref[pl.program_id(0), part, :] = mixed

    @pl.when(small_ref[0] == 1)
    def _():
        ones = jnp.ones((key_tile, LANES), BF16)
        outs = []
        for head in range(2):
            q = jnp.concatenate([half_of(q_ref[...], head), q_lanes_ref[...]], axis=1)
            total = None
            for at in range(0, keys, key_tile):
                part = slice(at, at + key_tile)
                k = jnp.concatenate([k_ref[part, :], k_lanes_ref[part, :]], axis=1)
                v = jnp.concatenate([v_ref[part, :], ones], axis=1)
                mixed = nn(jnp.exp2(nt(q, k)).astype(BF16), v)
                total = mixed if total is None else total + mixed
            weight = total[:, LANES:]
            outs.append(total[:, :LANES] / weight)
            back_lanes_ref[head] = with_log_sum(q_lanes_ref[...], jnp.log2(weight))
        put(slice(0, rows), outs)

    @pl.when(small_ref[0] == 0)
    def _():
        k = jnp.concatenate([k_ref[...], k_lanes_ref[...]], axis=1)
        v = jnp.concatenate([v_ref[...], jnp.ones((keys, LANES), BF16)], axis=1)
        for at in range(0, rows, tile):
            part = slice(at, at + tile)
            outs = []
            for head in range(2):
                q = jnp.concatenate([half_of(q_ref[part, :], head), q_lanes_ref[part, :]], axis=1)
                s = nt(q, k)
                top = jnp.max(s, axis=1, keepdims=True)
                total = nn(jnp.exp2(s - top).astype(BF16), v)
                weight = total[:, LANES:]
                outs.append(total[:, :LANES] / weight)
                back_lanes_ref[head, part, :] = with_log_sum(q_lanes_ref[part, :], top + jnp.log2(weight))
            put(part, outs)

    @pl.when(pl.program_id(0) == PAIRS - 1)
    def _():
        self_finish(mixed_ref, hidden_ref, w_out_ref, gain_ref, None, hidden_out, norm_out, None, None)


def grad_lanes(o, do):
    inner = jnp.sum(o.astype(F32) * do.astype(F32), axis=1, keepdims=True)
    pieces = [piece.astype(F32) for piece in in_three(-inner)]
    return put_lanes(jnp.zeros(do.shape, F32), 0, pieces).astype(BF16)


def put_parts(at, dk, dv, own_ref, other_ref):
    rows = own_ref.shape[1]
    ref, start = (own_ref, at) if at < rows else (other_ref, at - rows)
    ref[0, start : start + dk.shape[0], :] = (dk * LN2).astype(BF16)
    ref[1, start : start + dv.shape[0], :] = dv.astype(BF16)


def cross_backward_kernel(
    q_ref, k_ref, v_ref, o_ref, do_ref, back_lanes_ref, k_lanes_ref, dq_ref, own_ref, other_ref
):
    rows, keys = q_ref.shape[0], k_ref.shape[0]
    tile = min(256, rows)
    k_turned = k_ref[...].T
    k_wide = jnp.concatenate([k_ref[...], k_lanes_ref[...]], axis=1)
    v_wide = jnp.concatenate([v_ref[...], jnp.ones((keys, LANES), BF16)], axis=1)
    dk = dv = None
    for at in range(0, rows, tile):
        part = slice(at, at + tile)
        dqs = []
        for head in range(2):
            q, do = half_of(q_ref[part, :], head), half_of(do_ref[part, :], head)
            q_wide = jnp.concatenate([q, back_lanes_ref[head, part, :]], axis=1)
            do_wide = jnp.concatenate([do, grad_lanes(o_ref[part, :], do)], axis=1)
            p = jnp.exp2(nt(k_wide, q_wide))
            ds = (p * nt(v_wide, do_wide)).astype(BF16)
            dv_part, dk_part = nn(p.astype(BF16), do), nn(ds, q)
            dv = dv_part if dv is None else dv + dv_part
            dk = dk_part if dk is None else dk + dk_part
            dqs.append(nn(k_turned[head * HEAD_DIM : (head + 1) * HEAD_DIM, :], ds))
        dq_ref[part, :] = jnp.concatenate(dqs, axis=0).T.astype(BF16)
    for at, size in ((0, rows), (rows, keys - rows)):
        put_parts(at, dk[at : at + size], dv[at : at + size], own_ref, other_ref)


def self_backward_kernel(
    blocks,
    q_ref,
    k_ref,
    v_ref,
    o_ref,
    do_ref,
    back_lanes_ref,
    k_lanes_ref,
    table_ref,
    dq_ref,
    own_ref,
    other_ref,
    grad_ref,
    do_lanes_ref,
    dq_sum,
    dk_sum,
    dv_sum,
):
    rows = q_ref.shape[0]
    piece = rows // 2
    mem_size = k_ref.shape[0] // rows
    count = 2 * mem_size + 1
    ones = jnp.ones((piece, LANES), BF16)
    for head in range(2):
        do_lanes_ref[head] = grad_lanes(o_ref[...], half_of(do_ref[...], head))
    dq_sum[...] = jnp.zeros_like(dq_sum)
    dk_sum[...] = jnp.zeros_like(dk_sum)
    dv_sum[...] = jnp.zeros_like(dv_sum)
    grad_ref[...] = jnp.zeros_like(grad_ref)
    for i in reversed(range(count)):
        q_at = pl.multiple_of(blocks[0, i], piece)
        k_at = pl.multiple_of(blocks[1, i], piece)
        k, v = k_ref[pl.ds(k_at, piece), :], v_ref[pl.ds(k_at, piece), :]
        k_turned = k.T
        k_wide = jnp.concatenate([k, k_lanes_ref[pl.ds(k_at, piece), :]], axis=1)
        v_wide = jnp.concatenate([v, ones], axis=1)
        dk = dv = None
        dqs = []
        for head in range(2):
            q = half_of(q_ref[pl.ds(q_at, piece), :], head)
            do = half_of(do_ref[pl.ds(q_at, piece), :], head)
            q_wide = jnp.concatenate([q, back_lanes_ref[head, pl.ds(q_at, piece), :]], axis=1)
            do_wide = jnp.concatenate([do, do_lanes_ref[head, pl.ds(q_at, piece), :]], axis=1)
            s = nt(k_wide, q_wide)
            kind = 2 * mem_size - i if i >= mem_size else blocks[2, i]
            p = jnp.exp2(with_bias(s, table_ref, head, kind, turned=True))
            ds = p * nt(v_wide, do_wide)
            add_grad(ds, grad_ref, head, kind)
            ds = ds.astype(BF16)
            dv_part, dk_part = nn(p.astype(BF16), do), nn(ds, q)
            dv = dv_part if dv is None else dv + dv_part
            dk = dk_part if dk is None else dk + dk_part
            dqs.append(nn(k_turned[head * HEAD_DIM : (head + 1) * HEAD_DIM, :], ds))
        which = 1 - blocks[3, i]
        dq_sum[which] = dq_sum[which] + jnp.concatenate(dqs, axis=0)
        dk_sum[pl.ds(k_at, piece), :] = dk_sum[pl.ds(k_at, piece), :] + dk
        dv_sum[pl.ds(k_at, piece), :] = dv_sum[pl.ds(k_at, piece), :] + dv
    for i in range(2):
        dq_ref[i * piece : (i + 1) * piece, :] = dq_sum[i].T.astype(BF16)
    for at in (0, rows):
        size = rows if at == 0 else k_ref.shape[0] - rows
        put_parts(at, dk_sum[at : at + size, :], dv_sum[at : at + size, :], own_ref, other_ref)


def table_spec(table):
    return pl.BlockSpec((2,) + table.shape[1:], lambda p, *_: (p, 0, 0, 0))


def attention_flops(scores, matmuls):
    return 2 * HEADS * scores * 256 * matmuls


def self_forward(blocks, q, k, v, table, q_lanes, k_lanes, hidden, w_out, gain, w_next, norms, after=()):
    rows, keys = q.shape[0], k.shape[0]
    piece = rows // 2
    return run(
        self_forward_kernel,
        "self_forward",
        (PAIRS,),
        [
            (q, pair_spec(rows)),
            (k, pair_spec(keys)),
            (v, pair_spec(keys)),
            (table, table_spec(table)),
            (q_lanes, None),
            (k_lanes, None, pltpu.HBM),
            (hidden, pl.BlockSpec((rows, gain.shape[1]), lambda *_: (0, 0))),
            (w_out, None),
            (gain, None),
            (w_next, None),
        ]
        + [(norm, None) for norm in norms],
        [
            (q.shape, BF16, pair_spec(rows)),
            ((HEADS, rows, LANES), BF16, lanes_spec(rows)),
            (q.shape, F32, None),
            (q.shape, BF16, None),
            (q.shape, BF16, None),
            ((1, LANES), F32, None),
        ],
        scratch=[
            pltpu.VMEM((blocks.shape[1], piece, piece), F32),
            pltpu.VMEM((PAIRS, rows, LANES), BF16),
            pltpu.SMEM((1,), jnp.int32),
        ],
        scalars=(blocks,),
        after=after,
        flops=attention_flops(blocks.shape[1] * piece * piece, 2),
    )


def cross_forward(q, k, v, q_lanes, k_lanes, hidden, w_out, gain, norms, after=()):
    rows, keys = q.shape[0], k.shape[0]
    return run(
        cross_forward_kernel,
        "cross_forward",
        (PAIRS,),
        [
            (q, pair_spec(rows)),
            (k, pair_spec(keys)),
            (v, pair_spec(keys)),
            (q_lanes, None),
            (k_lanes, None, pltpu.HBM),
            (hidden, None),
            (w_out, None),
            (gain, None),
        ]
        + [(norm, None) for norm in norms],
        [
            (q.shape, BF16, pair_spec(rows)),
            ((HEADS, rows, LANES), BF16, lanes_spec(rows)),
            (q.shape, F32, None),
            (q.shape, BF16, None),
        ],
        scratch=[pltpu.VMEM((PAIRS, rows, LANES), BF16), pltpu.SMEM((1,), jnp.int32)],
        after=after,
        flops=attention_flops(rows * keys, 2),
    )


def half_spec(rows, start):
    return pl.BlockSpec((rows, LANES), lambda p, *_: (0, p + start))


def cross_backward(q, k, v, o, do, back_lanes, k_lanes, start, count, after=()):
    rows, keys = q.shape[0], k.shape[0]
    width = count * LANES
    parts = pl.BlockSpec((2, rows, LANES), lambda p, *_: (0, 0, p))
    others_spec = pl.BlockSpec((2, keys - rows, LANES), lambda p, *_: (0, 0, p))
    return run(
        cross_backward_kernel,
        "cross_backward",
        (count,),
        [
            (q, half_spec(rows, start)),
            (k, half_spec(keys, start)),
            (v, half_spec(keys, start)),
            (o, half_spec(rows, start)),
            (do, half_spec(rows, start), None),
            (back_lanes, pl.BlockSpec((2, rows, LANES), lambda p, *_: (p + start, 0, 0))),
            (k_lanes, None, pltpu.HBM),
        ],
        [
            ((rows, width), BF16, pair_spec(rows)),
            ((2, rows, width), BF16, parts),
            ((2, keys - rows, width), BF16, others_spec),
        ],
        after=after,
        flops=attention_flops(rows * keys, 5) * count // PAIRS,
    )


def self_backward(blocks, q, k, v, o, do, back_lanes, k_lanes, table_t, start, count, after=()):
    rows, keys = q.shape[0], k.shape[0]
    piece = rows // 2
    width = count * LANES
    parts = pl.BlockSpec((2, rows, LANES), lambda p, *_: (0, 0, p))
    others_spec = pl.BlockSpec((2, keys - rows, LANES), lambda p, *_: (0, 0, p))
    return run(
        self_backward_kernel,
        "self_backward",
        (count,),
        [
            (q, half_spec(rows, start)),
            (k, half_spec(keys, start)),
            (v, half_spec(keys, start)),
            (o, half_spec(rows, start)),
            (do, half_spec(rows, start), None),
            (back_lanes, pl.BlockSpec((2, rows, LANES), lambda p, *_: (p + start, 0, 0))),
            (k_lanes, None, pltpu.HBM),
            (table_t, pl.BlockSpec((2,) + table_t.shape[1:], lambda p, *_: (p + start, 0, 0, 0))),
        ],
        [
            ((rows, width), BF16, pair_spec(rows)),
            ((2, rows, width), BF16, parts),
            ((2, keys - rows, width), BF16, others_spec),
            ((2 * count,) + table_t.shape[1:], F32, table_spec(table_t)),
        ],
        scratch=[
            pltpu.VMEM((2, rows, LANES), BF16),
            pltpu.VMEM((2, LANES, piece), F32),
            pltpu.VMEM((keys, LANES), F32),
            pltpu.VMEM((keys, LANES), F32),
        ],
        scalars=(blocks,),
        after=after,
        flops=attention_flops(blocks.shape[1] * piece * piece, 5) * count // PAIRS,
    )


def on_device(
    decoder_in,
    encoder_out,
    dec_segments,
    dec_mask,
    enc_segments,
    enc_mask,
    self_gain,
    cross_gain,
    ffn_gain,
    rel_bias,
    self_query,
    self_key,
    self_value,
    self_out,
    cross_query,
    cross_key,
    cross_value,
    cross_out,
    ffn_in,
    ffn_out,
    out_grad,
):
    mem_size = lax.axis_size("mem")
    rows, width = decoder_in.shape[1:]
    keys = rows * mem_size
    dp_index = lax.axis_index("dp")
    mine = (dp_index % 2).astype(jnp.int32)[None]
    group = group_of(dp_index, lax.axis_index("mem"), mem_size)
    odd = group % 2 == 1
    blocks = block_list(group, mem_size, rows)
    bits = bit_values()
    gain_self, gain_cross, gain_ffn = (g[None, :] for g in (self_gain, cross_gain, ffn_gain))
    first, rest = PAIRS // 2, PAIRS - PAIRS // 2

    lane = jnp.arange(LANES, dtype=jnp.int32)[None, :]
    tags = jnp.zeros((rows, LANES), jnp.int32)
    for i, tag in enumerate((dec_segments, dec_mask, enc_segments, enc_mask)):
        tags = jnp.where(lane == i, tag[0][:, None], tags)
    pieces = to_rows(jnp.concatenate([decoder_in[0], tags.astype(BF16)], axis=1))
    table, table_t = bias_tables(rel_bias, small_block(rows // 2))
    pieces, table, table_t, encoder_in, grad_in = fence([], pieces, table, table_t, encoder_out[0], out_grad[0])
    hidden_own = arranged(pieces, odd)

    hidden_others = jnp.concatenate(others(hidden_own))
    self_in, query_rows, *so_far, q_lanes, q_norm, k_norm0 = own_project(
        hidden_own, gain_self, self_query, self_key, self_value, keys
    )
    hidden_others, so_far, grad_in, encoder_in = fence([], hidden_others, so_far, grad_in, encoder_in)
    encoder_pieces = to_rows(encoder_in)
    key_all, value_all, dec_lanes, enc_lanes, k_norm1 = other_project(hidden_others, gain_self, self_key, self_value, *so_far)
    self_mixed, self_lanes, hidden_one, cross_in, cross_rows, cross_norm = self_forward(
        blocks,
        query_rows,
        key_all,
        value_all,
        table,
        q_lanes,
        dec_lanes,
        hidden_own,
        self_out,
        gain_cross,
        cross_query,
        (q_norm, k_norm0, k_norm1),
    )
    encoder_pieces, cross_rows, grad_in = fence([], encoder_pieces, cross_rows, grad_in)

    encoder_own = arranged(encoder_pieces, odd)
    grad_pieces = to_rows(grad_in)
    encoder_others = jnp.concatenate(others(encoder_own))
    *so_far, k_norm0 = encoder_project(encoder_own, cross_key, cross_value, keys)
    encoder_others, so_far = fence([], encoder_others, so_far)

    cross_key_all, cross_value_all, k_norm1 = encoder_project(encoder_others, cross_key, cross_value, keys, so_far)
    cross_mixed, cross_lanes, hidden_two, ffn_input = cross_forward(
        cross_rows,
        cross_key_all,
        cross_value_all,
        q_lanes,
        enc_lanes,
        hidden_one,
        cross_out,
        gain_ffn,
        (cross_norm, k_norm0, k_norm1),
    )
    grad_pieces, ffn_input = fence([], grad_pieces, ffn_input)
    cotangent = arranged(grad_pieces, odd)
    (layer_out, hidden_two_grad, cross_branch_grad, cross_mixed_grad, ffn_gain_grad), ffn_grads = feed_forward(
        mine, ffn_input, cotangent, ffn_in, ffn_out, hidden_two, gain_ffn, cross_out
    )

    ffn_a, ffn_b = Scatter(ffn_grads[0], "xyz"), Scatter(ffn_grads[1], "yxz", ffn_in.shape[1] // width)
    layer_out = from_rows(layer_out, odd)

    def cross_half(start, count, do):
        return cross_backward(
            cross_rows, cross_key_all, cross_value_all, cross_mixed, do, cross_lanes, enc_lanes, start, count
        )

    cross_q0, cross_own0, cross_other0 = cross_half(0, first, cross_mixed_grad)
    layer_out, cross_q0, cross_own0, cross_other0, cross_mixed_grad = fence(
        [ffn_a, ffn_b], layer_out, cross_q0, cross_own0, cross_other0, cross_mixed_grad
    )

    third = (ffn_a.span[1] + ffn_b.span[1]) // 3
    left = ffn_a.span[1] - third
    ffn_mid = (ffn_a.part(third, left, "yxz"), ffn_b.part(0, third - left, "yxz"))
    ffn_a, ffn_b, ffn_c = ffn_a.part(0, third, "xyz"), ffn_mid[0], ffn_b.part(third - left, third, "zxy")
    advance(bits, ffn_a, ffn_mid, ffn_c)
    came0 = came_parts(cross_other0, rows)
    cross_q1, cross_own1, cross_other1 = cross_half(first, rest, cross_mixed_grad)
    came0, cross_q1, cross_own1, cross_other1 = fence([], came0, cross_q1, cross_own1, cross_other1)

    came1 = came_parts(cross_other1, rows)
    (hidden_one_grad, self_mixed_grad, cross_gain_grad), grads = cross_finish(
        mine,
        (cross_q0, cross_q1),
        cross_query,
        hidden_one,
        gain_cross,
        hidden_two_grad,
        self_mixed,
        cross_mixed,
        cross_branch_grad,
        cross_in,
        self_out,
    )
    came1, hidden_one_grad, self_mixed_grad, grads = fence(
        [ffn_a, ffn_b, ffn_c], came1, hidden_one_grad, self_mixed_grad, grads
    )

    advance(bits, ffn_a, ffn_b)
    rest_a = Scatter(grads, "xyz")
    encoder_out_grad, grads = encoder_finish(
        mine, (cross_own0, cross_own1), (came0, came1), encoder_own, cross_key, cross_value, after=[ffn_a.keep]
    )
    encoder_out_grad, grads, self_mixed_grad = fence([rest_a], encoder_out_grad, grads, self_mixed_grad)

    rest_b = Scatter(grads, "yxz")
    encoder_out_grad = from_rows(encoder_out_grad, odd)

    def self_half(start, count, do):
        return self_backward(
            blocks, query_rows, key_all, value_all, self_mixed, do, self_lanes, dec_lanes, table_t, start, count
        )

    self_q0, self_own0, self_other0, table_grad0 = self_half(0, first, self_mixed_grad)
    encoder_out_grad, self_q0, self_own0, self_other0, self_mixed_grad = fence(
        [ffn_a, ffn_b, rest_a, rest_b], encoder_out_grad, self_q0, self_own0, self_other0, self_mixed_grad
    )

    level(ffn_a, ffn_b, bits=bits)
    advance(bits, (ffn_a, ffn_b), ffn_c, rest_a, rest_b)
    came0 = came_parts(self_other0, rows)
    self_q1, self_own1, self_other1, table_grad1 = self_half(first, rest, self_mixed_grad)
    came0, self_q1, self_own1, self_other1, table_grad1 = fence(
        [ffn_a, ffn_c, rest_b], came0, self_q1, self_own1, self_other1, table_grad1
    )

    came1 = came_parts(self_other1, rows)
    query_grads = query_grad(mine, (self_q0, self_q1), self_in)
    (query_grads,) = fence([], query_grads)
    advance(bits, ffn_a, ffn_c)

    own_q = Scatter(query_grads, "xyz")
    small = table_sums(table_grad0, table_grad1, cross_gain_grad, ffn_gain_grad)
    came1, small = fence([ffn_c, rest_a, rest_b, own_q], came1, small)

    advance(bits, rest_a, rest_b, own_q)
    sums, grads = key_grads(mine, (self_own0, self_own1), (came0, came1), self_in, after=[rest_a.keep])
    sums, grads = fence([], sums, grads)

    own = Scatter(grads, "yxz")
    decoder_in_grad, small = self_finish_back(
        (self_q0, self_q1),
        sums,
        hidden_own,
        gain_self,
        hidden_one_grad,
        self_query,
        self_key,
        self_value,
        small,
    )
    decoder_in_grad, small = fence([ffn_a, ffn_c, rest_a, rest_b, own_q, own], decoder_in_grad, small)

    small_bits = [("dp", 0), ("dp", 2), ("dp", 1), ("mem", 0), ("dp", 3)]
    small_bits = [name for name in small_bits if name in all_bits()]
    small_bits += [name for name in all_bits() if name not in small_bits]

    def add_small(small, rounds=1):
        for _ in range(min(rounds, len(small_bits))):
            small = small + swap_many(small, (small_bits.pop(0),))
        return small

    half = own.span[1] // 2
    own_k, own_v = own.part(0, half, "yxz"), own.part(half, half, "xyz")
    level(rest_a, rest_b, bits=bits)
    advance(bits, own_k, own_v, own_q, (rest_a, rest_b))
    (small,) = fence([own_k, own_v, own_q, rest_a], add_small(small, 2))

    advance(bits, own_k, own_v, ffn_c)
    decoder_in_grad = from_rows(decoder_in_grad, odd)
    (small,) = fence([own_k, own_v], add_small(small))

    level(own_k, own_v, own_q, bits=bits)
    advance(bits, (own_k, own_v, own_q), rest_a)
    (small,) = fence([own_k], add_small(small))
    small = add_small(small, len(small_bits))
    for scatter in (own_k, ffn_a, ffn_c, rest_a):
        while scatter.order:
            advance(bits, scatter)
    parts = small
    self_gain_sum, cross_gain_sum, ffn_gain_sum, table_sum, grad_fo, grad_fi, *squares = write_grads(
        (ffn_a, ffn_c), rest_a, own_k, parts, small_block(rows // 2), width, ffn_in.shape[1]
    )
    self_gain_sum, cross_gain_sum, ffn_gain_sum = (v.reshape(-1) for v in (self_gain_sum, cross_gain_sum, ffn_gain_sum))
    grad_co, grad_cq, grad_so, grad_ck, grad_cv, grad_sk, grad_sv, grad_sq = squares
    return (
        layer_out[None],
        decoder_in_grad[None],
        encoder_out_grad[None],
        self_gain_sum,
        cross_gain_sum,
        ffn_gain_sum,
        table_sum,
        grad_sq,
        grad_sk,
        grad_sv,
        grad_so,
        grad_cq,
        grad_ck,
        grad_cv,
        grad_co,
        grad_fi,
        grad_fo,
    )


def solution(mesh):
    in_specs = (
        P("dp", "mem", None),
        P("dp", "mem", None),
        P("dp", "mem"),
        P("dp", "mem"),
        P("dp", "mem"),
        P("dp", "mem"),
        P(),
        P(),
        P(),
        P(),
        P(),
        P(),
        P(),
        P(),
        P(),
        P(),
        P(),
        P(),
        P(),
        P(),
        P("dp", "mem", None),
    )
    out_specs = (
        P("dp", "mem", None),
        P("dp", "mem", None),
        P("dp", "mem", None),
        P(),
        P(),
        P(),
        P(),
        P("dp", "mem"),
        P("dp", "mem"),
        P("dp", "mem"),
        P("dp", "mem"),
        P("dp", "mem"),
        P("dp", "mem"),
        P("dp", "mem"),
        P("dp", "mem"),
        P("dp", "mem"),
        P("dp", "mem"),
    )
    return jax.shard_map(
        on_device, mesh=mesh, in_specs=in_specs, out_specs=out_specs, check_vma=False
    )
```
